32 devices in a mesh: dp: 8 (over z, x), fsdp: 4 (over y, core).
Axes of the slice: x: 2, y: 2, z: 4, core: 2. Of those that a mesh axis runs over, the one named last changes fastest.
Arguments:
- decoder_states: bfloat16 [4096, 768], P(('dp', 'fsdp')), may hold values from -6 to 6
- encodings: bfloat16 [196608, 768], P(('dp', 'fsdp')), may hold values from -6 to 6
- owner_query: int32 [196608], P(('dp', 'fsdp')), may hold values from 0 to 128, as said below
- buckets: int32 [32, 32], replicated, may hold values from 0 to 31
- gain_self: bfloat16 [768], P(('dp', 'fsdp')), may hold values from 0.5 to 1.5
- bias_table: bfloat16 [384], P(('dp', 'fsdp')), may hold values from -4 to 4
- self_query: bfloat16 [768, 768], P(('dp', 'fsdp')), may hold values from -0.0546875 to 0.0546875
- self_key: bfloat16 [768, 768], P(('dp', 'fsdp')), may hold values from -0.21875 to 0.21875
- self_value: bfloat16 [768, 768], P(('dp', 'fsdp')), may hold values from -0.21875 to 0.21875
- self_output: bfloat16 [768, 768], P(('dp', 'fsdp')), may hold values from -0.3125 to 0.3125
- gain_cross: bfloat16 [768], P(('dp', 'fsdp')), may hold values from 0.5 to 1.5
- cross_query: bfloat16 [768, 768], P(('dp', 'fsdp')), may hold values from -0.0546875 to 0.0546875
- cross_key: bfloat16 [768, 768], P(('dp', 'fsdp')), may hold values from -0.21875 to 0.21875
- cross_value: bfloat16 [768, 768], P(('dp', 'fsdp')), may hold values from -0.21875 to 0.21875
- cross_output: bfloat16 [768, 768], P(('dp', 'fsdp')), may hold values from -0.875 to 0.875
- gain_feed: bfloat16 [768], P(('dp', 'fsdp')), may hold values from 0.5 to 1.5
- feed_in: bfloat16 [768, 3072], P(('dp', 'fsdp')), may hold values from -0.21875 to 0.21875
- feed_out: bfloat16 [3072, 768], P(('dp', 'fsdp')), may hold values from -0.15625 to 0.15625
- cotangent: bfloat16 [4096, 768], P(('dp', 'fsdp')), may hold values from -6 to 6
Outputs:
- layer_output: bfloat16 [4096, 768], P(('dp', 'fsdp'))
- decoder_grad: bfloat16 [4096, 768], P(('dp', 'fsdp'))
- encodings_grad: bfloat16 [196608, 768], P(('dp', 'fsdp'))
- grad_gain_self: float32 [768], P(('dp', 'fsdp'))
- grad_bias_table: float32 [384], P(('dp', 'fsdp'))
- grad_self_query: float32 [768, 768], P(('dp', 'fsdp'))
- grad_self_key: float32 [768, 768], P(('dp', 'fsdp'))
- grad_self_value: float32 [768, 768], P(('dp', 'fsdp'))
- grad_self_output: float32 [768, 768], P(('dp', 'fsdp'))
- grad_gain_cross: float32 [768], P(('dp', 'fsdp'))
- grad_cross_query: float32 [768, 768], P(('dp', 'fsdp'))
- grad_cross_key: float32 [768, 768], P(('dp', 'fsdp'))
- grad_cross_value: float32 [768, 768], P(('dp', 'fsdp'))
- grad_cross_output: float32 [768, 768], P(('dp', 'fsdp'))
- grad_gain_feed: float32 [768], P(('dp', 'fsdp'))
- grad_feed_in: float32 [768, 3072], P(('dp', 'fsdp'))
- grad_feed_out: float32 [3072, 768], P(('dp', 'fsdp'))
The draws below stay inside these ranges and needn't reach their ends.
Inputs may be any that keep to these rules, and one draw needn't show every extreme that they name: owner_query names the query of each encoding slot, 128 marking padding. Of the 6144 slots of the device at dp index i and fsdp index j, slot block k (rows k * 768 to (k + 1) * 768 - 1) holds only the 4 queries (k * 4 + j) * 4 onward, those of the device at dp index k and fsdp index j: one contiguous run of each of these queries in order, each run one row or more, then padding; some blocks hold no padding.
All inputs are finite; a program needn't handle non-finite values.
Results may differ from the reference program's by a relative error of at most 0.025.
The reference program's roundings to bfloat16 on the way count: a program that leaves them out, or rounds other values in their place, can miss the bound.
Values may be sent and summed in bfloat16 or wider, within the bound.
No kernel may reach another device: no remote copies, remote signals or barrier semaphores. Data moves between devices by JAX's collectives and lax.ppermute only.
A program may use at most 256 MiB of HBM per device.

```python
import jax
import jax.numpy as jnp
from jax import lax

D = 768
H = 12
DH = 64
FF = 3072
NB = 32
TGT = 32
QPD = 4
SLOT = 768
QUERIES = 128
ROWS = 4096
EROWS = 196608
N_DP = 8
N_FSDP = 4
DEVICES = 32


def draw_owner_query(key, part):
    key = jax.random.fold_in(key, 7)
    length_key, weight_key = jax.random.split(key)
    lowest = max(SLOT // 4, QPD + 1)
    lengths = jax.random.randint(length_key, (N_DP, N_FSDP, N_DP), lowest, SLOT + 1)
    target = jnp.arange(N_DP, dtype=jnp.int32)[None, None, :]
    source = jnp.arange(N_DP, dtype=jnp.int32)[:, None, None]
    fsdp_index = jnp.arange(N_FSDP, dtype=jnp.int32)[None, :, None]
    lengths = jnp.where((target == 0) & (fsdp_index == 0), SLOT, lengths)
    lengths = jnp.where((target == N_DP - 1) & (fsdp_index == 0) & (source == 0), lowest, lengths)
    run_weights = jax.random.randint(weight_key, (N_DP, N_FSDP, N_DP, QPD), 1, 9)
    running = jnp.cumsum(run_weights, axis=-1)
    total = running[..., -1:]
    steps_up = jnp.arange(1, QPD, dtype=jnp.int32)
    bounds = steps_up + (lengths[..., None] - QPD) * running[..., :-1] // total
    position = jnp.arange(SLOT, dtype=jnp.int32)[None, None, None, :]
    chosen = jnp.sum((position[..., None] >= bounds[..., None, :]).astype(jnp.int32), axis=-1)
    owners_all = (target[..., None] * N_FSDP + fsdp_index[..., None]) * QPD + chosen
    owners_all = jnp.where(position < lengths[..., None], owners_all, QUERIES)
    return owners_all.reshape(-1).astype(jnp.int32)


def place_ends(drawn, key, smallest, high):
    extent = drawn.shape
    index_at = [jax.random.randint(jax.random.fold_in(key, axis), (), 0, extent[axis]) for axis in range(len(extent))]
    drawn = drawn.at[tuple(index_at)].set(smallest)
    longest = extent.index(max(extent))
    index_at[longest] = (index_at[longest] + 1) % extent[longest]
    return drawn.at[tuple(index_at)].set(high)


def level_of(stream_key, extent, pieces, least, largest):
    factor_of = 1.0
    for dim, shards_of in pieces:
        heights = jax.random.uniform(jax.random.fold_in(jax.random.fold_in(stream_key, 6), dim), (shards_of,), jnp.float32, least / len(pieces), largest / len(pieces))
        factor_of = factor_of * jnp.repeat(jnp.exp(heights), extent[dim] // shards_of).reshape((-1,) + (1,) * (len(extent) - 1 - dim))
    return factor_of


def centred(stream_key, shape, deviation, reach, cuts=(), kind=jnp.bfloat16):
    array = jax.random.normal(stream_key, shape, jnp.float32) * deviation
    if len(cuts) > 0:
        array = level_of(stream_key, shape, cuts, -0.22, 0.18) * array
    return jnp.clip(array, min=-reach, max=reach).astype(kind)


def setup_inputs(seed: int = 0) -> dict:
    streams_of = jax.random.split(jax.random.key(seed), 20)
    decoder_states = centred(streams_of[0], (ROWS, D), 1.0, 6.0, ((0, 32),))
    encodings = centred(streams_of[1], (EROWS, D), 1.0, 6.0, ((0, 32),))
    owner_query = draw_owner_query(jax.random.fold_in(streams_of[19], 71), 0)
    buckets = place_ends(jax.random.randint(streams_of[3], (TGT, TGT), 0, NB), jax.random.fold_in(streams_of[3], 1), 0, NB - 1).astype(jnp.int32)
    gain_self = jnp.clip(1.0 + 0.1 * jax.random.normal(streams_of[4], (D,), jnp.float32), 0.5, 1.5).astype(jnp.bfloat16)
    bias_table = centred(streams_of[5], (NB * H,), 1.0, 4.0, ((0, 32),))
    self_query = centred(streams_of[6], (D, D), (D * 16) ** -0.5, 0.0546875, ((0, 32),))
    self_key = centred(streams_of[7], (D, D), D ** -0.5, 0.21875, ((0, 32),))
    self_value = centred(streams_of[8], (D, D), D ** -0.5, 0.21875, ((0, 32),))
    self_output = centred(streams_of[9], (D, D), (D // 2) ** -0.5, 0.3125, ((0, 32),))
    gain_cross = jnp.clip(1.0 + 0.1 * jax.random.normal(streams_of[10], (D,), jnp.float32), 0.5, 1.5).astype(jnp.bfloat16)
    cross_query = centred(streams_of[11], (D, D), (D * 16) ** -0.5, 0.0546875, ((0, 32),))
    cross_key = centred(streams_of[12], (D, D), D ** -0.5, 0.21875, ((0, 32),))
    cross_value = centred(streams_of[13], (D, D), D ** -0.5, 0.21875, ((0, 32),))
    cross_output = centred(streams_of[14], (D, D), (D // 16) ** -0.5, 0.875, ((0, 32),))
    gain_feed = jnp.clip(1.0 + 0.1 * jax.random.normal(streams_of[15], (D,), jnp.float32), 0.5, 1.5).astype(jnp.bfloat16)
    feed_in = centred(streams_of[16], (D, FF), D ** -0.5, 0.21875, ((0, 32),))
    feed_out = centred(streams_of[17], (FF, D), (FF // 2) ** -0.5, 0.15625, ((0, 32),))
    cotangent = centred(streams_of[18], (ROWS, D), 1.0, 6.0, ((0, 32),))
    return {"decoder_states": decoder_states, "encodings": encodings, "owner_query": owner_query, "buckets": buckets, "gain_self": gain_self, "bias_table": bias_table, "self_query": self_query, "self_key": self_key, "self_value": self_value, "self_output": self_output, "gain_cross": gain_cross, "cross_query": cross_query, "cross_key": cross_key, "cross_value": cross_value, "cross_output": cross_output, "gain_feed": gain_feed, "feed_in": feed_in, "feed_out": feed_out, "cotangent": cotangent}


@jax.custom_vjp
def low(v):
    return lax.optimization_barrier(v.astype(jnp.bfloat16)).astype(jnp.float32)

@jax.custom_vjp
def low_back(v):
    return v

def low_keep(v):
    return (low(v), None)

def low_pass(kept, grad):
    return (grad,)

def back_keep(v):
    return (v, None)

def back_low(kept, grad):
    return (low(grad),)
low.defvjp(low_keep, low_pass)
low_back.defvjp(back_keep, back_low)
epsilon = 1e-06
masked_score = -1e+30

def project(values, weight):
    return jnp.dot(values, weight, precision=lax.Precision.HIGHEST)

def rms_norm(values, gain_vector):
    return values * lax.rsqrt(lax.optimization_barrier(jnp.mean(values * values, axis=-1, keepdims=True)) + epsilon) * gain_vector

def self_attention(normed, query_weight, key_weight, value_weight, out_weight, bias_table, buckets):
    query_count = normed.shape[0] // TGT
    queries = low(low_back(project(normed, query_weight))).reshape(query_count, TGT, H, DH)
    key_rows = low(low_back(project(normed, key_weight))).reshape(query_count, TGT, H, DH)
    value_rows = low(low_back(project(normed, value_weight))).reshape(query_count, TGT, H, DH)
    bias_rows = bias_table.reshape(NB, H)[buckets]
    scores = jnp.einsum('bqhd,bkhd->bhqk', queries, key_rows, precision=lax.Precision.HIGHEST)
    scores = low_back(scores + jnp.transpose(bias_rows, (2, 0, 1))[None])
    causal = jnp.arange(TGT, dtype=jnp.int32)[:, None] >= jnp.arange(TGT, dtype=jnp.int32)[None, :]
    scores = jnp.where(causal[None, None], scores, masked_score)
    attention = low(jax.nn.softmax(scores, axis=-1))
    mixed_rows = jnp.einsum('bhqk,bkhd->bqhd', attention, value_rows, precision=lax.Precision.HIGHEST)
    mixed_rows = low(low_back(mixed_rows.reshape(-1, D)))
    return low_back(project(mixed_rows, out_weight))

def cross_group(normed, encoded, owners, group_index, query_weight, key_weight, value_weight, out_weight):
    row_count = normed.shape[0]
    queries = low(low_back(project(normed, query_weight))).reshape(row_count, H, DH)
    key_rows = low(low_back(project(encoded, key_weight))).reshape(-1, H, DH)
    value_rows = low(low_back(project(encoded, value_weight))).reshape(-1, H, DH)
    scores = low_back(jnp.einsum('qhd,khd->hqk', queries, key_rows, precision=lax.Precision.HIGHEST))
    row_query = group_index * (row_count // TGT) + jnp.arange(row_count, dtype=jnp.int32) // TGT
    allowed = owners[None, :] == row_query[:, None]
    scores = jnp.where(allowed[None], scores, masked_score)
    attention = low(jax.nn.softmax(scores, axis=-1))
    mixed_rows = jnp.einsum('hqk,khd->qhd', attention, value_rows, precision=lax.Precision.HIGHEST)
    mixed_rows = low(low_back(mixed_rows.reshape(row_count, D)))
    return low_back(project(mixed_rows, out_weight))

def forward(floats, owner_query, buckets):
    states, encodings, gain_self, bias_table, self_query, self_key, self_value, self_output, gain_cross, cross_query, cross_key, cross_value, cross_output, gain_feed, feed_in, feed_out = floats
    normed_self = low(rms_norm(states, gain_self))
    first_residual = states + self_attention(normed_self, self_query, self_key, self_value, self_output, bias_table, buckets)
    normed_cross = low(rms_norm(first_residual, gain_cross))
    grouped = encodings.reshape(N_DP, N_FSDP, N_DP, -1, D).transpose(2, 1, 0, 3, 4).reshape(DEVICES, -1, D)
    owners = owner_query.reshape(N_DP, N_FSDP, N_DP, -1).transpose(2, 1, 0, 3).reshape(DEVICES, -1)
    group_rows = normed_cross.reshape(DEVICES, -1, D)

    def one_group(packed):
        return cross_group(packed[0], packed[1], packed[2], packed[3], cross_query, cross_key, cross_value, cross_output)
    cross_branch = lax.map(jax.checkpoint(one_group), (group_rows, grouped, owners, jnp.arange(DEVICES, dtype=jnp.int32)))
    second_residual = first_residual + cross_branch.reshape(-1, D)
    normed_feed = low(rms_norm(second_residual, gain_feed))
    pre_act = low_back(project(normed_feed, feed_in))
    hidden = low(jax.nn.gelu(pre_act))
    return second_residual + low_back(project(hidden, feed_out))

def reference(decoder_states, encodings, owner_query, buckets, gain_self, bias_table, self_query, self_key, self_value, self_output, gain_cross, cross_query, cross_key, cross_value, cross_output, gain_feed, feed_in, feed_out, cotangent):
    floats = tuple((item.astype(jnp.float32) for item in (decoder_states, encodings, gain_self, bias_table, self_query, self_key, self_value, self_output, gain_cross, cross_query, cross_key, cross_value, cross_output, gain_feed, feed_in, feed_out)))

    def closed(values):
        return forward(values, owner_query, buckets)
    output, pullback = jax.vjp(closed, floats)
    grads = pullback(cotangent.astype(jnp.float32))[0]
    return (output.astype(jnp.bfloat16), grads[0].astype(jnp.bfloat16), grads[1].astype(jnp.bfloat16), grads[2], grads[3], grads[4], grads[5], grads[6], grads[7], grads[8], grads[9], grads[10], grads[11], grads[12], grads[13], grads[14], grads[15])
```

```python
import functools

import jax
import jax.numpy as jnp
from jax import lax
from jax.experimental import pallas as pl
from jax.experimental.pallas import tpu as pltpu
from jax.sharding import PartitionSpec as P

D = 768
H = 12
DH = 64
NB = 32
TGT = 32
QPD = 4
GROUPS = 3
TILE = 128

epsilon = 1e-06
masked_score = -1e30
both = ("dp", "fsdp")
bf16 = jnp.bfloat16
f32 = jnp.float32


def matmul(left_side, right_side):
    return jnp.dot(left_side, right_side, preferred_element_type=f32)


def dot_tn(left_side, right_side):
    return lax.dot_general(
        left_side, right_side, (((0,), (0,)), ((), ())), preferred_element_type=f32
    )


def dot_nt(left_side, right_side):
    return lax.dot_general(
        left_side, right_side, (((1,), (1,)), ((), ())), preferred_element_type=f32
    )


def rms_norm(values, gain_vector):
    return (
        values
        * lax.rsqrt(jnp.mean(values * values, axis=-1, keepdims=True) + epsilon)
        * gain_vector
    )


def pieces_of(values):
    high = values.astype(bf16)
    rest = values - high.astype(f32)
    mid = rest.astype(bf16)
    low = (rest - mid.astype(f32)).astype(bf16)
    return high, mid, low


def split_pieces(values):
    high = lax.reduce_precision(values, 8, 7)
    mid = lax.reduce_precision(values - high, 8, 7)
    low = values - high - mid
    return high.astype(bf16), mid.astype(bf16), low.astype(bf16)


def spread_heads(rows):
    tall = jnp.concatenate([rows, rows, rows, rows], axis=0)
    head_row = lax.broadcasted_iota(jnp.int32, (4 * TGT, 4 * DH), 0) // TGT
    head_col = lax.broadcasted_iota(jnp.int32, (4 * TGT, 4 * DH), 1) // DH
    return jnp.where(head_row == head_col, tall, jnp.zeros_like(tall))


def gather_heads(tall):
    head_col = lax.broadcasted_iota(jnp.int32, (TGT, 4 * DH), 1) // DH
    rows = jnp.zeros((TGT, 4 * DH), f32)
    for head in range(4):
        rows = jnp.where(head_col == head, tall[head * TGT : (head + 1) * TGT], rows)
    return rows


def run_tiles(bounds_ref, block, query, slot):
    start = bounds_ref[block, query]
    end = bounds_ref[block, query + 1]
    first = (start // 16) * 16
    count = (end - first + TILE - 1) // TILE
    return start, end, first, count


def tile_rows(first, step, start, end, slot):
    want = first + step * TILE
    base = pl.multiple_of(jnp.minimum(want, slot - TILE), 16)
    rows = base + lax.broadcasted_iota(jnp.int32, (TILE, 4 * TGT), 0)
    inside = (rows >= jnp.maximum(start, want)) & (rows < end)
    return base, inside


def column_of(row):
    return jnp.transpose(jnp.broadcast_to(row, (8, 4 * TGT)))[:, :1]


def mix_kernel(slot, bounds_ref, q_ref, k_ref, v_ref, o_ref, x_ref, score_ref, mix_ref):
    block = pl.program_id(0)
    lane = lax.broadcasted_iota(jnp.int32, (TGT, 128), 1)
    for query in range(QPD):
        start, end, first, count = run_tiles(bounds_ref, block, query, slot)
        rows_of = slice(query * TGT, (query + 1) * TGT)
        spread = [
            spread_heads(q_ref[0, rows_of, g * 256 : (g + 1) * 256]) for g in range(GROUPS)
        ]

        def score_step(step, tops):
            base, inside = tile_rows(first, step, start, end, slot)
            new_tops = []
            for g in range(GROUPS):
                keys = k_ref[0, pl.ds(base, TILE), g * 256 : (g + 1) * 256]
                scores = jnp.where(inside, dot_nt(keys, spread[g]), masked_score)
                score_ref[g, pl.ds(pl.multiple_of(step * TILE, TILE), TILE), :] = scores
                new_tops.append(jnp.maximum(tops[g], jnp.max(scores, axis=0, keepdims=True)))
            return tuple(new_tops)

        tops = lax.fori_loop(
            0,
            count,
            score_step,
            tuple(jnp.full((1, 4 * TGT), masked_score, f32) for g in range(GROUPS)),
        )
        mix_ref[...] = jnp.zeros_like(mix_ref)

        def mix_step(step, sums):
            want = first + step * TILE
            base = pl.multiple_of(jnp.minimum(want, slot - TILE), 16)
            new_sums = []
            for g in range(GROUPS):
                scores = score_ref[g, pl.ds(pl.multiple_of(step * TILE, TILE), TILE), :]
                weights = jnp.exp(scores - tops[g])
                new_sums.append(sums[g] + jnp.sum(weights, axis=0, keepdims=True))
                values = v_ref[0, pl.ds(base, TILE), g * 256 : (g + 1) * 256]
                mix_ref[g] += dot_tn(weights.astype(bf16), values)
            return tuple(new_sums)

        sums = lax.fori_loop(
            0, count, mix_step, tuple(jnp.zeros((1, 4 * TGT), f32) for g in range(GROUPS))
        )
        logs = jnp.zeros((TGT, 128), f32)
        for g in range(GROUPS):
            scale = column_of(1.0 / sums[g])
            log_sum = column_of(tops[g] + jnp.log(sums[g]))
            o_ref[0, rows_of, g * 256 : (g + 1) * 256] = gather_heads(mix_ref[g] * scale).astype(
                bf16
            )
            for head in range(4):
                logs = jnp.where(
                    (lane % 16 == g * 4 + head) & (lane < 48),
                    log_sum[head * TGT : (head + 1) * TGT],
                    logs,
                )
        high, mid, low = pieces_of(logs)
        x_ref[0, rows_of, :] = jnp.where(
            lane < 16, high.astype(f32), jnp.where(lane < 32, mid.astype(f32), low.astype(f32))
        ).astype(bf16)


def grad_kernel(
    slot,
    bounds_ref,
    q_ref,
    m_ref,
    place_ref,
    k_ref,
    v_ref,
    dq_ref,
    dk_ref,
    dv_ref,
    sum_ref,
):
    block = pl.program_id(0)
    dk_ref[...] = jnp.zeros_like(dk_ref)
    dv_ref[...] = jnp.zeros_like(dv_ref)
    row = lax.broadcasted_iota(jnp.int32, (TGT, 2 * H * TGT), 0)
    target = lax.broadcasted_iota(jnp.int32, (TGT, 2 * H * TGT), 1) % TGT
    for query in range(QPD):
        start, end, first, count = run_tiles(bounds_ref, block, query, slot)
        rows_of = slice(query * TGT, (query + 1) * TGT)
        spread = [
            spread_heads(q_ref[0, rows_of, g * 256 : (g + 1) * 256]) for g in range(GROUPS)
        ]
        spread_m = [
            spread_heads(m_ref[0, rows_of, g * 256 : (g + 1) * 256]) for g in range(GROUPS)
        ]
        placed = matmul(m_ref[0, rows_of, D : D + 128], place_ref[...])
        flat = jnp.sum(jnp.where(row == target, placed, 0.0), axis=0, keepdims=True)
        logs = [flat[:, g * 128 : (g + 1) * 128] for g in range(GROUPS)]
        deltas = [flat[:, (GROUPS + g) * 128 : (GROUPS + g + 1) * 128] for g in range(GROUPS)]
        sum_ref[...] = jnp.zeros_like(sum_ref)

        def step_of(step, carry):
            base, inside = tile_rows(first, step, start, end, slot)
            for g in range(GROUPS):
                columns = slice(g * 256, (g + 1) * 256)
                keys = k_ref[0, pl.ds(base, TILE), columns]
                values = v_ref[0, pl.ds(base, TILE), columns]
                soft = jnp.where(inside, jnp.exp(dot_nt(keys, spread[g]) - logs[g]), 0.0)
                d_soft = dot_nt(values, spread_m[g])
                d_scores = (soft * (d_soft - deltas[g])).astype(bf16)
                sum_ref[g] += dot_tn(d_scores, keys)
                d_keys = matmul(d_scores, spread[g])
                d_values = matmul(soft.astype(bf16), spread_m[g])
                dk_ref[0, pl.ds(base, TILE), columns] += d_keys.astype(bf16)
                dv_ref[0, pl.ds(base, TILE), columns] += d_values.astype(bf16)
            return carry

        lax.fori_loop(0, count, step_of, 0)
        for g in range(GROUPS):
            dq_ref[0, rows_of, g * 256 : (g + 1) * 256] = gather_heads(sum_ref[g]).astype(bf16)


def cross_mix(bounds, queries, keys, values):
    blocks, slot = keys.shape[0], keys.shape[1]
    rows = queries.shape[1]
    at = lambda i, *refs: (i, 0, 0)
    return pl.pallas_call(
        functools.partial(mix_kernel, slot),
        grid_spec=pltpu.PrefetchScalarGridSpec(
            num_scalar_prefetch=1,
            grid=(blocks,),
            in_specs=[
                pl.BlockSpec((1, rows, D), at),
                pl.BlockSpec((1, slot, D), at),
                pl.BlockSpec((1, slot, D), at),
            ],
            out_specs=[pl.BlockSpec((1, rows, D), at), pl.BlockSpec((1, rows, 128), at)],
            scratch_shapes=[
                pltpu.VMEM((GROUPS, slot + TILE, 4 * TGT), f32),
                pltpu.VMEM((GROUPS, 4 * TGT, 256), f32),
            ],
        ),
        out_shape=[
            jax.ShapeDtypeStruct((blocks, rows, D), bf16),
            jax.ShapeDtypeStruct((blocks, rows, 128), bf16),
        ],
        compiler_params=pltpu.CompilerParams(vmem_limit_bytes=40 * 1024 * 1024),
        cost_estimate=pl.CostEstimate(
            flops=12_000_000_000, bytes_accessed=22_000_000, transcendentals=4_000_000
        ),
        name="cross_mix",
    )(bounds, queries, keys, values)


def cross_grad(bounds, queries, mixed, place, keys, values):
    blocks, slot = keys.shape[0], keys.shape[1]
    rows = queries.shape[1]
    at = lambda i, *refs: (i, 0, 0)
    return pl.pallas_call(
        functools.partial(grad_kernel, slot),
        grid_spec=pltpu.PrefetchScalarGridSpec(
            num_scalar_prefetch=1,
            grid=(blocks,),
            in_specs=[
                pl.BlockSpec((1, rows, D), at),
                pl.BlockSpec((1, rows, D + 128), at),
                pl.BlockSpec((128, 2 * H * TGT), lambda i, *refs: (0, 0)),
                pl.BlockSpec((1, slot, D), at),
                pl.BlockSpec((1, slot, D), at),
            ],
            out_specs=[
                pl.BlockSpec((1, rows, D), at),
                pl.BlockSpec((1, slot, D), at),
                pl.BlockSpec((1, slot, D), at),
            ],
            scratch_shapes=[pltpu.VMEM((GROUPS, 4 * TGT, 256), f32)],
        ),
        out_shape=[
            jax.ShapeDtypeStruct((blocks, rows, D), bf16),
            jax.ShapeDtypeStruct((blocks, slot, D), bf16),
            jax.ShapeDtypeStruct((blocks, slot, D), bf16),
        ],
        compiler_params=pltpu.CompilerParams(vmem_limit_bytes=40 * 1024 * 1024),
        cost_estimate=pl.CostEstimate(
            flops=24_000_000_000, bytes_accessed=42_000_000, transcendentals=4_000_000
        ),
        name="cross_grad",
    )(bounds, queries, mixed, place, keys, values)


def permute(value, n_dp, n_fsdp, move):
    pairs = []
    for dp in range(n_dp):
        for fsdp in range(n_fsdp):
            to = move(dp, fsdp)
            pairs.append((dp * n_fsdp + fsdp, to[0] * n_fsdp + to[1]))
    return lax.ppermute(value, both, pairs)


def gather_dp(value, n_dp, n_fsdp):
    x_size = n_fsdp // 2
    z_size = n_dp // x_size
    index = lax.axis_index("dp")
    z, x = index // x_size, index % x_size
    found = []
    held = value
    for z_step in range(z_size):
        across = held
        for x_step in range(x_size):
            place = ((z - z_step) % z_size) * x_size + (x - x_step) % x_size
            found.append((place, across))
            if x_step < x_size - 1:
                across = permute(
                    across,
                    n_dp,
                    n_fsdp,
                    lambda d, f: (d // x_size * x_size + (d + 1) % x_size, f),
                )
        if z_step < z_size - 1:
            held = permute(held, n_dp, n_fsdp, lambda d, f: ((d + x_size) % n_dp, f))
    whole = jnp.zeros((n_dp,) + value.shape, value.dtype)
    for place, piece in found:
        whole = lax.dynamic_update_slice(whole, piece[None], (place,) + (0,) * value.ndim)
    return whole


def shards(
    n_dp,
    n_fsdp,
    decoder_states,
    encodings,
    owner_query,
    buckets,
    gain_self,
    bias_table,
    self_query,
    self_key,
    self_value,
    self_output,
    gain_cross,
    cross_query,
    cross_key,
    cross_value,
    cross_output,
    gain_feed,
    feed_in,
    feed_out,
    cotangent,
):
    n_dev = n_dp * n_fsdp
    fsdp_index = lax.axis_index("fsdp")
    row_count = decoder_states.shape[0]
    query_count = row_count // TGT
    keys_total = encodings.shape[0]
    slot = keys_total // n_dp
    part = D // n_dev
    bias_part = bias_table.shape[0]

    small = jnp.zeros((part, 128), bf16)
    small = small.at[:, 0].set(gain_self).at[:, 1].set(gain_cross).at[:, 2].set(gain_feed)
    small = small.at[:bias_part, 3].set(bias_table)
    first_pack = lax.all_gather(
        jnp.concatenate([self_query, self_key, self_value, self_output, cross_query, small], axis=1),
        both,
        axis=0,
        tiled=True,
    )
    second_pack = lax.all_gather(
        jnp.concatenate([cross_key, cross_value], axis=1), both, axis=0, tiled=True
    )
    third_pack = lax.all_gather(
        jnp.concatenate([cross_output, feed_in, feed_out.reshape(part, 4 * D)], axis=1),
        both,
        axis=0,
        tiled=True,
    )
    w_self_query, w_self_key, w_self_value, w_self_output, w_cross_query = (
        first_pack[:, i * D : (i + 1) * D] for i in range(5)
    )
    w_cross_key, w_cross_value = second_pack[:, :D], second_pack[:, D:]
    w_cross_output = third_pack[:, :D]
    w_feed_in = third_pack[:, D : 5 * D]
    w_feed_out = third_pack[:, 5 * D :].reshape(4 * D, D)
    g_self = first_pack[:, 5 * D].astype(f32)
    g_cross = first_pack[:, 5 * D + 1].astype(f32)
    g_feed = first_pack[:, 5 * D + 2].astype(f32)
    bias_rows = (
        first_pack[:, 5 * D + 3].reshape(n_dev, part)[:, :bias_part].reshape(NB, H).astype(f32)
    )

    owners = owner_query.reshape(n_dp, slot)
    block_ids = (jnp.arange(n_dp, dtype=jnp.int32) * n_fsdp + fsdp_index) * QPD
    counts = [
        jnp.sum((owners == (block_ids + n)[:, None]).astype(jnp.int32), axis=1)
        for n in range(QPD)
    ]
    bounds = jnp.cumsum(
        jnp.stack([jnp.zeros((n_dp,), jnp.int32)] + counts, axis=1), axis=1
    ).astype(jnp.int32)

    states = decoder_states.astype(f32)
    normed_self = rms_norm(states, g_self).astype(bf16)
    query_self = matmul(normed_self, w_self_query).astype(bf16)
    key_self = matmul(normed_self, w_self_key).astype(bf16)
    value_self = matmul(normed_self, w_self_value).astype(bf16)
    heads_query = query_self.reshape(query_count, TGT, H, DH)
    heads_key = key_self.reshape(query_count, TGT, H, DH)
    heads_value = value_self.reshape(query_count, TGT, H, DH)
    bucket_hot = (buckets.reshape(-1)[:, None] == jnp.arange(NB, dtype=jnp.int32)[None, :]).astype(
        f32
    )
    position_bias = (
        jnp.dot(bucket_hot, bias_rows, precision=lax.Precision.HIGHEST)
        .reshape(TGT, TGT, H)
        .transpose(2, 0, 1)
    )
    causal = jnp.arange(TGT, dtype=jnp.int32)[:, None] >= jnp.arange(TGT, dtype=jnp.int32)[None, :]
    self_scores = (
        jnp.einsum("bqhd,bkhd->bhqk", heads_query, heads_key, preferred_element_type=f32)
        + position_bias[None]
    )
    self_scores = jnp.where(causal[None, None], self_scores, masked_score)
    self_soft = jax.nn.softmax(self_scores, axis=-1)
    self_probs = self_soft.astype(bf16)
    self_mixed = (
        jnp.einsum("bhqk,bkhd->bqhd", self_probs, heads_value, preferred_element_type=f32)
        .reshape(row_count, D)
        .astype(bf16)
    )
    first_residual = states + matmul(self_mixed, w_self_output)
    normed_cross = rms_norm(first_residual, g_cross).astype(bf16)
    query_cross = matmul(normed_cross, w_cross_query).astype(bf16)

    key_cross = matmul(encodings, w_cross_key).astype(bf16).reshape(n_dp, slot, D)
    value_cross = matmul(encodings, w_cross_value).astype(bf16).reshape(n_dp, slot, D)
    all_queries = gather_dp(query_cross, n_dp, n_fsdp)
    part_mixed, part_logs = cross_mix(bounds, all_queries, key_cross, value_cross)
    back = lax.all_to_all(
        jnp.concatenate([part_mixed, part_logs], axis=2), "dp", split_axis=0, concat_axis=0
    )
    lane = jnp.arange(128, dtype=jnp.int32)
    head_of = jnp.arange(D, dtype=jnp.int32) // DH
    widen = ((lane[:, None] % 16 == head_of[None, :]) & (lane[:, None] < 48)).astype(bf16)
    logs = matmul(back[:, :, D:].reshape(-1, 128), widen).reshape(n_dp, row_count, D)
    log_top = jnp.max(logs, axis=0)
    shares = jnp.exp(logs - log_top)
    share_sum = jnp.sum(shares, axis=0)
    mixed_wide = jnp.sum(shares * back[:, :, :D].astype(f32), axis=0) / share_sum
    log_whole = (log_top + jnp.log(share_sum)).reshape(row_count, H, DH)[:, :, 0]
    cross_mixed = mixed_wide.astype(bf16)

    second_residual = first_residual + matmul(cross_mixed, w_cross_output)
    normed_feed = rms_norm(second_residual, g_feed).astype(bf16)
    pre_act = matmul(normed_feed, w_feed_in)
    hidden = jax.nn.gelu(pre_act).astype(bf16)
    layer_output = (second_residual + matmul(hidden, w_feed_out)).astype(bf16)

    grad_feed_out = dot_tn(hidden, cotangent)
    d_hidden = dot_nt(cotangent, w_feed_out)
    unused, gelu_pull = jax.vjp(jax.nn.gelu, pre_act)
    d_pre = gelu_pull(d_hidden)[0].astype(bf16)
    grad_feed_in = dot_tn(normed_feed, d_pre)
    d_normed_feed = dot_nt(d_pre, w_feed_in)
    unused, norm_pull = jax.vjp(rms_norm, second_residual, g_feed)
    d_second_norm, grad_gain_feed = norm_pull(d_normed_feed)
    d_second = cotangent.astype(f32) + d_second_norm
    d_cross_branch = d_second.astype(bf16)
    grad_cross_output = dot_tn(cross_mixed, d_cross_branch)
    d_cross_mixed = dot_nt(d_cross_branch, w_cross_output).astype(bf16)

    delta = jnp.sum(
        (d_cross_mixed.astype(f32) * mixed_wide).reshape(row_count, H, DH), axis=-1
    )
    gap = jnp.zeros((row_count, 16 - H), bf16)
    extras = []
    for values in (log_whole, delta):
        for piece in split_pieces(values):
            extras += [piece, gap]
    extras.append(jnp.zeros((row_count, 32), bf16))
    all_mixed = gather_dp(
        jnp.concatenate([d_cross_mixed] + extras, axis=1), n_dp, n_fsdp
    )
    column = jnp.arange(2 * H * TGT, dtype=jnp.int32)
    place = (
        (lane[:, None] // 48 == column[None, :] // (H * TGT))
        & (lane[:, None] % 16 == (column[None, :] // TGT) % H)
    ).astype(bf16)
    part_query, d_key_cross, d_value_cross = cross_grad(
        bounds, all_queries, all_mixed, place, key_cross, value_cross
    )
    d_key_cross = d_key_cross.reshape(keys_total, D)
    d_value_cross = d_value_cross.reshape(keys_total, D)
    back_query = lax.all_to_all(part_query, "dp", split_axis=0, concat_axis=0)
    d_query_cross = jnp.sum(back_query.astype(f32), axis=0).astype(bf16)
    grad_cross_query = dot_tn(normed_cross, d_query_cross)
    grad_cross_key = dot_tn(encodings, d_key_cross)
    grad_cross_value = dot_tn(encodings, d_value_cross)
    d_normed_cross = dot_nt(d_query_cross, w_cross_query)
    encodings_grad = (
        dot_nt(d_key_cross, w_cross_key) + dot_nt(d_value_cross, w_cross_value)
    ).astype(bf16)
    unused, norm_pull = jax.vjp(rms_norm, first_residual, g_cross)
    d_first_norm, grad_gain_cross = norm_pull(d_normed_cross)
    d_first = d_second + d_first_norm

    d_self_branch = d_first.astype(bf16)
    grad_self_output = dot_tn(self_mixed, d_self_branch)
    d_self_mixed = (
        dot_nt(d_self_branch, w_self_output).astype(bf16).reshape(query_count, TGT, H, DH)
    )
    d_self_probs = jnp.einsum(
        "bqhd,bkhd->bhqk", d_self_mixed, heads_value, preferred_element_type=f32
    )
    self_delta = jnp.sum(self_soft * d_self_probs, axis=-1, keepdims=True)
    d_self_scores = (self_soft * (d_self_probs - self_delta)).astype(bf16)
    d_value_self = (
        jnp.einsum("bhqk,bqhd->bkhd", self_probs, d_self_mixed, preferred_element_type=f32)
        .reshape(row_count, D)
        .astype(bf16)
    )
    d_query_self = (
        jnp.einsum("bhqk,bkhd->bqhd", d_self_scores, heads_key, preferred_element_type=f32)
        .reshape(row_count, D)
        .astype(bf16)
    )
    d_key_self = (
        jnp.einsum("bhqk,bqhd->bkhd", d_self_scores, heads_query, preferred_element_type=f32)
        .reshape(row_count, D)
        .astype(bf16)
    )
    score_sums = (
        jnp.sum(d_self_scores.astype(f32), axis=0).transpose(1, 2, 0).reshape(TGT * TGT, H)
    )
    grad_bias_table = jnp.dot(bucket_hot.T, score_sums, precision=lax.Precision.HIGHEST).reshape(-1)
    grad_self_query = dot_tn(normed_self, d_query_self)
    grad_self_key = dot_tn(normed_self, d_key_self)
    grad_self_value = dot_tn(normed_self, d_value_self)
    d_normed_self = (
        dot_nt(d_query_self, w_self_query)
        + dot_nt(d_key_self, w_self_key)
        + dot_nt(d_value_self, w_self_value)
    )
    unused, norm_pull = jax.vjp(rms_norm, states, g_self)
    d_states_norm, grad_gain_self = norm_pull(d_normed_self)
    decoder_grad = (d_first + d_states_norm).astype(bf16)

    def scatter(value):
        return lax.psum_scatter(value, both, scatter_dimension=0, tiled=True)

    feed_sum = scatter(
        jnp.concatenate(
            [grad_cross_output, grad_feed_in, grad_feed_out.reshape(D, 4 * D)], axis=1
        ).astype(bf16)
    ).astype(f32)
    key_sum = scatter(
        jnp.concatenate([grad_cross_key, grad_cross_value], axis=1).astype(bf16)
    ).astype(f32)
    bias_column = jnp.pad(
        grad_bias_table.reshape(n_dev, bias_part), ((0, 0), (0, part - bias_part))
    ).reshape(D)
    small_grad = jnp.stack(
        [grad_gain_self, grad_gain_cross, grad_gain_feed, bias_column] + [bias_column] * 4, axis=1
    )
    small_grad = jnp.pad(small_grad, ((0, 0), (0, 120)))
    last_sum = scatter(
        jnp.concatenate(
            [
                grad_self_query,
                grad_self_key,
                grad_self_value,
                grad_self_output,
                grad_cross_query,
                small_grad,
            ],
            axis=1,
        ).astype(bf16)
    ).astype(f32)
    sums = [last_sum[:, i * D : (i + 1) * D] for i in range(5)]
    small_sum = last_sum[:, 5 * D :]
    return (
        layer_output,
        decoder_grad,
        encodings_grad,
        small_sum[:, 0],
        small_sum[:bias_part, 3],
        sums[0],
        sums[1],
        sums[2],
        sums[3],
        small_sum[:, 1],
        sums[4],
        key_sum[:, :D],
        key_sum[:, D:],
        feed_sum[:, :D],
        small_sum[:, 2],
        feed_sum[:, D : 5 * D],
        feed_sum[:, 5 * D :].reshape(4 * part, D),
    )


def solution(mesh):
    rows = P(both, None)
    flat = P(both)
    in_specs = (rows, rows, flat, P(), flat, flat, rows, rows, rows, rows)
    in_specs += (flat, rows, rows, rows, rows, flat, rows, rows, rows)
    out_specs = (rows, rows, rows, flat, flat, rows, rows, rows, rows)
    out_specs += (flat, rows, rows, rows, rows, flat, rows, rows)
    return jax.shard_map(
        functools.partial(shards, mesh.shape["dp"], mesh.shape["fsdp"]),
        mesh=mesh,
        in_specs=in_specs,
        out_specs=out_specs,
        check_vma=False,
    )
```

```python
import functools

import jax
import jax.numpy as jnp
from jax import lax
from jax.experimental import pallas as pl
from jax.experimental.pallas import tpu as pltpu
from jax.sharding import PartitionSpec as P

D = 768
H = 12
DH = 64
NB = 32
TGT = 32
QPD = 4
GROUPS = 3
TILE = 256
CHUNKS = 16
stage_orders = ("zxy", "zyx", "xyz")

epsilon = 1e-06
masked_score = -1e30
both = ("dp", "fsdp")
bf16 = jnp.bfloat16
f32 = jnp.float32


def matmul(left_side, right_side):
    return jnp.dot(left_side, right_side, preferred_element_type=f32)


def dot_tn(left_side, right_side):
    return lax.dot_general(
        left_side, right_side, (((0,), (0,)), ((), ())), preferred_element_type=f32
    )


def dot_nt(left_side, right_side):
    return lax.dot_general(
        left_side, right_side, (((1,), (1,)), ((), ())), preferred_element_type=f32
    )


def rms_norm(values, gain_vector):
    return (
        values
        * lax.rsqrt(jnp.mean(values * values, axis=-1, keepdims=True) + epsilon)
        * gain_vector
    )


def pieces_of(values):
    high = values.astype(bf16)
    rest = values - high.astype(f32)
    mid = rest.astype(bf16)
    low = (rest - mid.astype(f32)).astype(bf16)
    return high, mid, low


def split_pieces(values):
    high = lax.reduce_precision(values, 8, 7)
    mid = lax.reduce_precision(values - high, 8, 7)
    low = values - high - mid
    return high.astype(bf16), mid.astype(bf16), low.astype(bf16)


def spread_heads(rows):
    tall = jnp.concatenate([rows, rows, rows, rows], axis=0)
    head_row = lax.broadcasted_iota(jnp.int32, (4 * TGT, 4 * DH), 0) // TGT
    head_col = lax.broadcasted_iota(jnp.int32, (4 * TGT, 4 * DH), 1) // DH
    return jnp.where(head_row == head_col, tall, jnp.zeros_like(tall))


def gather_heads(tall):
    head_col = lax.broadcasted_iota(jnp.int32, (TGT, 4 * DH), 1) // DH
    rows = jnp.zeros((TGT, 4 * DH), f32)
    for head in range(4):
        rows = jnp.where(head_col == head, tall[head * TGT : (head + 1) * TGT], rows)
    return rows


def run_tiles(bounds_ref, block, query, slot):
    start = bounds_ref[block, query]
    end = bounds_ref[block, query + 1]
    first = (start // 16) * 16
    count = (end - first + TILE - 1) // TILE
    return start, end, first, count


def tile_rows(first, step, start, end, slot):
    want = first + step * TILE
    base = pl.multiple_of(jnp.minimum(want, slot - TILE), 16)
    rows = base + lax.broadcasted_iota(jnp.int32, (TILE, 4 * TGT), 0)
    inside = (rows >= jnp.maximum(start, want)) & (rows < end)
    return base, inside


def column_of(row):
    return jnp.transpose(jnp.broadcast_to(row, (8, 4 * TGT)))[:, :1]


def mix_kernel(slot, bounds_ref, place_ref, q_ref, k_ref, v_ref, o_ref, score_ref, mix_ref):
    block = pl.program_id(0)
    lane = lax.broadcasted_iota(jnp.int32, (TGT, 128), 1)
    runs = [run_tiles(bounds_ref, block, query, slot) for query in range(QPD)]
    steps = functools.reduce(jnp.maximum, [run[3] for run in runs])
    pairs = [(query, g) for query in range(QPD) for g in range(GROUPS)]
    spread = {
        (query, g): spread_heads(
            q_ref[0, query * TGT : (query + 1) * TGT, g * 256 : (g + 1) * 256]
        )
        for query, g in pairs
    }

    def score_step(step, tops):
        held = pl.ds(pl.multiple_of(step * TILE, TILE), TILE)
        places = [tile_rows(first, step, start, end, slot) for start, end, first, count in runs]
        new_tops = []
        for i, (query, g) in enumerate(pairs):
            base, inside = places[query]
            keys = k_ref[0, pl.ds(base, TILE), g * 256 : (g + 1) * 256]
            scores = jnp.where(inside, dot_nt(keys, spread[query, g]), masked_score)
            score_ref[i, held, :] = scores
            new_tops.append(jnp.maximum(tops[i], jnp.max(scores, axis=0, keepdims=True)))
        return tuple(new_tops)

    tops = lax.fori_loop(
        0, steps, score_step, tuple(jnp.full((1, 4 * TGT), masked_score, f32) for pair in pairs)
    )
    mix_ref[...] = jnp.zeros_like(mix_ref)

    def mix_step(step, sums):
        held = pl.ds(pl.multiple_of(step * TILE, TILE), TILE)
        places = [tile_rows(first, step, start, end, slot) for start, end, first, count in runs]
        new_sums, raised = [], []
        for i in range(len(pairs)):
            weights = jnp.exp(score_ref[i, held, :] - tops[i])
            new_sums.append(sums[i] + jnp.sum(weights, axis=0, keepdims=True))
            raised.append(weights.astype(bf16))
        for i, (query, g) in enumerate(pairs):
            values = v_ref[0, pl.ds(places[query][0], TILE), g * 256 : (g + 1) * 256]
            mix_ref[i] += dot_tn(raised[i], values)
        return tuple(new_sums)

    sums = lax.fori_loop(
        0, steps, mix_step, tuple(jnp.zeros((1, 4 * TGT), f32) for pair in pairs)
    )
    total, top = jnp.concatenate(sums, axis=0), jnp.concatenate(tops, axis=0)
    scales = jnp.transpose(1.0 / total)
    log_sums = jnp.transpose(top + jnp.log(total))
    for query in range(QPD):
        rows_of = slice(query * TGT, (query + 1) * TGT)
        logs = jnp.zeros((TGT, 128), f32)
        for g in range(GROUPS):
            i = query * GROUPS + g
            scale = scales[:, i : i + 1]
            log_sum = log_sums[:, i : i + 1]
            o_ref[0, rows_of, g * 256 : (g + 1) * 256] = gather_heads(mix_ref[i] * scale).astype(
                bf16
            )
            for head in range(4):
                logs = jnp.where(
                    (lane % 16 == g * 4 + head) & (lane < 48),
                    log_sum[head * TGT : (head + 1) * TGT],
                    logs,
                )
        high, mid, low = pieces_of(logs)
        o_ref[0, rows_of, D:] = jnp.where(
            lane < 16, high.astype(f32), jnp.where(lane < 32, mid.astype(f32), low.astype(f32))
        ).astype(bf16)


def grad_kernel(
    slot,
    bounds_ref,
    order_ref,
    q_ref,
    m_ref,
    place_ref,
    k_ref,
    v_ref,
    dq_ref,
    dk_ref,
    dv_ref,
    sum_ref,
):
    block = pl.program_id(0)
    dk_ref[...] = jnp.zeros_like(dk_ref)
    dv_ref[...] = jnp.zeros_like(dv_ref)
    sum_ref[...] = jnp.zeros_like(sum_ref)
    runs = [run_tiles(bounds_ref, block, query, slot) for query in range(QPD)]
    steps = functools.reduce(jnp.maximum, [run[3] for run in runs])
    pairs = [(query, g) for query in range(QPD) for g in range(GROUPS)]
    row = lax.broadcasted_iota(jnp.int32, (TGT, 2 * H * TGT), 0)
    target = lax.broadcasted_iota(jnp.int32, (TGT, 2 * H * TGT), 1) % TGT
    spread, spread_m, logs, deltas = {}, {}, {}, {}
    for query in range(QPD):
        rows_of = slice(query * TGT, (query + 1) * TGT)
        placed = matmul(m_ref[0, rows_of, D : D + 128], place_ref[...])
        flat = jnp.sum(jnp.where(row == target, placed, 0.0), axis=0, keepdims=True)
        for g in range(GROUPS):
            columns = slice(g * 256, (g + 1) * 256)
            spread[query, g] = spread_heads(q_ref[0, rows_of, columns])
            spread_m[query, g] = spread_heads(m_ref[0, rows_of, columns])
            logs[query, g] = flat[:, g * 128 : (g + 1) * 128]
            deltas[query, g] = flat[:, (GROUPS + g) * 128 : (GROUPS + g + 1) * 128]

    def step_of(step, carry):
        places = [tile_rows(first, step, start, end, slot) for start, end, first, count in runs]
        softs, changes = [], []
        for query, g in pairs:
            base, inside = places[query]
            columns = slice(g * 256, (g + 1) * 256)
            scores = dot_nt(k_ref[0, pl.ds(base, TILE), columns], spread[query, g])
            soft = jnp.where(inside, jnp.exp(scores - logs[query, g]), 0.0)
            d_soft = dot_nt(v_ref[0, pl.ds(base, TILE), columns], spread_m[query, g])
            changes.append((soft * (d_soft - deltas[query, g])).astype(bf16))
            softs.append(soft.astype(bf16))
        for i, (query, g) in enumerate(pairs):
            keys = k_ref[0, pl.ds(places[query][0], TILE), g * 256 : (g + 1) * 256]
            sum_ref[i] += dot_tn(changes[i], keys)
        for i, (query, g) in enumerate(pairs):
            rows_of, columns = pl.ds(places[query][0], TILE), slice(g * 256, (g + 1) * 256)
            dk_ref[0, rows_of, columns] += matmul(changes[i], spread[query, g]).astype(bf16)
            dv_ref[0, rows_of, columns] += matmul(softs[i], spread_m[query, g]).astype(bf16)
        return carry

    lax.fori_loop(0, steps, step_of, 0)
    for query in range(QPD):
        rows_of = slice(query * TGT, (query + 1) * TGT)
        d_query = jnp.concatenate(
            [gather_heads(sum_ref[query * GROUPS + g]) for g in range(GROUPS)], axis=1
        )
        dq_ref[0, 0, rows_of, :] = d_query[:, : D // 2].astype(bf16)
        dq_ref[1, 0, rows_of, :] = d_query[:, D // 2 :].astype(bf16)


def cross_mix(bounds, arrival, queries, keys, values):
    blocks, slot = keys.shape[0], keys.shape[1]
    rows = queries.shape[1]
    at = lambda i, *refs: (i, 0, 0)
    come = lambda i, bounds_ref, order_ref: (order_ref[i], 0, 0)
    return pl.pallas_call(
        functools.partial(mix_kernel, slot),
        grid_spec=pltpu.PrefetchScalarGridSpec(
            num_scalar_prefetch=2,
            grid=(blocks,),
            in_specs=[
                pl.BlockSpec((1, rows, D), come),
                pl.BlockSpec((1, slot, D), at),
                pl.BlockSpec((1, slot, D), at),
            ],
            out_specs=[pl.BlockSpec((1, rows, D + 128), at)],
            scratch_shapes=[
                pltpu.VMEM((QPD * GROUPS, slot + TILE, 4 * TGT), f32),
                pltpu.VMEM((QPD * GROUPS, 4 * TGT, 256), f32),
            ],
        ),
        out_shape=[
            jax.ShapeDtypeStruct((blocks, rows, D + 128), bf16),
        ],
        compiler_params=pltpu.CompilerParams(vmem_limit_bytes=60 * 1024 * 1024),
        cost_estimate=pl.CostEstimate(
            flops=12_000_000_000, bytes_accessed=22_000_000, transcendentals=4_000_000
        ),
        name="cross_mix",
    )(bounds, arrival, queries, keys, values)[0]


def cross_grad(bounds, arrival, queries, mixed, place, keys, values):
    blocks, slot = keys.shape[0], keys.shape[1]
    rows = queries.shape[1]
    at = lambda i, *refs: (i, 0, 0)
    come = lambda i, bounds_ref, order_ref: (order_ref[i], 0, 0)
    return pl.pallas_call(
        functools.partial(grad_kernel, slot),
        grid_spec=pltpu.PrefetchScalarGridSpec(
            num_scalar_prefetch=2,
            grid=(blocks,),
            in_specs=[
                pl.BlockSpec((1, rows, D), come),
                pl.BlockSpec((1, rows, D + 128), come),
                pl.BlockSpec((128, 2 * H * TGT), lambda i, *refs: (0, 0)),
                pl.BlockSpec((1, slot, D), at),
                pl.BlockSpec((1, slot, D), at),
            ],
            out_specs=[
                pl.BlockSpec((2, 1, rows, D // 2), lambda i, b, order_ref: (0, order_ref[i], 0, 0)),
                pl.BlockSpec((1, slot, D), at),
                pl.BlockSpec((1, slot, D), at),
            ],
            scratch_shapes=[pltpu.VMEM((QPD * GROUPS, 4 * TGT, 256), f32)],
        ),
        out_shape=[
            jax.ShapeDtypeStruct((2, blocks, rows, D // 2), bf16),
            jax.ShapeDtypeStruct((blocks, slot, D), bf16),
            jax.ShapeDtypeStruct((blocks, slot, D), bf16),
        ],
        compiler_params=pltpu.CompilerParams(vmem_limit_bytes=60 * 1024 * 1024),
        cost_estimate=pl.CostEstimate(
            flops=24_000_000_000, bytes_accessed=42_000_000, transcendentals=4_000_000
        ),
        name="cross_grad",
    )(bounds, arrival, queries, mixed, place, keys, values)


def flag_of(orders_ref):
    return orders_ref[6 * CHUNKS]


def start_load(orders_ref, order, mine_ref, other_ref, columns, into, sem):
    chunks, rows = mine_ref.shape[0], mine_ref.shape[1]
    width = columns.stop - columns.start
    for part, source in enumerate((mine_ref, other_ref)):
        half = flag_of(orders_ref) if part == 0 else 1 - flag_of(orders_ref)
        for i in range(chunks):
            base = pl.multiple_of(orders_ref[order * CHUNKS + i] * rows, 16)
            pltpu.make_async_copy(
                source.at[i, :, columns],
                into.at[pl.ds(base, rows), pl.ds(pl.multiple_of(half * width, 128), width)],
                sem,
            ).start()


def wait_load(into, sem):
    pltpu.make_async_copy(into, into, sem).wait()


def store_grad(orders_ref, order, grad, mine_ref, other_ref, columns):
    chunks, rows = mine_ref.shape[0], mine_ref.shape[1]
    width = columns.stop - columns.start
    first = flag_of(orders_ref) == 0
    for i in range(chunks):
        to = orders_ref[(3 + order) * CHUNKS + i]
        left = grad[i * rows : (i + 1) * rows, :width]
        right = grad[i * rows : (i + 1) * rows, width:]
        mine_ref[to, :, columns] = jnp.where(first, left, right).astype(bf16)
        other_ref[to, :, columns] = jnp.where(first, right, left).astype(bf16)


def iota(shape, axis):
    return lax.broadcasted_iota(jnp.int32, shape, axis)


def project_kernel(order, orders_ref, enc_ref, a_ref, b_ref, out_ref, w_ref, sems):
    @pl.when(pl.program_id(0) == 0)
    def load():
        start_load(orders_ref, order, a_ref, b_ref, slice(D, D + D // 2), w_ref, sems.at[0])
        wait_load(w_ref, sems.at[0])

    out_ref[0] = matmul(enc_ref[...], w_ref[...]).astype(bf16)


def encode_grad_kernel(orders_ref, dk_ref, dv_ref, ka_ref, kb_ref, va_ref, vb_ref, out_ref, w_ref, sems):
    @pl.when(pl.program_id(0) == 0)
    def load():
        start_load(orders_ref, 0, ka_ref, kb_ref, slice(D, D + D // 2), w_ref.at[0], sems.at[0])
        start_load(orders_ref, 1, va_ref, vb_ref, slice(D, D + D // 2), w_ref.at[1], sems.at[1])
        wait_load(w_ref.at[0], sems.at[0])
        wait_load(w_ref.at[1], sems.at[1])

    out_ref[...] = (dot_nt(dk_ref[0], w_ref[0]) + dot_nt(dv_ref[0], w_ref[1])).astype(bf16)


def weight_grad_kernel(steps, order, orders_ref, enc_ref, d_ref, mine_ref, other_ref, sum_ref):
    step = pl.program_id(0)
    product = dot_tn(enc_ref[...], d_ref[0])

    @pl.when(step == 0)
    def first():
        sum_ref[...] = product

    @pl.when(step > 0)
    def later():
        sum_ref[...] += product

    @pl.when(step == steps - 1)
    def store():
        store_grad(orders_ref, order, sum_ref, mine_ref, other_ref, slice(0, D // 2))


def self_kernel(
    orders_ref,
    states_ref,
    buckets_ref,
    aa_ref,
    ab_ref,
    ba_ref,
    bb_ref,
    ca_ref,
    cb_ref,
    normed_ref,
    q_ref,
    k_ref,
    v_ref,
    mixed_ref,
    first_ref,
    normed_cross_ref,
    q_cross_ref,
    gains_ref,
    bias_ref,
    w_ref,
    small_ref,
    sems,
):
    half = D // 2
    start_load(orders_ref, 2, ca_ref, cb_ref, slice(half, half + 128), small_ref, sems.at[5])
    start_load(orders_ref, 0, aa_ref, ab_ref, slice(0, half), w_ref.at[0], sems.at[0])
    start_load(orders_ref, 0, aa_ref, ab_ref, slice(half, D), w_ref.at[1], sems.at[1])
    start_load(orders_ref, 1, ba_ref, bb_ref, slice(0, half), w_ref.at[2], sems.at[2])
    start_load(orders_ref, 1, ba_ref, bb_ref, slice(half, D), w_ref.at[3], sems.at[3])
    start_load(orders_ref, 2, ca_ref, cb_ref, slice(0, half), w_ref.at[4], sems.at[4])
    wait_load(small_ref, sems.at[5])
    small = small_ref[:, :128]
    gains_ref[...] = jnp.transpose(small.astype(f32))[:8]
    span = D // NB
    first_row, row = span * iota((NB, D), 0), iota((NB, D), 1)
    pick = ((row >= first_row) & (row < first_row + span)).astype(f32).astype(bf16)
    table = matmul(pick, small).astype(bf16)
    wide = (iota((128, H * TGT), 0) == 16 + (iota((128, H * TGT), 1) >> 5)).astype(f32).astype(bf16)
    table = matmul(table, wide)
    buckets = buckets_ref[...]
    later = iota((TGT, 128), 0) > (iota((TGT, 128), 1) & (TGT - 1))
    for g in range(GROUPS):
        bias = jnp.zeros((TGT, 128), f32)
        for n in range(NB):
            bias = jnp.where(buckets == n, table[n : n + 1, g * 128 : (g + 1) * 128], bias)
        bias_ref[:, g * 128 : (g + 1) * 128] = jnp.where(later, masked_score, bias)

    states = states_ref[...].astype(f32)
    normed = rms_norm(states, gains_ref[0:1]).astype(bf16)
    normed_ref[...] = normed
    wait_load(w_ref.at[0], sems.at[0])
    q_ref[...] = matmul(normed, w_ref[0]).astype(bf16)
    wait_load(w_ref.at[1], sems.at[1])
    k_ref[...] = matmul(normed, w_ref[1]).astype(bf16)
    wait_load(w_ref.at[2], sems.at[2])
    v_ref[...] = matmul(normed, w_ref[2]).astype(bf16)
    for query in range(QPD):
        rows_of = slice(query * TGT, (query + 1) * TGT)
        for g in range(GROUPS):
            columns = slice(g * 256, (g + 1) * 256)
            spread = spread_heads(q_ref[rows_of, columns])
            scores = dot_nt(k_ref[rows_of, columns], spread) + bias_ref[:, g * 128 : (g + 1) * 128]
            raised = jnp.exp(scores - jnp.max(scores, axis=0, keepdims=True))
            soft = raised / jnp.sum(raised, axis=0, keepdims=True)
            tall = dot_tn(soft.astype(bf16), v_ref[rows_of, columns])
            mixed_ref[rows_of, columns] = gather_heads(tall).astype(bf16)
    wait_load(w_ref.at[3], sems.at[3])
    first = states + matmul(mixed_ref[...], w_ref[3])
    first_ref[...] = first
    normed_cross = rms_norm(first, gains_ref[1:2]).astype(bf16)
    normed_cross_ref[...] = normed_cross
    wait_load(w_ref.at[4], sems.at[4])
    q_cross_ref[...] = matmul(normed_cross, w_ref[4]).astype(bf16)


def exact_sum(values, picks):
    high, mid, low = pieces_of(values)
    return matmul(high, picks) + matmul(mid, picks) + matmul(low, picks)


def norm_back(values, gain, d_normed):
    scale = lax.rsqrt(jnp.mean(values * values, axis=-1, keepdims=True) + epsilon)
    scaled = d_normed * gain
    inner = jnp.mean(scaled * values, axis=-1, keepdims=True)
    d_values = scale * scaled - values * (scale * scale * scale * inner)
    d_gain = jnp.sum(d_normed * values * scale, axis=0, keepdims=True)
    return d_values, d_gain


def feed_kernel(
    back_ref,
    first_ref,
    cot_ref,
    gains_ref,
    fi_ref,
    fo_ref,
    co_ref,
    out_ref,
    send_ref,
    second_ref,
    branch_ref,
    mixed_ref,
    normed_ref,
    hidden_ref,
    pre_ref,
    gain_ref,
    wc_ref,
    wi_ref,
    wo_ref,
    logs_ref,
    sems,
):
    blocks, rows = back_ref.shape[0], back_ref.shape[1]
    copies = [
        pltpu.make_async_copy(source, into, sems.at[i])
        for i, (source, into) in enumerate(((co_ref, wc_ref), (fi_ref, wi_ref), (fo_ref, wo_ref)))
    ]
    for copy in copies:
        copy.start()
    widen = ((iota((128, D), 0) & 15) == (iota((128, D), 1) >> 6)) & (iota((128, D), 0) < 48)
    widen = widen.astype(f32).astype(bf16)

    def log_step(i, top):
        logs = matmul(back_ref[i, :, D:], widen)
        logs_ref[i] = logs
        return jnp.maximum(top, logs)

    top = lax.fori_loop(0, blocks, log_step, jnp.full((rows, D), masked_score, f32))

    def share_step(i, carry):
        total, mixed = carry
        share = jnp.exp(logs_ref[i] - top)
        return total + share, mixed + share * back_ref[i, :, :D].astype(f32)

    zero = jnp.zeros((rows, D), f32)
    total, mixed = lax.fori_loop(0, blocks, share_step, (zero, zero))
    mixed = mixed / total
    logs = top + jnp.log(total)
    mixed_ref[...] = mixed.astype(bf16)
    copies[0].wait()
    second = first_ref[...] + matmul(mixed_ref[...], wc_ref[...])
    normed = rms_norm(second, gains_ref[2:3]).astype(bf16)
    normed_ref[...] = normed
    copies[1].wait()
    copies[2].wait()
    cot = cot_ref[...]
    root = 0.7978845608028654

    def feed_step(t, carry):
        out, d_normed = carry
        pre = matmul(normed, wi_ref[t])
        w_out = wo_ref[pl.ds(pl.multiple_of(t * D, D), D), :]
        bent = jnp.tanh(root * (pre + 0.044715 * pre * pre * pre))
        hidden = (0.5 * pre * (1.0 + bent)).astype(bf16)
        slope = 0.5 * (1.0 + bent) + 0.5 * pre * (1.0 - bent * bent) * (
            root * (1.0 + 3 * 0.044715 * pre * pre)
        )
        d_pre = (dot_nt(cot, w_out) * slope).astype(bf16)
        hidden_ref[t] = hidden
        pre_ref[t] = d_pre
        return out + matmul(hidden, w_out), d_normed + dot_nt(d_pre, wi_ref[t])

    out, d_normed = lax.fori_loop(0, 4, feed_step, (zero, zero))
    out_ref[...] = (second + out).astype(bf16)
    d_values, gain_ref[...] = norm_back(second, gains_ref[2:3], d_normed)
    d_second = cot.astype(f32) + d_values
    second_ref[...] = d_second
    branch_ref[...] = d_second.astype(bf16)
    d_mixed = dot_nt(branch_ref[...], wc_ref[...]).astype(bf16)
    send_ref[:, :D] = d_mixed
    lane = iota((D, 128), 1)
    row = iota((D, 128), 0)
    pick = ((row == (lane & 15) * DH) & (lane < 48)).astype(f32).astype(bf16)
    add = (((row >> 6) == (lane & 15)) & (lane >= 48) & (lane < 96)).astype(f32).astype(bf16)
    extra = exact_sum(logs, pick) + exact_sum(d_mixed.astype(f32) * mixed, add)
    high, mid, low = pieces_of(extra)
    slot_of = iota((rows, 128), 1) >> 4
    slot_of = jnp.where(slot_of >= 3, slot_of - 3, slot_of)
    send_ref[:, D:] = jnp.where(
        slot_of == 0, high.astype(f32), jnp.where(slot_of == 1, mid.astype(f32), low.astype(f32))
    ).astype(bf16)


def feed_grad_kernel(hidden_ref, pre_ref, normed_ref, mixed_ref, branch_ref, cot_ref, out_ref):
    blocks, slabs, part, width = out_ref.shape

    def put(grad, block, slab, row):
        out_ref[block, slab] = grad[row : row + part].astype(bf16)

    for t in range(4):
        grad = dot_tn(normed_ref[...], pre_ref[t])
        for i in range(blocks):
            put(grad, i, t, i * part)
        grad = dot_tn(hidden_ref[t], cot_ref[...])
        for i in range(blocks):
            place = t * blocks + i
            put(grad, place // 4, 4 + place % 4, i * part)
    grad = dot_tn(mixed_ref[...], branch_ref[...])
    for i in range(blocks):
        put(grad, i, 8, i * part)


def self_grad_kernel(
    orders_ref,
    back_ref,
    second_ref,
    first_ref,
    states_ref,
    normed_cross_ref,
    normed_ref,
    q_ref,
    k_ref,
    v_ref,
    mixed_ref,
    gains_ref,
    bias_ref,
    buckets_ref,
    gain_feed_ref,
    aa_ref,
    ab_ref,
    ba_ref,
    bb_ref,
    ca_ref,
    cb_ref,
    out_ref,
    ga_ref,
    ha_ref,
    gb_ref,
    hb_ref,
    gc_ref,
    hc_ref,
    w_ref,
    dq_ref,
    dk_ref,
    dv_ref,
    dm_ref,
    sums_ref,
    sems,
):
    half = D // 2
    start_load(orders_ref, 2, ca_ref, cb_ref, slice(0, half), w_ref.at[4], sems.at[4])
    start_load(orders_ref, 1, ba_ref, bb_ref, slice(half, D), w_ref.at[3], sems.at[3])
    start_load(orders_ref, 0, aa_ref, ab_ref, slice(0, half), w_ref.at[0], sems.at[0])
    start_load(orders_ref, 0, aa_ref, ab_ref, slice(half, D), w_ref.at[1], sems.at[1])
    start_load(orders_ref, 1, ba_ref, bb_ref, slice(0, half), w_ref.at[2], sems.at[2])

    d_query = back_ref[...].astype(bf16)
    store_grad(orders_ref, 2, dot_tn(normed_cross_ref[...], d_query), gc_ref, hc_ref, slice(0, half))
    wait_load(w_ref.at[4], sems.at[4])
    d_values, gain_cross = norm_back(first_ref[...], gains_ref[1:2], dot_nt(d_query, w_ref[4]))
    d_first = second_ref[...] + d_values
    branch = d_first.astype(bf16)
    store_grad(orders_ref, 1, dot_tn(mixed_ref[...], branch), gb_ref, hb_ref, slice(half, D))
    wait_load(w_ref.at[3], sems.at[3])
    dm_ref[...] = dot_nt(branch, w_ref[3]).astype(bf16)
    sums_ref[...] = jnp.zeros_like(sums_ref)
    for query in range(QPD):
        rows_of = slice(query * TGT, (query + 1) * TGT)
        for g in range(GROUPS):
            columns = slice(g * 256, (g + 1) * 256)
            lanes = slice(g * 128, (g + 1) * 128)
            spread = spread_heads(q_ref[rows_of, columns])
            spread_m = spread_heads(dm_ref[rows_of, columns])
            keys = k_ref[rows_of, columns]
            scores = dot_nt(keys, spread) + bias_ref[:, lanes]
            raised = jnp.exp(scores - jnp.max(scores, axis=0, keepdims=True))
            soft = raised / jnp.sum(raised, axis=0, keepdims=True)
            d_soft = dot_nt(v_ref[rows_of, columns], spread_m)
            delta = jnp.sum(soft * d_soft, axis=0, keepdims=True)
            d_scores = (soft * (d_soft - delta)).astype(bf16)
            sums_ref[:, lanes] += d_scores.astype(f32)
            dq_ref[rows_of, columns] = gather_heads(dot_tn(d_scores, keys)).astype(bf16)
            dk_ref[rows_of, columns] = matmul(d_scores, spread).astype(bf16)
            dv_ref[rows_of, columns] = matmul(soft.astype(bf16), spread_m).astype(bf16)
    normed = normed_ref[...]
    store_grad(orders_ref, 0, dot_tn(normed, dq_ref[...]), ga_ref, ha_ref, slice(0, half))
    store_grad(orders_ref, 0, dot_tn(normed, dk_ref[...]), ga_ref, ha_ref, slice(half, D))
    store_grad(orders_ref, 1, dot_tn(normed, dv_ref[...]), gb_ref, hb_ref, slice(0, half))
    wait_load(w_ref.at[0], sems.at[0])
    wait_load(w_ref.at[1], sems.at[1])
    wait_load(w_ref.at[2], sems.at[2])
    d_normed = (
        dot_nt(dq_ref[...], w_ref[0]) + dot_nt(dk_ref[...], w_ref[1]) + dot_nt(dv_ref[...], w_ref[2])
    )
    d_values, gain_self = norm_back(states_ref[...].astype(f32), gains_ref[0:1], d_normed)
    out_ref[...] = (d_first + d_values).astype(bf16)
    buckets = buckets_ref[...]
    by_bucket = []
    for n in range(NB):
        sums = []
        for g in range(GROUPS):
            mine = jnp.where(buckets == n, sums_ref[:, g * 128 : (g + 1) * 128], 0.0)
            sums.append(jnp.sum(mine, axis=0, keepdims=True))
        by_bucket.append(jnp.concatenate(sums, axis=1))
    by_bucket = jnp.concatenate(by_bucket, axis=0)
    lane = iota((H * TGT, 128), 1)
    narrow = ((iota((H * TGT, 128), 0) >> 5) == lane - 16).astype(f32).astype(bf16)
    table = exact_sum(by_bucket, narrow).astype(bf16)
    span = D // NB
    first_row, row = span * iota((D, NB), 1), iota((D, NB), 0)
    put = ((row >= first_row) & (row < first_row + span)).astype(f32).astype(bf16)
    gains = jnp.concatenate([gain_self, gain_cross, gain_feed_ref[...], jnp.zeros((125, D), f32)])
    small = matmul(put, table) + jnp.transpose(gains)
    small = jnp.concatenate([small, jnp.zeros_like(small)], axis=1)
    store_grad(orders_ref, 2, small, gc_ref, hc_ref, slice(half, half + 128))


hbm = pl.BlockSpec(memory_space=pl.ANY)
vmem = pl.BlockSpec(memory_space=pltpu.VMEM)
smem = pl.BlockSpec(memory_space=pltpu.SMEM)


def like(shape, kind=bf16):
    return jax.ShapeDtypeStruct(shape, kind)


def call(kernel, name, ins, outs, scratch, flops, moved, *values, **more):
    return pl.pallas_call(
        kernel,
        in_specs=ins,
        out_shape=outs,
        scratch_shapes=scratch,
        compiler_params=pltpu.CompilerParams(vmem_limit_bytes=60 * 1024 * 1024),
        cost_estimate=pl.CostEstimate(flops=flops, bytes_accessed=moved, transcendentals=0),
        name=name,
        **more,
    )(*values)


def weights(*shape):
    return pltpu.VMEM(shape, bf16)


class Wires:
    def __init__(self, n_dp, n_fsdp):
        self.n_dp, self.n_fsdp = n_dp, n_fsdp
        self.sizes = {"x": n_fsdp // 2, "y": n_fsdp // 2, "z": n_dp // (n_fsdp // 2), "c": 2}
        dp, fsdp = lax.axis_index("dp"), lax.axis_index("fsdp")
        size = self.sizes
        self.at = {"z": dp // size["x"], "x": dp % size["x"], "y": fsdp // 2, "c": fsdp % 2}

    def shift(self, value, axis):
        size = self.sizes
        pairs = []
        for dp in range(self.n_dp):
            for fsdp in range(self.n_fsdp):
                at = {"z": dp // size["x"], "x": dp % size["x"], "y": fsdp // 2, "c": fsdp % 2}
                here = dp * self.n_fsdp + fsdp
                at[axis] = (at[axis] + 1) % size[axis]
                there = (at["z"] * size["x"] + at["x"]) * self.n_fsdp + at["y"] * 2 + at["c"]
                pairs.append((here, there))
        return lax.ppermute(value, both, pairs)

    def around(self, value, axis):
        found = [value]
        while len(found) < self.sizes[axis]:
            found.append(self.shift(found[-1], axis))
        return found

    def gather_dp(self, value):
        found = []
        for held in self.around(value, "z"):
            found += self.around(held, "x")
        return jnp.stack(found)

    def scatter_dp(self, value, beside):
        size = self.sizes
        left, right = (
            value[i].reshape((size["z"], size["x"]) + value.shape[2:]) for i in range(2)
        )

        def walk(value, first, second):
            held = yield from self.sum_walk(value, first, bf16)
            return (yield from self.sum_walk(held, second, f32))

        low, high, *made = self.together(
            walk(left.swapaxes(0, 1), "x", "z"), walk(right, "z", "x"), beside=beside
        )
        return jnp.concatenate([low, high], axis=1), made

    def arrival(self):
        size = self.sizes
        dp = jnp.arange(self.n_dp, dtype=jnp.int32)
        z_back = (self.at["z"] - dp // size["x"]) % size["z"]
        x_back = (self.at["x"] - dp % size["x"]) % size["x"]
        return z_back * size["x"] + x_back

    def orders(self):
        size = self.sizes
        chunk = jnp.arange(CHUNKS, dtype=jnp.int32)
        y, x, z = chunk % size["y"], chunk // size["y"] % size["x"], chunk // size["y"] // size["x"]
        places = []
        for order in stage_orders:
            place = jnp.zeros_like(chunk)
            for axis in reversed(order):
                value = {"x": x, "y": y, "z": z}[axis]
                place = place * size[axis] + (self.at[axis] - value) % size[axis]
            places.append(place)
        chunks = [jnp.sum(jnp.where(p[:, None] == chunk[None, :], chunk[:, None], 0), 0) for p in places]
        flat = jnp.concatenate(chunks + places + [self.at["c"][None]])
        return jnp.pad(flat, (0, 128 - flat.shape[0])).astype(jnp.int32)

    def together(self, *walks, beside=()):
        asks = {i: next(walk) for i, walk in enumerate(walks)}
        results = [None] * len(walks)
        made = []
        step = 0
        while asks:
            got = [self.shift(value, axis) for value, axis in asks.values()]
            if step < len(beside) and beside[step] is not None:
                made.append(beside[step]())
                got, made[-1] = lax.optimization_barrier((got, made[-1]))
            else:
                got = lax.optimization_barrier(tuple(got))
            left = {}
            for i, value in zip(list(asks), got):
                try:
                    left[i] = walks[i].send(value)
                except StopIteration as end:
                    results[i] = end.value
            asks = left
            step += 1
        return results + made

    def gather_walk(self, left, right, order):
        core = self.at["c"]
        mine = jnp.where(core == 0, left, right)
        other = yield jnp.where(core == 0, right, left), "c"
        low, high = jnp.where(core == 0, mine, other), jnp.where(core == 0, other, mine)
        held = jnp.concatenate([low, high], axis=0)[None]
        for axis in stage_orders[order]:
            found = [held]
            while len(found) < self.sizes[axis]:
                found.append((yield found[-1], axis))
            held = jnp.concatenate(found, axis=0)
        other = yield held, "c"
        return held, other

    def gather(self, packs):
        return self.together(*(self.gather_walk(*pack, i) for i, pack in enumerate(packs)))

    def sum_walk(self, value, axis, kind):
        n = value.shape[0]
        moving = value[1]
        for step in range(2, n + 1):
            got = yield moving, axis
            moving = plus(got, value[step % n], kind if step == n else bf16)
        return moving

    def scatter_walk(self, grad, order):
        other = yield grad[1], "c"
        held = plus(grad[0], other)
        for stage, axis in enumerate(reversed(stage_orders[order])):
            value = held.reshape((self.sizes[axis], -1) + held.shape[1:])
            held = yield from self.sum_walk(value, axis, f32 if stage == 2 else bf16)
        core = self.at["c"]
        low, high = jnp.split(held[0], 2, axis=0)
        mine = jnp.where(core == 0, low, high)
        other = yield jnp.where(core == 0, high, low), "c"
        return jnp.where(core == 0, mine, other), jnp.where(core == 0, other, mine)

    def scatter(self, grads, beside):
        walks = (self.scatter_walk(grad, order) for order, grad in grads)
        return self.together(*walks, beside=beside)


def plus(one, two, kind=bf16):
    return (one.astype(f32) + two.astype(f32)).astype(kind)


class Plain:
    def __init__(self, wires):
        self.wires = wires

    def orders(self):
        return jnp.zeros((128,), jnp.int32)

    def gather(self, packs):
        return [
            tuple(lax.all_gather(part, both, axis=0, tiled=True)[None] for part in pack)
            for pack in packs
        ]

    def scatter(self, grads, beside):
        parts = [part[0] for order, grad in grads for part in grad]
        whole = jnp.concatenate(parts, axis=1)
        whole = lax.psum_scatter(whole, both, scatter_dimension=0, tiled=True).astype(f32)
        ends = [0]
        for part in parts:
            ends.append(ends[-1] + part.shape[1])
        sums = [whole[:, low:high] for low, high in zip(ends[:-1], ends[1:])]
        return list(zip(sums[::2], sums[1::2])) + [make() for make in beside if make]


def halves(value):
    middle = value.shape[1] // 2
    return value[:, :middle], value[:, middle:]


def pack(*values):
    parts = [halves(value) for value in values]
    return tuple(jnp.concatenate([part[i] for part in parts], axis=1) for i in range(2))


def shards(
    n_dp,
    n_fsdp,
    decoder_states,
    encodings,
    owner_query,
    buckets,
    gain_self,
    bias_table,
    self_query,
    self_key,
    self_value,
    self_output,
    gain_cross,
    cross_query,
    cross_key,
    cross_value,
    cross_output,
    gain_feed,
    feed_in,
    feed_out,
    cotangent,
):
    n_dev = n_dp * n_fsdp
    wires = Wires(n_dp, n_fsdp)
    chunks = n_dev // 2 if D % (n_dev // 2 * 16) == 0 and n_dev // 2 == CHUNKS else 1
    moves = wires if chunks > 1 else Plain(wires)
    rows = decoder_states.shape[0]
    keys_total = encodings.shape[0]
    slot = keys_total // n_dp
    part = D // n_dev
    bias_part = bias_table.shape[0]
    orders = moves.orders()
    half = D // 2

    device = lax.axis_index("dp") * n_fsdp + lax.axis_index("fsdp")
    lane = jnp.arange(256, dtype=jnp.int32)
    entry = device * bias_part + jnp.arange(bias_part, dtype=jnp.int32)
    spot = (16 + entry % H)[:, None] == lane[None, :]
    small = jnp.sum(jnp.where(spot, bias_table[:, None].astype(f32), 0.0), axis=0)
    small = jnp.where(jnp.arange(part)[:, None] == 0, small[None, :], 0.0)
    for i, gain in enumerate((gain_self, gain_cross, gain_feed)):
        small = jnp.where(lane[None, :] == i, gain[:, None].astype(f32), small)
    small = small.astype(bf16)
    first_weights = moves.gather(
        [
            pack(self_query, self_key, cross_key),
            pack(self_value, self_output, cross_value),
            pack(cross_query, small),
        ]
    )
    feed_pack = jnp.concatenate(
        [feed_in[:, t * D : (t + 1) * D] for t in range(4)] + [feed_out, cross_output], axis=0
    )
    tied = lax.optimization_barrier((feed_pack, first_weights[0][1], first_weights[1][1]))
    feed_pack = lax.all_gather(tied[0], both, axis=0)
    w_feed_in = feed_pack[:, : 4 * part].reshape(n_dev, 4, part, D).transpose(1, 0, 2, 3)
    w_feed_in = w_feed_in.reshape(4, D, D)
    w_feed_out = feed_pack[:, 4 * part : 8 * part].reshape(4 * D, D)
    w_cross_output = feed_pack[:, 8 * part :].reshape(D, D)
    (qk_a, qk_b), (vo_a, vo_b), (cq_a, cq_b) = first_weights

    owner_query, buckets, tied = lax.optimization_barrier((owner_query, buckets, cq_a))
    owners = owner_query.reshape(n_dp, slot)
    ids = (jnp.arange(n_dp, dtype=jnp.int32) * n_fsdp + lax.axis_index("fsdp")) * QPD
    counts = [
        jnp.sum((owners == (ids + n)[:, None]).astype(jnp.int32), axis=1) for n in range(QPD)
    ]
    bounds = jnp.cumsum(
        jnp.stack([jnp.zeros((n_dp,), jnp.int32)] + counts, axis=1), axis=1
    ).astype(jnp.int32)
    arrival = wires.arrival()

    buckets_wide = jnp.tile(buckets.T, (1, 4))
    wide = (rows, D)
    (
        normed_self,
        query_self,
        key_self,
        value_self,
        self_mixed,
        first_residual,
        normed_cross,
        query_cross,
        gains,
        bias,
    ) = call(
        self_kernel,
        "self_forward",
        [smem, vmem, vmem] + [hbm] * 6,
        [like(wide)] * 5
        + [like(wide, f32), like(wide), like(wide), like((8, D), f32), like((TGT, H * TGT), f32)],
        [weights(5, D, D), weights(D, 256), pltpu.SemaphoreType.DMA((6,))],
        1_500_000_000,
        9_000_000,
        orders,
        decoder_states,
        buckets_wide,
        qk_a,
        qk_b,
        vo_a,
        vo_b,
        cq_a,
        cq_b,
    )

    block = pl.BlockSpec((slot, D), lambda i: (i, 0))
    deep = pl.BlockSpec((1, slot, D), lambda i: (i, 0, 0))
    key_cross, value_cross = (
        call(
            functools.partial(project_kernel, order),
            "cross_project",
            [smem, block] + [hbm] * 2,
            like((n_dp, slot, D)),
            [weights(D, D), pltpu.SemaphoreType.DMA((1,))],
            7_300_000_000,
            20_000_000,
            orders,
            encodings,
            *pair,
            grid=(n_dp,),
            out_specs=deep,
        )
        for order, pair in enumerate(((qk_a, qk_b), (vo_a, vo_b)))
    )
    all_queries = wires.gather_dp(query_cross)
    parts = cross_mix(bounds, arrival, all_queries, key_cross, value_cross)
    back = lax.all_to_all(parts, "dp", split_axis=0, concat_axis=0)

    (
        layer_output,
        d_send,
        d_second,
        d_branch,
        cross_mixed,
        normed_feed,
        hidden,
        d_pre,
        grad_gain_feed,
    ) = call(
        feed_kernel,
        "feed_both_ways",
        [vmem, vmem, vmem, vmem] + [hbm] * 3,
        [
            like(wide),
            like((rows, D + 128)),
            like(wide, f32),
            like(wide),
            like(wide),
            like(wide),
            like((4, rows, D)),
            like((4, rows, D)),
            like((1, D), f32),
        ],
        [
            weights(D, D),
            weights(4, D, D),
            weights(4 * D, D),
            pltpu.VMEM((n_dp, rows, D), f32),
            pltpu.SemaphoreType.DMA((3,)),
        ],
        3_000_000_000,
        14_000_000,
        back,
        first_residual,
        cotangent,
        gains,
        w_feed_in,
        w_feed_out,
        w_cross_output,
    )
    blocks = n_dev if part % 8 == 0 else 1
    feed_grad = call(
        feed_grad_kernel,
        "feed_grads",
        [vmem] * 6,
        like((blocks, 9, D // blocks, D)),
        [],
        1_500_000_000,
        14_000_000,
        hidden,
        d_pre,
        normed_feed,
        cross_mixed,
        d_branch,
        cotangent,
    )
    if blocks == 1:
        feed_grad = jnp.concatenate(
            [
                feed_grad[0, :4].reshape(4, n_dev, part, D).transpose(1, 0, 2, 3),
                feed_grad[0, 4:8].reshape(n_dev, 4, part, D),
                feed_grad[0, 8].reshape(n_dev, 1, part, D),
            ],
            axis=1,
        )
    all_mixed, feed_grad = lax.optimization_barrier((wires.gather_dp(d_send), feed_grad))
    feed_sum = lax.psum_scatter(feed_grad, both, scatter_dimension=0).astype(f32)
    lane = lane[:128]
    column = jnp.arange(2 * H * TGT, dtype=jnp.int32)
    place = (
        (lane[:, None] // 48 == column[None, :] // (H * TGT))
        & (lane[:, None] % 16 == (column[None, :] // TGT) % H)
    ).astype(bf16)
    part_query, d_key_cross, d_value_cross = cross_grad(
        bounds, arrival, all_queries, all_mixed, place, key_cross, value_cross
    )
    chunked = pl.BlockSpec((chunks, D // chunks, half), lambda i: (0, 0, 0))

    def weight_grad(order, d_rows):
        return call(
            functools.partial(weight_grad_kernel, n_dp, order),
            "cross_weight_grad",
            [smem, block, deep],
            [like((chunks, D // chunks, half))] * 2,
            [pltpu.VMEM((D, D), f32)],
            7_000_000_000,
            20_000_000,
            orders,
            encodings,
            d_rows,
            grid=(n_dp,),
            out_specs=[chunked, chunked],
        )

    d_query_cross, (grad_cross_key, grad_cross_value) = wires.scatter_dp(
        part_query,
        [lambda: weight_grad(0, d_key_cross), lambda: weight_grad(1, d_value_cross)],
    )
    decoder_grad, *grads = call(
        self_grad_kernel,
        "self_backward",
        [smem] + [vmem] * 14 + [hbm] * 6,
        [
            like(wide),
            *[like((chunks, D // chunks, D))] * 4,
            *[like((chunks, D // chunks, half + 128))] * 2,
        ],
        [
            weights(5, D, D),
            weights(rows, D),
            weights(rows, D),
            weights(rows, D),
            weights(rows, D),
            pltpu.VMEM((TGT, H * TGT), f32),
            pltpu.SemaphoreType.DMA((5,)),
        ],
        3_000_000_000,
        14_000_000,
        orders,
        d_query_cross,
        d_second,
        first_residual,
        decoder_states,
        normed_cross,
        normed_self,
        query_self,
        key_self,
        value_self,
        self_mixed,
        gains,
        bias,
        buckets_wide,
        grad_gain_feed,
        qk_a,
        qk_b,
        vo_a,
        vo_b,
        cq_a,
        cq_b,
    )

    def encode_grad():
        return call(
            encode_grad_kernel,
            "encodings_grad",
            [smem, deep, deep] + [hbm] * 4,
            like((keys_total, D)),
            [weights(2, D, D), pltpu.SemaphoreType.DMA((2,))],
            14_000_000_000,
            30_000_000,
            orders,
            d_key_cross,
            d_value_cross,
            qk_a,
            qk_b,
            vo_a,
            vo_b,
            grid=(n_dp,),
            out_specs=block,
        )

    def whole(low, high, *columns):
        return jnp.concatenate([low[:, columns[0] : columns[1]], high[:, columns[0] : columns[1]]], axis=1)

    *last_sums, encodings_grad, feed_sum = moves.scatter(
        [
            (0, grads[0:2]),
            (1, grads[2:4]),
            (2, grads[4:6]),
            (0, grad_cross_key),
            (1, grad_cross_value),
        ],
        (None, encode_grad, None, lambda: feed_sum),
    )
    small_sum = last_sums[2][0][:, half:]
    bias_sum = jnp.sum(jnp.where(spot[:, :128], small_sum[:1], 0.0), axis=1)
    return (
        layer_output,
        decoder_grad,
        encodings_grad,
        small_sum[:, 0],
        bias_sum,
        whole(*last_sums[0], 0, half),
        whole(*last_sums[0], half, D),
        whole(*last_sums[1], 0, half),
        whole(*last_sums[1], half, D),
        small_sum[:, 1],
        whole(*last_sums[2], 0, half),
        whole(*last_sums[3], 0, half),
        whole(*last_sums[4], 0, half),
        feed_sum[8],
        small_sum[:, 2],
        jnp.concatenate([feed_sum[t] for t in range(4)], axis=1),
        feed_sum[4:8].reshape(4 * part, D),
    )


def solution(mesh):
    rows = P(both, None)
    flat = P(both)
    in_specs = (rows, rows, flat, P(), flat, flat, rows, rows, rows, rows)
    in_specs += (flat, rows, rows, rows, rows, flat, rows, rows, rows)
    out_specs = (rows, rows, rows, flat, flat, rows, rows, rows, rows)
    out_specs += (flat, rows, rows, rows, rows, flat, rows, rows)
    return jax.shard_map(
        functools.partial(shards, mesh.shape["dp"], mesh.shape["fsdp"]),
        mesh=mesh,
        in_specs=in_specs,
        out_specs=out_specs,
        check_vma=False,
    )
```

```python
import functools
import math

import jax
import jax.numpy as jnp
from jax import lax
from jax.experimental import pallas as pl
from jax.experimental.pallas import tpu as pltpu
from jax.sharding import PartitionSpec as P

D = 768
H = 12
DH = 64
NB = 32
TGT = 32
QPD = 4
GROUPS = 3
TILE = 256
CHUNKS = 16
stage_orders = ("zxy", "zyx", "xyz")

epsilon = 1e-06
masked_score = -1e30
both = ("dp", "fsdp")
bf16 = jnp.bfloat16
f32 = jnp.float32


def matmul(left_side, right_side):
    return jnp.dot(left_side, right_side, preferred_element_type=f32)


def dot_tn(left_side, right_side):
    return lax.dot_general(
        left_side, right_side, (((0,), (0,)), ((), ())), preferred_element_type=f32
    )


def dot_nt(left_side, right_side):
    return lax.dot_general(
        left_side, right_side, (((1,), (1,)), ((), ())), preferred_element_type=f32
    )


def rms_norm(values, gain_vector):
    return (
        values
        * lax.rsqrt(jnp.mean(values * values, axis=-1, keepdims=True) + epsilon)
        * gain_vector
    )


def pieces_of(values):
    high = values.astype(bf16)
    rest = values - high.astype(f32)
    mid = rest.astype(bf16)
    low = (rest - mid.astype(f32)).astype(bf16)
    return high, mid, low


def split_pieces(values):
    high = lax.reduce_precision(values, 8, 7)
    mid = lax.reduce_precision(values - high, 8, 7)
    low = values - high - mid
    return high.astype(bf16), mid.astype(bf16), low.astype(bf16)


def spread_heads(rows):
    tall = jnp.concatenate([rows, rows, rows, rows], axis=0)
    head_row = lax.broadcasted_iota(jnp.int32, (4 * TGT, 4 * DH), 0) // TGT
    head_col = lax.broadcasted_iota(jnp.int32, (4 * TGT, 4 * DH), 1) // DH
    return jnp.where(head_row == head_col, tall, jnp.zeros_like(tall))


def gather_heads(tall):
    head_col = lax.broadcasted_iota(jnp.int32, (TGT, 4 * DH), 1) // DH
    rows = jnp.zeros((TGT, 4 * DH), f32)
    for head in range(4):
        rows = jnp.where(head_col == head, tall[head * TGT : (head + 1) * TGT], rows)
    return rows


def run_tiles(bounds_ref, block, query, slot):
    start = bounds_ref[block, query]
    end = bounds_ref[block, query + 1]
    first = (start // 16) * 16
    count = (end - first + TILE - 1) // TILE
    return start, end, first, count


def tile_rows(first, step, start, end, slot):
    want = first + step * TILE
    base = pl.multiple_of(jnp.minimum(want, slot - TILE), 16)
    rows = base + lax.broadcasted_iota(jnp.int32, (TILE, 4 * TGT), 0)
    inside = (rows >= jnp.maximum(start, want)) & (rows < end)
    return base, inside


def column_of(row):
    return jnp.transpose(jnp.broadcast_to(row, (8, 4 * TGT)))[:, :1]


def mix_kernel(slot, bounds_ref, place_ref, q_ref, k_ref, v_ref, o_ref, score_ref, mix_ref):
    block = pl.program_id(0)
    lane = lax.broadcasted_iota(jnp.int32, (TGT, 128), 1)
    runs = [run_tiles(bounds_ref, block, query, slot) for query in range(QPD)]
    steps = functools.reduce(jnp.maximum, [run[3] for run in runs])
    pairs = [(query, g) for query in range(QPD) for g in range(GROUPS)]
    spread = {
        (query, g): spread_heads(
            q_ref[0, query * TGT : (query + 1) * TGT, g * 256 : (g + 1) * 256]
        )
        for query, g in pairs
    }

    def score_step(step, tops):
        held = pl.ds(pl.multiple_of(step * TILE, TILE), TILE)
        places = [tile_rows(first, step, start, end, slot) for start, end, first, count in runs]
        new_tops = []
        for i, (query, g) in enumerate(pairs):
            base, inside = places[query]
            keys = k_ref[0, pl.ds(base, TILE), g * 256 : (g + 1) * 256]
            scores = jnp.where(inside, dot_nt(keys, spread[query, g]), masked_score)
            score_ref[i, held, :] = scores
            new_tops.append(jnp.maximum(tops[i], jnp.max(scores, axis=0, keepdims=True)))
        return tuple(new_tops)

    tops = lax.fori_loop(
        0, steps, score_step, tuple(jnp.full((1, 4 * TGT), masked_score, f32) for pair in pairs)
    )
    mix_ref[...] = jnp.zeros_like(mix_ref)

    def mix_step(step, sums):
        held = pl.ds(pl.multiple_of(step * TILE, TILE), TILE)
        places = [tile_rows(first, step, start, end, slot) for start, end, first, count in runs]
        new_sums, raised = [], []
        for i in range(len(pairs)):
            weights = jnp.exp(score_ref[i, held, :] - tops[i])
            new_sums.append(sums[i] + jnp.sum(weights, axis=0, keepdims=True))
            raised.append(weights.astype(bf16))
        for i, (query, g) in enumerate(pairs):
            values = v_ref[0, pl.ds(places[query][0], TILE), g * 256 : (g + 1) * 256]
            mix_ref[i] += dot_tn(raised[i], values)
        return tuple(new_sums)

    sums = lax.fori_loop(
        0, steps, mix_step, tuple(jnp.zeros((1, 4 * TGT), f32) for pair in pairs)
    )
    total, top = jnp.concatenate(sums, axis=0), jnp.concatenate(tops, axis=0)
    scales = jnp.transpose(1.0 / total)
    log_sums = jnp.transpose(top + jnp.log(total))
    for query in range(QPD):
        rows_of = slice(query * TGT, (query + 1) * TGT)
        logs = jnp.zeros((TGT, 128), f32)
        for g in range(GROUPS):
            i = query * GROUPS + g
            scale = scales[:, i : i + 1]
            log_sum = log_sums[:, i : i + 1]
            o_ref[0, rows_of, g * 256 : (g + 1) * 256] = gather_heads(mix_ref[i] * scale).astype(
                bf16
            )
            for head in range(4):
                logs = jnp.where(
                    (lane % 16 == g * 4 + head) & (lane < 48),
                    log_sum[head * TGT : (head + 1) * TGT],
                    logs,
                )
        high, mid, low = pieces_of(logs)
        o_ref[0, rows_of, D:] = jnp.where(
            lane < 16, high.astype(f32), jnp.where(lane < 32, mid.astype(f32), low.astype(f32))
        ).astype(bf16)


def grad_kernel(
    slot,
    bounds_ref,
    order_ref,
    q_ref,
    m_ref,
    place_ref,
    k_ref,
    v_ref,
    short_ref,
    long_ref,
    dk_ref,
    dv_ref,
    sum_ref,
):
    block = pl.program_id(0)
    dk_ref[...] = jnp.zeros_like(dk_ref)
    dv_ref[...] = jnp.zeros_like(dv_ref)
    sum_ref[...] = jnp.zeros_like(sum_ref)
    runs = [run_tiles(bounds_ref, block, query, slot) for query in range(QPD)]
    steps = functools.reduce(jnp.maximum, [run[3] for run in runs])
    pairs = [(query, g) for query in range(QPD) for g in range(GROUPS)]
    row = lax.broadcasted_iota(jnp.int32, (TGT, 2 * H * TGT), 0)
    target = lax.broadcasted_iota(jnp.int32, (TGT, 2 * H * TGT), 1) % TGT
    spread, spread_m, logs, deltas = {}, {}, {}, {}
    for query in range(QPD):
        rows_of = slice(query * TGT, (query + 1) * TGT)
        placed = matmul(m_ref[0, rows_of, D : D + 128], place_ref[...])
        flat = jnp.sum(jnp.where(row == target, placed, 0.0), axis=0, keepdims=True)
        for g in range(GROUPS):
            columns = slice(g * 256, (g + 1) * 256)
            spread[query, g] = spread_heads(q_ref[0, rows_of, columns])
            spread_m[query, g] = spread_heads(m_ref[0, rows_of, columns])
            logs[query, g] = flat[:, g * 128 : (g + 1) * 128]
            deltas[query, g] = flat[:, (GROUPS + g) * 128 : (GROUPS + g + 1) * 128]

    def step_of(step, carry):
        places = [tile_rows(first, step, start, end, slot) for start, end, first, count in runs]
        softs, changes = [], []
        for query, g in pairs:
            base, inside = places[query]
            columns = slice(g * 256, (g + 1) * 256)
            scores = dot_nt(k_ref[0, pl.ds(base, TILE), columns], spread[query, g])
            soft = jnp.where(inside, jnp.exp(scores - logs[query, g]), 0.0)
            d_soft = dot_nt(v_ref[0, pl.ds(base, TILE), columns], spread_m[query, g])
            changes.append((soft * (d_soft - deltas[query, g])).astype(bf16))
            softs.append(soft.astype(bf16))
        for i, (query, g) in enumerate(pairs):
            keys = k_ref[0, pl.ds(places[query][0], TILE), g * 256 : (g + 1) * 256]
            sum_ref[i] += dot_tn(changes[i], keys)
        for i, (query, g) in enumerate(pairs):
            rows_of, columns = pl.ds(places[query][0], TILE), slice(g * 256, (g + 1) * 256)
            dk_ref[0, rows_of, columns] += matmul(changes[i], spread[query, g]).astype(bf16)
            dv_ref[0, rows_of, columns] += matmul(softs[i], spread_m[query, g]).astype(bf16)
        return carry

    lax.fori_loop(0, steps, step_of, 0)
    for query in range(QPD):
        rows_of = slice(query * TGT, (query + 1) * TGT)
        d_query = jnp.concatenate(
            [gather_heads(sum_ref[query * GROUPS + g]) for g in range(GROUPS)], axis=1
        )
        short_ref[0, rows_of, :] = d_query[:, : D // 3].astype(bf16)
        long_ref[0, rows_of, :] = d_query[:, D // 3 :].astype(bf16)


def cross_mix(bounds, arrival, queries, keys, values):
    blocks, slot = keys.shape[0], keys.shape[1]
    rows = queries.shape[1]
    at = lambda i, *refs: (i, 0, 0)
    come = lambda i, bounds_ref, order_ref: (order_ref[i], 0, 0)
    return pl.pallas_call(
        functools.partial(mix_kernel, slot),
        grid_spec=pltpu.PrefetchScalarGridSpec(
            num_scalar_prefetch=2,
            grid=(blocks,),
            in_specs=[
                pl.BlockSpec((1, rows, D), come),
                pl.BlockSpec((1, slot, D), at),
                pl.BlockSpec((1, slot, D), at),
            ],
            out_specs=[pl.BlockSpec((1, rows, D + 128), at)],
            scratch_shapes=[
                pltpu.VMEM((QPD * GROUPS, slot + TILE, 4 * TGT), f32),
                pltpu.VMEM((QPD * GROUPS, 4 * TGT, 256), f32),
            ],
        ),
        out_shape=[
            jax.ShapeDtypeStruct((blocks, rows, D + 128), bf16),
        ],
        compiler_params=pltpu.CompilerParams(vmem_limit_bytes=60 * 1024 * 1024),
        cost_estimate=pl.CostEstimate(
            flops=12_000_000_000, bytes_accessed=22_000_000, transcendentals=4_000_000
        ),
        name="cross_mix",
    )(bounds, arrival, queries, keys, values)[0]


def cross_grad(bounds, arrival, queries, mixed, place, keys, values):
    blocks, slot = keys.shape[0], keys.shape[1]
    rows = queries.shape[1]
    at = lambda i, *refs: (i, 0, 0)
    come = lambda i, bounds_ref, order_ref: (order_ref[i], 0, 0)
    return pl.pallas_call(
        functools.partial(grad_kernel, slot),
        grid_spec=pltpu.PrefetchScalarGridSpec(
            num_scalar_prefetch=2,
            grid=(blocks,),
            in_specs=[
                pl.BlockSpec((1, rows, D), come),
                pl.BlockSpec((1, rows, D + 128), come),
                pl.BlockSpec((128, 2 * H * TGT), lambda i, *refs: (0, 0)),
                pl.BlockSpec((1, slot, D), at),
                pl.BlockSpec((1, slot, D), at),
            ],
            out_specs=[
                pl.BlockSpec((1, rows, D // 3), come),
                pl.BlockSpec((1, rows, D - D // 3), come),
                pl.BlockSpec((1, slot, D), at),
                pl.BlockSpec((1, slot, D), at),
            ],
            scratch_shapes=[pltpu.VMEM((QPD * GROUPS, 4 * TGT, 256), f32)],
        ),
        out_shape=[
            jax.ShapeDtypeStruct((blocks, rows, D // 3), bf16),
            jax.ShapeDtypeStruct((blocks, rows, D - D // 3), bf16),
            jax.ShapeDtypeStruct((blocks, slot, D), bf16),
            jax.ShapeDtypeStruct((blocks, slot, D), bf16),
        ],
        compiler_params=pltpu.CompilerParams(vmem_limit_bytes=60 * 1024 * 1024),
        cost_estimate=pl.CostEstimate(
            flops=24_000_000_000, bytes_accessed=42_000_000, transcendentals=4_000_000
        ),
        name="cross_grad",
    )(bounds, arrival, queries, mixed, place, keys, values)


def flag_of(orders_ref):
    return orders_ref[6 * CHUNKS]


def start_load(orders_ref, mine, other, stage, sem):
    flag = flag_of(orders_ref)
    for core, sources in ((flag, mine), (1 - flag, other)):
        place = 0
        for source in sources:
            count = source.shape[0]
            pltpu.make_async_copy(source, stage.at[core, pl.ds(place, count)], sem).start()
            place += count


def wait_load(into, sem):
    pltpu.make_async_copy(into, into, sem).wait()


def assemble(orders_ref, order, stage, columns, into):
    if stage.shape[1] == 1:
        into[...] = stage[0, 0, :, columns]
        return
    rows = 2 * stage.shape[2]
    for i in range(stage.shape[1]):
        base = pl.multiple_of(orders_ref[order * CHUNKS + i] * rows, 16)
        into[pl.ds(base, rows), :] = jnp.concatenate(
            [stage[0, i, :, columns], stage[1, i, :, columns]], axis=0
        )


def store_grad(orders_ref, order, grad, mine_ref, other_ref, columns):
    chunks, rows = mine_ref.shape[0], mine_ref.shape[1]
    if chunks == 1:
        mine_ref[0, :, columns] = grad[...].astype(bf16)
        return
    first = flag_of(orders_ref) == 0
    for i in range(chunks):
        to = orders_ref[(3 + order) * CHUNKS + i]
        low = grad[2 * i * rows : (2 * i + 1) * rows, :]
        high = grad[(2 * i + 1) * rows : (2 * i + 2) * rows, :]
        mine_ref[to, :, columns] = jnp.where(first, low, high).astype(bf16)
        other_ref[to, :, columns] = jnp.where(first, high, low).astype(bf16)


def iota(shape, axis):
    return lax.broadcasted_iota(jnp.int32, shape, axis)


def project_kernel(enc_ref, w_ref, out_ref):
    out_ref[...] = matmul(enc_ref[...], w_ref[0]).astype(bf16)


def encode_grad_kernel(dk_ref, dv_ref, wk_ref, wv_ref, *refs):
    out_ref = refs[-1]
    out_ref[...] = (dot_nt(dk_ref[...], wk_ref[0]) + dot_nt(dv_ref[...], wv_ref[0])).astype(bf16)


def weight_grad_kernel(steps, orders_ref, enc_ref, dk_ref, dv_ref, mine_ref, other_ref, sum_ref):
    step = pl.program_id(0)
    rows = enc_ref[...]
    products = [dot_tn(rows, dk_ref[...]), dot_tn(rows, dv_ref[...])]

    @pl.when(step == 0)
    def first():
        for i in range(2):
            sum_ref[i] = products[i]

    @pl.when(step > 0)
    def later():
        for i in range(2):
            sum_ref[i] += products[i]

    @pl.when(step == steps - 1)
    def store():
        for i in range(2):
            columns = slice(i * D, (i + 1) * D)
            store_grad(orders_ref, i, sum_ref.at[i], mine_ref, other_ref, columns)


def self_kernel(counts, orders_ref, states_ref, buckets_ref, *refs):
    refs = list(refs)
    pieces = []
    for mine, other in counts:
        pieces.append((refs[:mine], refs[mine : mine + other]))
        refs = refs[mine + other :]
    normed_ref, q_ref, k_ref, v_ref, mixed_ref, first_ref, normed_cross_ref = refs[:7]
    q_cross_ref, gains_ref, bias_ref, out_ref, w_ref, small_ref = refs[7:13]
    stages, sems, out_sems = refs[13:16], refs[16], refs[17]
    for order in (2, 0, 1):
        start_load(orders_ref, *pieces[order], stages[order], sems.at[order])

    def put(weight, order, place):
        assemble(
            orders_ref, order, stages[order], slice(place * D, (place + 1) * D), w_ref.at[weight]
        )
        pltpu.make_async_copy(w_ref.at[weight], out_ref.at[weight], out_sems.at[weight]).start()

    wait_load(stages[2], sems.at[2])
    assemble(orders_ref, 2, stages[2], slice(D, D + 128), small_ref)
    small = small_ref[...]
    gains_ref[...] = jnp.transpose(small.astype(f32))[:8]
    span = D // NB
    first_row, row = span * iota((NB, D), 0), iota((NB, D), 1)
    pick = ((row >= first_row) & (row < first_row + span)).astype(f32).astype(bf16)
    table = matmul(pick, small).astype(bf16)
    wide = (iota((128, H * TGT), 0) == 16 + (iota((128, H * TGT), 1) >> 5)).astype(f32).astype(bf16)
    table = matmul(table, wide)
    buckets = buckets_ref[...]
    later = iota((TGT, 128), 0) > (iota((TGT, 128), 1) & (TGT - 1))
    for g in range(GROUPS):
        bias = jnp.zeros((TGT, 128), f32)
        for n in range(NB):
            bias = jnp.where(buckets == n, table[n : n + 1, g * 128 : (g + 1) * 128], bias)
        bias_ref[:, g * 128 : (g + 1) * 128] = jnp.where(later, masked_score, bias)

    states = states_ref[...].astype(f32)
    normed = rms_norm(states, gains_ref[0:1]).astype(bf16)
    normed_ref[...] = normed
    wait_load(stages[0], sems.at[0])
    put(0, 0, 0)
    q_ref[...] = matmul(normed, w_ref[0]).astype(bf16)
    put(1, 0, 1)
    k_ref[...] = matmul(normed, w_ref[1]).astype(bf16)
    wait_load(stages[1], sems.at[1])
    put(2, 1, 0)
    v_ref[...] = matmul(normed, w_ref[2]).astype(bf16)
    for query in range(QPD):
        rows_of = slice(query * TGT, (query + 1) * TGT)
        for g in range(GROUPS):
            columns = slice(g * 256, (g + 1) * 256)
            spread = spread_heads(q_ref[rows_of, columns])
            scores = dot_nt(k_ref[rows_of, columns], spread) + bias_ref[:, g * 128 : (g + 1) * 128]
            raised = jnp.exp(scores - jnp.max(scores, axis=0, keepdims=True))
            soft = raised / jnp.sum(raised, axis=0, keepdims=True)
            tall = dot_tn(soft.astype(bf16), v_ref[rows_of, columns])
            mixed_ref[rows_of, columns] = gather_heads(tall).astype(bf16)
    put(3, 1, 1)
    first = states + matmul(mixed_ref[...], w_ref[3])
    first_ref[...] = first
    normed_cross = rms_norm(first, gains_ref[1:2]).astype(bf16)
    normed_cross_ref[...] = normed_cross
    put(4, 2, 0)
    q_cross_ref[...] = matmul(normed_cross, w_ref[4]).astype(bf16)
    put(5, 0, 2)
    put(6, 1, 2)
    for weight in range(7):
        pltpu.make_async_copy(w_ref.at[weight], out_ref.at[weight], out_sems.at[weight]).wait()


def exact_sum(values, picks):
    high, mid, low = pieces_of(values)
    return matmul(high, picks) + matmul(mid, picks) + matmul(low, picks)


def norm_back(values, gain, d_normed):
    scale = lax.rsqrt(jnp.mean(values * values, axis=-1, keepdims=True) + epsilon)
    scaled = d_normed * gain
    inner = jnp.mean(scaled * values, axis=-1, keepdims=True)
    d_values = scale * scaled - values * (scale * scale * scale * inner)
    d_gain = jnp.sum(d_normed * values * scale, axis=0, keepdims=True)
    return d_values, d_gain


def feed_kernel(
    back_ref,
    first_ref,
    cot_ref,
    gains_ref,
    fi_ref,
    fo_ref,
    co_ref,
    out_ref,
    send_ref,
    second_ref,
    branch_ref,
    mixed_ref,
    normed_ref,
    hidden_ref,
    pre_ref,
    gain_ref,
    wc_ref,
    wi_ref,
    wo_ref,
    logs_ref,
    sems,
):
    blocks, rows = back_ref.shape[0], back_ref.shape[1]
    copies = [
        pltpu.make_async_copy(source, into, sems.at[i])
        for i, (source, into) in enumerate(((co_ref, wc_ref), (fi_ref, wi_ref), (fo_ref, wo_ref)))
    ]
    for copy in copies:
        copy.start()
    widen = ((iota((128, D), 0) & 15) == (iota((128, D), 1) >> 6)) & (iota((128, D), 0) < 48)
    widen = widen.astype(f32).astype(bf16)

    def log_step(i, top):
        logs = matmul(back_ref[i, :, D:], widen)
        logs_ref[i] = logs
        return jnp.maximum(top, logs)

    top = lax.fori_loop(0, blocks, log_step, jnp.full((rows, D), masked_score, f32))

    def share_step(i, carry):
        total, mixed = carry
        share = jnp.exp(logs_ref[i] - top)
        return total + share, mixed + share * back_ref[i, :, :D].astype(f32)

    zero = jnp.zeros((rows, D), f32)
    total, mixed = lax.fori_loop(0, blocks, share_step, (zero, zero))
    mixed = mixed / total
    logs = top + jnp.log(total)
    mixed_ref[...] = mixed.astype(bf16)
    copies[0].wait()
    second = first_ref[...] + matmul(mixed_ref[...], wc_ref[...])
    normed = rms_norm(second, gains_ref[2:3]).astype(bf16)
    normed_ref[...] = normed
    copies[1].wait()
    copies[2].wait()
    cot = cot_ref[...]
    root = 0.7978845608028654

    def feed_step(t, carry):
        out, d_normed = carry
        pre = matmul(normed, wi_ref[t])
        w_out = wo_ref[pl.ds(pl.multiple_of(t * D, D), D), :]
        bent = jnp.tanh(root * (pre + 0.044715 * pre * pre * pre))
        hidden = (0.5 * pre * (1.0 + bent)).astype(bf16)
        slope = 0.5 * (1.0 + bent) + 0.5 * pre * (1.0 - bent * bent) * (
            root * (1.0 + 3 * 0.044715 * pre * pre)
        )
        d_pre = (dot_nt(cot, w_out) * slope).astype(bf16)
        hidden_ref[t] = hidden
        pre_ref[t] = d_pre
        return out + matmul(hidden, w_out), d_normed + dot_nt(d_pre, wi_ref[t])

    out, d_normed = lax.fori_loop(0, 4, feed_step, (zero, zero))
    out_ref[...] = (second + out).astype(bf16)
    d_values, gain_ref[...] = norm_back(second, gains_ref[2:3], d_normed)
    d_second = cot.astype(f32) + d_values
    second_ref[...] = d_second
    branch_ref[...] = d_second.astype(bf16)
    d_mixed = dot_nt(branch_ref[...], wc_ref[...]).astype(bf16)
    send_ref[:, :D] = d_mixed
    lane = iota((D, 128), 1)
    row = iota((D, 128), 0)
    pick = ((row == (lane & 15) * DH) & (lane < 48)).astype(f32).astype(bf16)
    add = (((row >> 6) == (lane & 15)) & (lane >= 48) & (lane < 96)).astype(f32).astype(bf16)
    extra = exact_sum(logs, pick) + exact_sum(d_mixed.astype(f32) * mixed, add)
    high, mid, low = pieces_of(extra)
    slot_of = iota((rows, 128), 1) >> 4
    slot_of = jnp.where(slot_of >= 3, slot_of - 3, slot_of)
    send_ref[:, D:] = jnp.where(
        slot_of == 0, high.astype(f32), jnp.where(slot_of == 1, mid.astype(f32), low.astype(f32))
    ).astype(bf16)


def feed_grad_kernel(hidden_ref, pre_ref, normed_ref, mixed_ref, branch_ref, cot_ref, out_ref):
    blocks, slabs, part, width = out_ref.shape

    def put(grad, block, slab, row):
        out_ref[block, slab] = grad[row : row + part].astype(bf16)

    for t in range(4):
        grad = dot_tn(normed_ref[...], pre_ref[t])
        for i in range(blocks):
            put(grad, i, t, i * part)
        grad = dot_tn(hidden_ref[t], cot_ref[...])
        for i in range(blocks):
            place = t * blocks + i
            put(grad, place // 4, 4 + place % 4, i * part)
    grad = dot_tn(mixed_ref[...], branch_ref[...])
    for i in range(blocks):
        put(grad, i, 8, i * part)


def self_grad_kernel(
    orders_ref,
    back_ref,
    second_ref,
    first_ref,
    states_ref,
    normed_cross_ref,
    normed_ref,
    q_ref,
    k_ref,
    v_ref,
    mixed_ref,
    gains_ref,
    bias_ref,
    buckets_ref,
    gain_feed_ref,
    *refs,
):
    weights_ref, out_ref, ga_ref, ha_ref, gc_ref, hc_ref = refs[:6]
    w_ref, dq_ref, dk_ref, dv_ref, dm_ref, sums_ref, sems = refs[6:]
    for i in (4, 3, 0, 1, 2):
        pltpu.make_async_copy(weights_ref.at[i], w_ref.at[i], sems.at[i]).start()

    d_query = back_ref[...].astype(bf16)
    store_grad(orders_ref, 2, dot_tn(normed_cross_ref[...], d_query), gc_ref, hc_ref, slice(0, D))
    wait_load(w_ref.at[4], sems.at[4])
    d_values, gain_cross = norm_back(first_ref[...], gains_ref[1:2], dot_nt(d_query, w_ref[4]))
    d_first = second_ref[...] + d_values
    branch = d_first.astype(bf16)
    store_grad(orders_ref, 1, dot_tn(mixed_ref[...], branch), ga_ref, ha_ref, slice(3 * D, 4 * D))
    wait_load(w_ref.at[3], sems.at[3])
    dm_ref[...] = dot_nt(branch, w_ref[3]).astype(bf16)
    sums_ref[...] = jnp.zeros_like(sums_ref)
    for query in range(QPD):
        rows_of = slice(query * TGT, (query + 1) * TGT)
        for g in range(GROUPS):
            columns = slice(g * 256, (g + 1) * 256)
            lanes = slice(g * 128, (g + 1) * 128)
            spread = spread_heads(q_ref[rows_of, columns])
            spread_m = spread_heads(dm_ref[rows_of, columns])
            keys = k_ref[rows_of, columns]
            scores = dot_nt(keys, spread) + bias_ref[:, lanes]
            raised = jnp.exp(scores - jnp.max(scores, axis=0, keepdims=True))
            soft = raised / jnp.sum(raised, axis=0, keepdims=True)
            d_soft = dot_nt(v_ref[rows_of, columns], spread_m)
            delta = jnp.sum(soft * d_soft, axis=0, keepdims=True)
            d_scores = (soft * (d_soft - delta)).astype(bf16)
            sums_ref[:, lanes] += d_scores.astype(f32)
            dq_ref[rows_of, columns] = gather_heads(dot_tn(d_scores, keys)).astype(bf16)
            dk_ref[rows_of, columns] = matmul(d_scores, spread).astype(bf16)
            dv_ref[rows_of, columns] = matmul(soft.astype(bf16), spread_m).astype(bf16)
    normed = normed_ref[...]
    store_grad(orders_ref, 0, dot_tn(normed, dq_ref[...]), ga_ref, ha_ref, slice(0, D))
    store_grad(orders_ref, 0, dot_tn(normed, dk_ref[...]), ga_ref, ha_ref, slice(D, 2 * D))
    store_grad(orders_ref, 1, dot_tn(normed, dv_ref[...]), ga_ref, ha_ref, slice(2 * D, 3 * D))
    wait_load(w_ref.at[0], sems.at[0])
    wait_load(w_ref.at[1], sems.at[1])
    wait_load(w_ref.at[2], sems.at[2])
    d_normed = (
        dot_nt(dq_ref[...], w_ref[0]) + dot_nt(dk_ref[...], w_ref[1]) + dot_nt(dv_ref[...], w_ref[2])
    )
    d_values, gain_self = norm_back(states_ref[...].astype(f32), gains_ref[0:1], d_normed)
    out_ref[...] = (d_first + d_values).astype(bf16)
    buckets = buckets_ref[...]
    by_bucket = []
    for n in range(NB):
        sums = []
        for g in range(GROUPS):
            mine = jnp.where(buckets == n, sums_ref[:, g * 128 : (g + 1) * 128], 0.0)
            sums.append(jnp.sum(mine, axis=0, keepdims=True))
        by_bucket.append(jnp.concatenate(sums, axis=1))
    by_bucket = jnp.concatenate(by_bucket, axis=0)
    lane = iota((H * TGT, 128), 1)
    narrow = ((iota((H * TGT, 128), 0) >> 5) == lane - 16).astype(f32).astype(bf16)
    table = exact_sum(by_bucket, narrow).astype(bf16)
    span = D // NB
    first_row, row = span * iota((D, NB), 1), iota((D, NB), 0)
    put = ((row >= first_row) & (row < first_row + span)).astype(f32).astype(bf16)
    gains = jnp.concatenate([gain_self, gain_cross, gain_feed_ref[...], jnp.zeros((125, D), f32)])
    small = matmul(put, table) + jnp.transpose(gains)
    store_grad(orders_ref, 2, small, gc_ref, hc_ref, slice(D, D + 128))


hbm = pl.BlockSpec(memory_space=pl.ANY)
vmem = pl.BlockSpec(memory_space=pltpu.VMEM)
smem = pl.BlockSpec(memory_space=pltpu.SMEM)


def like(shape, kind=bf16):
    return jax.ShapeDtypeStruct(shape, kind)


def call(kernel, name, ins, outs, scratch, flops, moved, *values, **more):
    return pl.pallas_call(
        kernel,
        in_specs=ins,
        out_shape=outs,
        scratch_shapes=scratch,
        compiler_params=pltpu.CompilerParams(vmem_limit_bytes=60 * 1024 * 1024),
        cost_estimate=pl.CostEstimate(flops=flops, bytes_accessed=moved, transcendentals=0),
        name=name,
        **more,
    )(*values)


def weights(*shape):
    return pltpu.VMEM(shape, bf16)


class Wires:
    def __init__(self, n_dp, n_fsdp):
        self.n_dp, self.n_fsdp = n_dp, n_fsdp
        self.sizes = {"x": n_fsdp // 2, "y": n_fsdp // 2, "z": n_dp // (n_fsdp // 2), "c": 2}
        dp, fsdp = lax.axis_index("dp"), lax.axis_index("fsdp")
        size = self.sizes
        self.at = {"z": dp // size["x"], "x": dp % size["x"], "y": fsdp // 2, "c": fsdp % 2}

    def shift(self, value, axis, steps=1):
        size = self.sizes
        pairs = []
        for dp in range(self.n_dp):
            for fsdp in range(self.n_fsdp):
                at = {"z": dp // size["x"], "x": dp % size["x"], "y": fsdp // 2, "c": fsdp % 2}
                here = dp * self.n_fsdp + fsdp
                at[axis] = (at[axis] + steps) % size[axis]
                there = (at["z"] * size["x"] + at["x"]) * self.n_fsdp + at["y"] * 2 + at["c"]
                pairs.append((here, there))
        return lax.ppermute(value, both, pairs)

    def begin(self, walks):
        return [[self.shift(*ask) for ask in walk.asks] for walk in walks if not walk.over]

    def finish(self, walks, got, *tied):
        got, tied = lax.optimization_barrier((got, tied))
        for walk, values in zip([walk for walk in walks if not walk.over], got):
            walk.take(values)
        return tied

    def together(self, walks, steps=100):
        for step in range(steps):
            if all(walk.over for walk in walks):
                break
            self.finish(walks, self.begin(walks))
        return [walk.result for walk in walks]

    def around_asks(self, value, axis):
        return [(value, axis, steps) for steps in range(1, self.sizes[axis])]

    def gather_dp_walk(self, value, order):
        for axis in order:
            value = jnp.stack([value] + (yield self.around_asks(value, axis)))
        return value if order == "xz" else value.swapaxes(0, 1)

    def gather_dp(self, value):
        cut = value.shape[1] // 3 // 128 * 128
        walks = [
            Walk(self.gather_dp_walk(value[:, cut:], "zx")),
            Walk(self.gather_dp_walk(value[:, :cut], "xz")),
        ]

        def join():
            long, short = (walk.result for walk in walks)
            return jnp.concatenate([short, long], axis=3).reshape((-1,) + value.shape)

        return walks, join

    def scatter_dp(self, short, long):
        size = self.sizes
        parts = [value.reshape((size["z"], size["x"]) + value.shape[1:]) for value in (short, long)]

        def walk(value, first, second):
            held = yield from self.sum_walk(value, first, bf16)
            return (yield from self.sum_walk(held, second, f32))

        return [Walk(walk(parts[0], "z", "x")), Walk(walk(parts[1].swapaxes(0, 1), "x", "z"))]

    def arrival(self):
        size = self.sizes
        dp = jnp.arange(self.n_dp, dtype=jnp.int32)
        z_back = (self.at["z"] - dp // size["x"]) % size["z"]
        x_back = (self.at["x"] - dp % size["x"]) % size["x"]
        return z_back * size["x"] + x_back

    def orders(self):
        size = self.sizes
        chunk = jnp.arange(CHUNKS, dtype=jnp.int32)
        y, x, z = chunk % size["y"], chunk // size["y"] % size["x"], chunk // size["y"] // size["x"]
        places = []
        for order in stage_orders:
            place = jnp.zeros_like(chunk)
            for axis in reversed(order):
                value = {"x": x, "y": y, "z": z}[axis]
                place = place * size[axis] + (self.at[axis] - value) % size[axis]
            places.append(place)
        chunks = [jnp.sum(jnp.where(p[:, None] == chunk[None, :], chunk[:, None], 0), 0) for p in places]
        flat = jnp.concatenate(chunks + places + [self.at["c"][None]])
        return jnp.pad(flat, (0, 128 - flat.shape[0])).astype(jnp.int32)

    def gather_walk(self, block, order):
        held = block[None]
        for axis in order[:2]:
            held = jnp.concatenate([held] + (yield self.around_asks(held, axis)), axis=0)
        *found, first = yield self.around_asks(held, order[2]) + [(held, "c")]
        others = yield [(value, "c") for value in found]
        return [held] + found, [first] + others

    def beside(self, *steps):
        walks = [Walk(step) for step in steps]
        while not all(walk.over for walk in walks):
            live = [walk for walk in walks if not walk.over]
            asks = [ask for walk in live for ask in walk.asks]
            got = yield asks
            for walk in live:
                count = len(walk.asks)
                walk.take(got[:count])
                got = got[count:]
        return [walk.result for walk in walks]

    def gather_pair_walk(self, block, cut):
        held = block[None]
        held = jnp.concatenate([held] + (yield self.around_asks(held, "z")), axis=0)

        def rest(held, first, second):
            held = jnp.concatenate([held] + (yield self.around_asks(held, first)), axis=0)
            *found, own = yield self.around_asks(held, second) + [(held, "c")]
            others = yield [(value, "c") for value in found]
            return [held] + found, [own] + others

        return (
            yield from self.beside(
                rest(held[:, :, :cut], "x", "y"), rest(held[:, :, cut:], "y", "x")
            )
        )

    def sum_walk(self, value, axis, kind):
        n = value.shape[0]
        got = yield [(value[steps], axis, n - steps) for steps in range(1, n)]
        return sum((one.astype(f32) for one in got), value[0].astype(f32)).astype(kind)

    def scatter_walk(self, mine, other, order):
        (got,) = yield [(other, "c")]
        held = plus(mine, got)
        for stage, axis in enumerate(reversed(order)):
            value = held.reshape((self.sizes[axis], -1) + held.shape[1:])
            held = yield from self.sum_walk(value, axis, f32 if stage == 2 else bf16)
        return held[0]

    def scatter_pair_walk(self, mine, other, cut):
        (got,) = yield [(other, "c")]

        def first(held, one, two):
            for axis in (one, two):
                value = held.reshape((self.sizes[axis], -1) + held.shape[1:])
                held = yield from self.sum_walk(value, axis, bf16)
            return held

        parts = yield from self.beside(
            first(plus(mine[:, :, :cut], got[:, :, :cut]), "y", "x"),
            first(plus(mine[:, :, cut:], got[:, :, cut:]), "x", "y"),
        )
        held = yield from self.sum_walk(jnp.concatenate(parts, axis=2)[:, None], "z", f32)
        return held[0]


class Walk:
    def __init__(self, steps):
        self.steps, self.over, self.result = steps, False, None
        self.asks = next(steps)

    def tie(self, value):
        value, held = lax.optimization_barrier((value, [ask[0] for ask in self.asks]))
        self.asks = [(new, *ask[1:]) for new, ask in zip(held, self.asks)]
        return value

    def take(self, got):
        try:
            self.asks = self.steps.send(got)
        except StopIteration as end:
            self.over, self.result = True, end.value


def plus(one, two, kind=bf16):
    return (one.astype(f32) + two.astype(f32)).astype(kind)


def join_columns(one, two):
    return jnp.concatenate(lax.optimization_barrier((one, two)), axis=1)


def gather_plain(packs):
    return [([lax.all_gather(pack, both, axis=0, tiled=True)[None]], []) for pack in packs]


def scatter_plain(parts):
    whole = jnp.concatenate([part[0] for part in parts], axis=1)
    whole = lax.psum_scatter(whole, both, scatter_dimension=0, tiled=True).astype(f32)
    ends = [0]
    for part in parts:
        ends.append(ends[-1] + part.shape[2])
    return [whole[:, low:high] for low, high in zip(ends[:-1], ends[1:])]


def shards(
    n_dp,
    n_fsdp,
    decoder_states,
    encodings,
    owner_query,
    buckets,
    gain_self,
    bias_table,
    self_query,
    self_key,
    self_value,
    self_output,
    gain_cross,
    cross_query,
    cross_key,
    cross_value,
    cross_output,
    gain_feed,
    feed_in,
    feed_out,
    cotangent,
):
    n_dev = n_dp * n_fsdp
    wires = Wires(n_dp, n_fsdp)
    chunked = n_dev // 2 == CHUNKS and D % (8 * n_dev) == 0
    chunks = CHUNKS if chunked else 1
    rows = decoder_states.shape[0]
    keys_total = encodings.shape[0]
    slot = keys_total // n_dp
    part = D // n_dev
    bias_part = bias_table.shape[0]
    half = D // 2

    device = lax.axis_index("dp") * n_fsdp + lax.axis_index("fsdp")
    lane = jnp.arange(128, dtype=jnp.int32)
    entry = device * bias_part + jnp.arange(bias_part, dtype=jnp.int32)
    spot = (16 + entry % H)[:, None] == lane[None, :]
    small = jnp.sum(jnp.where(spot, bias_table[:, None].astype(f32), 0.0), axis=0)
    small = jnp.where(jnp.arange(part)[:, None] == 0, small[None, :], 0.0)
    for i, gain in enumerate((gain_self, gain_cross, gain_feed)):
        small = jnp.where(lane[None, :] == i, gain[:, None].astype(f32), small)
    small = small.astype(bf16)

    packs = [
        jnp.concatenate(values, axis=1)
        for values in (
            (self_query, self_key, cross_key),
            (self_value, self_output, cross_value),
            (cross_query, small),
        )
    ]

    def runs(owner_query, buckets):
        owners = owner_query.reshape(n_dp, slot)
        ids = (jnp.arange(n_dp, dtype=jnp.int32) * n_fsdp + lax.axis_index("fsdp")) * QPD
        before = owners[:, None, :] < (ids[:, None] + jnp.arange(QPD + 1, dtype=jnp.int32))[:, :, None]
        bounds = jnp.sum(before.astype(jnp.int32), axis=2)
        return bounds, wires.arrival(), jnp.tile(buckets.T, (1, 4)), orders_of()

    def orders_of():
        return wires.orders() if chunked else jnp.zeros((128,), jnp.int32)

    if chunked:
        walks = [
            Walk(wires.gather_pair_walk(join_columns(*packs[:2]), 3 * D)),
            Walk(wires.gather_walk(packs[2], "xyz")),
        ]
        owner_query, buckets = wires.finish(walks, wires.begin(walks), owner_query, buckets)
        got = wires.begin(walks)
        (places, feed_in, feed_out, cross_output) = wires.finish(
            walks, got, runs(owner_query, buckets), feed_in, feed_out, cross_output
        )
        bounds, arrival, buckets_wide, orders = places
        pair, third = wires.together(walks)
        first_weights = [*pair, third]
    else:
        first_weights = gather_plain(packs)
        bounds, arrival, buckets_wide, orders = runs(owner_query, buckets)
    feed_pack = jnp.concatenate(
        [feed_in[:, t * D : (t + 1) * D] for t in range(4)] + [feed_out, cross_output], axis=0
    )
    feed_pack = lax.all_gather(feed_pack, both, axis=0)
    w_feed_in = feed_pack[:, : 4 * part].reshape(n_dev, 4, part, D).transpose(1, 0, 2, 3)
    w_feed_in = w_feed_in.reshape(4, D, D)
    w_feed_out = feed_pack[:, 4 * part : 8 * part].reshape(4 * D, D)
    w_cross_output = feed_pack[:, 8 * part :].reshape(D, D)

    counts = [(len(mine), len(other)) for mine, other in first_weights]
    pieces = [piece for weight in first_weights for side in weight for piece in side]
    first_widths = [3 * D, 3 * D, D + 128]
    wide = (rows, D)
    (
        normed_self,
        query_self,
        key_self,
        value_self,
        self_mixed,
        first_residual,
        normed_cross,
        query_cross,
        gains,
        bias,
        w_first,
    ) = call(
        functools.partial(self_kernel, counts),
        "self_forward",
        [smem, vmem, vmem] + [hbm] * len(pieces),
        [like(wide)] * 5
        + [like(wide, f32), like(wide), like(wide), like((8, D), f32), like((TGT, H * TGT), f32)]
        + [like((7, D, D))],
        [weights(7, D, D), weights(D, 128)]
        + [weights(min(chunks, 2), chunks, D // (2 * chunks) if chunked else D, w) for w in first_widths]
        + [pltpu.SemaphoreType.DMA((3,)), pltpu.SemaphoreType.DMA((7,))],
        1_500_000_000,
        9_000_000,
        orders,
        decoder_states,
        buckets_wide,
        *pieces,
        out_specs=[vmem] * 10 + [hbm],
    )

    tall = math.gcd(keys_total, 1536)
    steps = keys_total // tall
    block = pl.BlockSpec((tall, D), lambda i: (i, 0))

    def weight_at(i):
        return pl.BlockSpec((1, D, D), lambda step: (i, 0, 0))

    def project(i):
        return call(
            project_kernel,
            "cross_project",
            [block, weight_at(i)],
            like((keys_total, D)),
            [],
            7_300_000_000,
            20_000_000,
            encodings,
            w_first,
            grid=(steps,),
            out_specs=block,
        ).reshape(n_dp, slot, D)

    walks, join = wires.gather_dp(query_cross)
    (key_cross,) = wires.finish(walks, wires.begin(walks), project(5))
    (value_cross,) = wires.finish(walks, wires.begin(walks), project(6))
    all_queries = join()
    parts = cross_mix(bounds, arrival, all_queries, key_cross, value_cross)
    back = lax.all_to_all(parts, "dp", split_axis=0, concat_axis=0)

    (
        layer_output,
        d_send,
        d_second,
        d_branch,
        cross_mixed,
        normed_feed,
        hidden,
        d_pre,
        grad_gain_feed,
    ) = call(
        feed_kernel,
        "feed_both_ways",
        [vmem] * 4 + [hbm] * 3,
        [
            like(wide),
            like((rows, D + 128)),
            like(wide, f32),
            like(wide),
            like(wide),
            like(wide),
            like((4, rows, D)),
            like((4, rows, D)),
            like((1, D), f32),
        ],
        [
            weights(D, D),
            weights(4, D, D),
            weights(4 * D, D),
            pltpu.VMEM((n_dp, rows, D), f32),
            pltpu.SemaphoreType.DMA((3,)),
        ],
        3_000_000_000,
        14_000_000,
        back,
        first_residual,
        cotangent,
        gains,
        w_feed_in,
        w_feed_out,
        w_cross_output,
    )
    blocks = n_dev if part % 8 == 0 else 1
    feed_grad = call(
        feed_grad_kernel,
        "feed_grads",
        [vmem] * 6,
        like((blocks, 9, D // blocks, D)),
        [],
        1_500_000_000,
        14_000_000,
        hidden,
        d_pre,
        normed_feed,
        cross_mixed,
        d_branch,
        cotangent,
    )
    if blocks == 1:
        feed_grad = jnp.concatenate(
            [
                feed_grad[0, :4].reshape(4, n_dev, part, D).transpose(1, 0, 2, 3),
                feed_grad[0, 4:8].reshape(n_dev, 4, part, D),
                feed_grad[0, 8].reshape(n_dev, 1, part, D),
            ],
            axis=1,
        )
    column = jnp.arange(2 * H * TGT, dtype=jnp.int32)
    place = (
        (lane[:, None] // 48 == column[None, :] // (H * TGT))
        & (lane[:, None] % 16 == (column[None, :] // TGT) % H)
    ).astype(bf16)
    walks, join = wires.gather_dp(d_send)
    (feed_grad,) = wires.finish(walks, wires.begin(walks), feed_grad)
    feed_sum = lax.psum_scatter(feed_grad, both, scatter_dimension=0).astype(f32)
    wires.together(walks)
    all_mixed = join()
    short, long, d_key_cross, d_value_cross = cross_grad(
        bounds, arrival, all_queries, all_mixed, place, key_cross, value_cross
    )

    height = D // (2 * chunks) if chunked else D

    def encode_grad(first, count, before=()):
        at = pl.BlockSpec((tall, D), lambda step: (step + first, 0))
        return call(
            encode_grad_kernel,
            "encodings_grad",
            [at, at, weight_at(5), weight_at(6)] + [hbm] * len(before),
            like((keys_total, D)),
            [],
            14_000_000_000 * count // steps,
            30_000_000 * count // steps,
            d_key_cross.reshape(keys_total, D),
            d_value_cross.reshape(keys_total, D),
            w_first,
            w_first,
            *before,
            grid=(count,),
            out_specs=at,
            input_output_aliases={4: 0} if before else {},
        )

    walks = wires.scatter_dp(short, long)
    got = wires.begin(walks)
    key_grads = call(
        functools.partial(weight_grad_kernel, steps),
        "cross_weight_grads",
        [smem, block, block, block],
        [like((chunks, height, 2 * D))] * 2,
        [pltpu.VMEM((2, D, D), f32)],
        14_500_000_000,
        32_000_000,
        orders,
        encodings,
        d_key_cross.reshape(keys_total, D),
        d_value_cross.reshape(keys_total, D),
        grid=(steps,),
        out_specs=[pl.BlockSpec((chunks, height, 2 * D), lambda i: (0, 0, 0))] * 2,
    )
    (key_grads,) = wires.finish(walks, got, key_grads)
    got = wires.begin(walks)
    if chunked:
        key_walk = [Walk(wires.scatter_pair_walk(*key_grads, D))]
        (got,) = wires.finish(key_walk, wires.begin(key_walk), got)
    (encodings_grad,) = wires.finish(walks, got, encode_grad(0, steps // 2))
    d_query_cross = jnp.concatenate([walk.result for walk in walks], axis=1)
    if chunked:
        d_query_cross = key_walk[0].tie(d_query_cross)
        got_key = wires.begin(key_walk)
    decoder_grad, *grads = call(
        self_grad_kernel,
        "self_backward",
        [smem] + [vmem] * 14 + [hbm],
        [
            like(wide),
            *[like((chunks, height, 4 * D))] * 2,
            *[like((chunks, height, D + 128))] * 2,
        ],
        [
            weights(5, D, D),
            weights(rows, D),
            weights(rows, D),
            weights(rows, D),
            weights(rows, D),
            pltpu.VMEM((TGT, H * TGT), f32),
            pltpu.SemaphoreType.DMA((5,)),
        ],
        3_000_000_000,
        14_000_000,
        orders,
        d_query_cross,
        d_second,
        first_residual,
        decoder_states,
        normed_cross,
        normed_self,
        query_self,
        key_self,
        value_self,
        self_mixed,
        gains,
        bias,
        buckets_wide,
        grad_gain_feed,
        w_first,
    )

    if chunked:
        (grads,) = wires.finish(key_walk, got_key, grads)
        walks = [
            Walk(wires.scatter_pair_walk(*grads[0:2], 2 * D)),
            Walk(wires.scatter_walk(*grads[2:4], "xyz")),
        ]
        got_key = wires.begin(key_walk)
        (encodings_grad,) = wires.finish(walks, wires.begin(walks), encodings_grad)
        got = wires.begin(walks)
        encodings_grad = encode_grad(steps // 2, steps - steps // 2, (encodings_grad,))
        (got, encodings_grad) = wires.finish(key_walk, got_key, got, encodings_grad)
        wires.finish(walks, got)
        got, got_key = wires.begin(walks), wires.begin(key_walk)
        wires.finish(walks, got)
        got = wires.begin(walks)
        (got,) = wires.finish(key_walk, got_key, got)
        (feed_sum,) = wires.finish(walks, got, feed_sum)
        first_sum, third_sum = wires.together(walks)
        key_sum = wires.together(key_walk)[0]
    else:
        first_sum, third_sum, key_sum = scatter_plain([grads[0], grads[2], key_grads[0]])
        encodings_grad = encode_grad(steps // 2, steps - steps // 2, (encodings_grad,))

    small_sum = third_sum[:, D:]
    bias_sum = jnp.sum(jnp.where(spot, small_sum[:1], 0.0), axis=1)
    return (
        layer_output,
        decoder_grad,
        encodings_grad,
        small_sum[:, 0],
        bias_sum,
        first_sum[:, :D],
        first_sum[:, D : 2 * D],
        first_sum[:, 2 * D : 3 * D],
        first_sum[:, 3 * D :],
        small_sum[:, 1],
        third_sum[:, :D],
        key_sum[:, :D],
        key_sum[:, D:],
        feed_sum[8],
        small_sum[:, 2],
        jnp.concatenate([feed_sum[t] for t in range(4)], axis=1),
        feed_sum[4:8].reshape(4 * part, D),
    )


def solution(mesh):
    rows = P(both, None)
    flat = P(both)
    in_specs = (rows, rows, flat, P(), flat, flat, rows, rows, rows, rows)
    in_specs += (flat, rows, rows, rows, rows, flat, rows, rows, rows)
    out_specs = (rows, rows, rows, flat, flat, rows, rows, rows, rows)
    out_specs += (flat, rows, rows, rows, rows, flat, rows, rows)
    return jax.shard_map(
        functools.partial(shards, mesh.shape["dp"], mesh.shape["fsdp"]),
        mesh=mesh,
        in_specs=in_specs,
        out_specs=out_specs,
        check_vma=False,
    )
```

```python
import functools
import math

import jax
import jax.numpy as jnp
from jax import lax
from jax.experimental import pallas as pl
from jax.experimental.pallas import tpu as pltpu
from jax.sharding import PartitionSpec as P

D = 768
H = 12
DH = 64
NB = 32
TGT = 32
QPD = 4
GROUPS = 3
TILE = 256
CHUNKS = 16
stage_orders = ("zxy", "zyx", "xyz")

epsilon = 1e-06
masked_score = -1e30
both = ("dp", "fsdp")
bf16 = jnp.bfloat16
f32 = jnp.float32


def matmul(left_side, right_side):
    return jnp.dot(left_side, right_side, preferred_element_type=f32)


def dot_tn(left_side, right_side):
    return lax.dot_general(
        left_side, right_side, (((0,), (0,)), ((), ())), preferred_element_type=f32
    )


def dot_nt(left_side, right_side):
    return lax.dot_general(
        left_side, right_side, (((1,), (1,)), ((), ())), preferred_element_type=f32
    )


def rms_norm(values, gain_vector):
    return (
        values
        * lax.rsqrt(jnp.mean(values * values, axis=-1, keepdims=True) + epsilon)
        * gain_vector
    )


def pieces_of(values):
    high = values.astype(bf16)
    rest = values - high.astype(f32)
    mid = rest.astype(bf16)
    low = (rest - mid.astype(f32)).astype(bf16)
    return high, mid, low


def split_pieces(values):
    high = lax.reduce_precision(values, 8, 7)
    mid = lax.reduce_precision(values - high, 8, 7)
    low = values - high - mid
    return high.astype(bf16), mid.astype(bf16), low.astype(bf16)


def spread_heads(rows):
    tall = jnp.concatenate([rows, rows, rows, rows], axis=0)
    head_row = lax.broadcasted_iota(jnp.int32, (4 * TGT, 4 * DH), 0) // TGT
    head_col = lax.broadcasted_iota(jnp.int32, (4 * TGT, 4 * DH), 1) // DH
    return jnp.where(head_row == head_col, tall, jnp.zeros_like(tall))


def gather_heads(tall):
    head_col = lax.broadcasted_iota(jnp.int32, (TGT, 4 * DH), 1) // DH
    rows = jnp.zeros((TGT, 4 * DH), f32)
    for head in range(4):
        rows = jnp.where(head_col == head, tall[head * TGT : (head + 1) * TGT], rows)
    return rows


def run_tiles(bounds_ref, block, query, slot):
    start = bounds_ref[block, query]
    end = bounds_ref[block, query + 1]
    first = (start // 16) * 16
    count = (end - first + TILE - 1) // TILE
    return start, end, first, count


def tile_rows(first, step, start, end, slot):
    want = first + step * TILE
    base = pl.multiple_of(jnp.minimum(want, slot - TILE), 16)
    rows = base + lax.broadcasted_iota(jnp.int32, (TILE, 4 * TGT), 0)
    inside = (rows >= jnp.maximum(start, want)) & (rows < end)
    return base, inside


def column_of(row):
    return jnp.transpose(jnp.broadcast_to(row, (8, 4 * TGT)))[:, :1]


def mix_kernel(slot, bounds_ref, place_ref, q_ref, k_ref, v_ref, o_ref, score_ref, mix_ref):
    block = pl.program_id(0)
    lane = lax.broadcasted_iota(jnp.int32, (TGT, 128), 1)
    runs = [run_tiles(bounds_ref, block, query, slot) for query in range(QPD)]
    steps = functools.reduce(jnp.maximum, [run[3] for run in runs])
    pairs = [(query, g) for query in range(QPD) for g in range(GROUPS)]
    spread = {
        (query, g): spread_heads(
            q_ref[0, query * TGT : (query + 1) * TGT, g * 256 : (g + 1) * 256]
        )
        for query, g in pairs
    }

    def score_step(step, tops):
        held = pl.ds(pl.multiple_of(step * TILE, TILE), TILE)
        places = [tile_rows(first, step, start, end, slot) for start, end, first, count in runs]
        new_tops = []
        for i, (query, g) in enumerate(pairs):
            base, inside = places[query]
            keys = k_ref[0, pl.ds(base, TILE), g * 256 : (g + 1) * 256]
            scores = jnp.where(inside, dot_nt(keys, spread[query, g]), masked_score)
            score_ref[i, held, :] = scores
            new_tops.append(jnp.maximum(tops[i], jnp.max(scores, axis=0, keepdims=True)))
        return tuple(new_tops)

    tops = lax.fori_loop(
        0, steps, score_step, tuple(jnp.full((1, 4 * TGT), masked_score, f32) for pair in pairs)
    )
    mix_ref[...] = jnp.zeros_like(mix_ref)

    def mix_step(step, sums):
        held = pl.ds(pl.multiple_of(step * TILE, TILE), TILE)
        places = [tile_rows(first, step, start, end, slot) for start, end, first, count in runs]
        new_sums, raised = [], []
        for i in range(len(pairs)):
            weights = jnp.exp(score_ref[i, held, :] - tops[i])
            new_sums.append(sums[i] + jnp.sum(weights, axis=0, keepdims=True))
            raised.append(weights.astype(bf16))
        for i, (query, g) in enumerate(pairs):
            values = v_ref[0, pl.ds(places[query][0], TILE), g * 256 : (g + 1) * 256]
            mix_ref[i] += dot_tn(raised[i], values)
        return tuple(new_sums)

    sums = lax.fori_loop(
        0, steps, mix_step, tuple(jnp.zeros((1, 4 * TGT), f32) for pair in pairs)
    )
    total, top = jnp.concatenate(sums, axis=0), jnp.concatenate(tops, axis=0)
    scales = jnp.transpose(1.0 / total)
    log_sums = jnp.transpose(top + jnp.log(total))
    for query in range(QPD):
        rows_of = slice(query * TGT, (query + 1) * TGT)
        logs = jnp.zeros((TGT, 128), f32)
        for g in range(GROUPS):
            i = query * GROUPS + g
            scale = scales[:, i : i + 1]
            log_sum = log_sums[:, i : i + 1]
            o_ref[0, rows_of, g * 256 : (g + 1) * 256] = gather_heads(mix_ref[i] * scale).astype(
                bf16
            )
            for head in range(4):
                logs = jnp.where(
                    (lane % 16 == g * 4 + head) & (lane < 48),
                    log_sum[head * TGT : (head + 1) * TGT],
                    logs,
                )
        high, mid, low = pieces_of(logs)
        o_ref[0, rows_of, D:] = jnp.where(
            lane < 16, high.astype(f32), jnp.where(lane < 32, mid.astype(f32), low.astype(f32))
        ).astype(bf16)


def grad_kernel(
    slot,
    bounds_ref,
    order_ref,
    q_ref,
    m_ref,
    place_ref,
    k_ref,
    v_ref,
    short_ref,
    long_ref,
    dk_ref,
    dv_ref,
    sum_ref,
):
    block = pl.program_id(0)
    dk_ref[...] = jnp.zeros_like(dk_ref)
    dv_ref[...] = jnp.zeros_like(dv_ref)
    sum_ref[...] = jnp.zeros_like(sum_ref)
    runs = [run_tiles(bounds_ref, block, query, slot) for query in range(QPD)]
    steps = functools.reduce(jnp.maximum, [run[3] for run in runs])
    pairs = [(query, g) for query in range(QPD) for g in range(GROUPS)]
    row = lax.broadcasted_iota(jnp.int32, (TGT, 2 * H * TGT), 0)
    target = lax.broadcasted_iota(jnp.int32, (TGT, 2 * H * TGT), 1) % TGT
    spread, spread_m, logs, deltas = {}, {}, {}, {}
    for query in range(QPD):
        rows_of = slice(query * TGT, (query + 1) * TGT)
        placed = matmul(m_ref[0, rows_of, D : D + 128], place_ref[...])
        flat = jnp.sum(jnp.where(row == target, placed, 0.0), axis=0, keepdims=True)
        for g in range(GROUPS):
            columns = slice(g * 256, (g + 1) * 256)
            spread[query, g] = spread_heads(q_ref[0, rows_of, columns])
            spread_m[query, g] = spread_heads(m_ref[0, rows_of, columns])
            logs[query, g] = flat[:, g * 128 : (g + 1) * 128]
            deltas[query, g] = flat[:, (GROUPS + g) * 128 : (GROUPS + g + 1) * 128]

    def step_of(step, carry):
        places = [tile_rows(first, step, start, end, slot) for start, end, first, count in runs]
        softs, changes = [], []
        for query, g in pairs:
            base, inside = places[query]
            columns = slice(g * 256, (g + 1) * 256)
            scores = dot_nt(k_ref[0, pl.ds(base, TILE), columns], spread[query, g])
            soft = jnp.where(inside, jnp.exp(scores - logs[query, g]), 0.0)
            d_soft = dot_nt(v_ref[0, pl.ds(base, TILE), columns], spread_m[query, g])
            changes.append((soft * (d_soft - deltas[query, g])).astype(bf16))
            softs.append(soft.astype(bf16))
        for i, (query, g) in enumerate(pairs):
            keys = k_ref[0, pl.ds(places[query][0], TILE), g * 256 : (g + 1) * 256]
            sum_ref[i] += dot_tn(changes[i], keys)
        for i, (query, g) in enumerate(pairs):
            rows_of, columns = pl.ds(places[query][0], TILE), slice(g * 256, (g + 1) * 256)
            dk_ref[0, rows_of, columns] += matmul(changes[i], spread[query, g]).astype(bf16)
            dv_ref[0, rows_of, columns] += matmul(softs[i], spread_m[query, g]).astype(bf16)
        return carry

    lax.fori_loop(0, steps, step_of, 0)
    for query in range(QPD):
        rows_of = slice(query * TGT, (query + 1) * TGT)
        d_query = jnp.concatenate(
            [gather_heads(sum_ref[query * GROUPS + g]) for g in range(GROUPS)], axis=1
        )
        short_ref[0, rows_of, :] = d_query[:, : D // 3].astype(bf16)
        long_ref[0, rows_of, :] = d_query[:, D // 3 :].astype(bf16)


def cross_mix(bounds, arrival, queries, keys, values):
    blocks, slot = keys.shape[0], keys.shape[1]
    rows = queries.shape[1]
    at = lambda i, *refs: (i, 0, 0)
    come = lambda i, bounds_ref, order_ref: (order_ref[i], 0, 0)
    return pl.pallas_call(
        functools.partial(mix_kernel, slot),
        grid_spec=pltpu.PrefetchScalarGridSpec(
            num_scalar_prefetch=2,
            grid=(blocks,),
            in_specs=[
                pl.BlockSpec((1, rows, D), come),
                pl.BlockSpec((1, slot, D), at),
                pl.BlockSpec((1, slot, D), at),
            ],
            out_specs=[pl.BlockSpec((1, rows, D + 128), at)],
            scratch_shapes=[
                pltpu.VMEM((QPD * GROUPS, slot + TILE, 4 * TGT), f32),
                pltpu.VMEM((QPD * GROUPS, 4 * TGT, 256), f32),
            ],
        ),
        out_shape=[
            jax.ShapeDtypeStruct((blocks, rows, D + 128), bf16),
        ],
        compiler_params=pltpu.CompilerParams(vmem_limit_bytes=60 * 1024 * 1024),
        cost_estimate=pl.CostEstimate(
            flops=12_000_000_000, bytes_accessed=22_000_000, transcendentals=4_000_000
        ),
        name="cross_mix",
    )(bounds, arrival, queries, keys, values)[0]


def cross_grad(bounds, arrival, queries, mixed, place, keys, values):
    blocks, slot = keys.shape[0], keys.shape[1]
    rows = queries.shape[1]
    at = lambda i, *refs: (i, 0, 0)
    come = lambda i, bounds_ref, order_ref: (order_ref[i], 0, 0)
    return pl.pallas_call(
        functools.partial(grad_kernel, slot),
        grid_spec=pltpu.PrefetchScalarGridSpec(
            num_scalar_prefetch=2,
            grid=(blocks,),
            in_specs=[
                pl.BlockSpec((1, rows, D), come),
                pl.BlockSpec((1, rows, D + 128), come),
                pl.BlockSpec((128, 2 * H * TGT), lambda i, *refs: (0, 0)),
                pl.BlockSpec((1, slot, D), at),
                pl.BlockSpec((1, slot, D), at),
            ],
            out_specs=[
                pl.BlockSpec((1, rows, D // 3), come),
                pl.BlockSpec((1, rows, D - D // 3), come),
                pl.BlockSpec((1, slot, D), at),
                pl.BlockSpec((1, slot, D), at),
            ],
            scratch_shapes=[pltpu.VMEM((QPD * GROUPS, 4 * TGT, 256), f32)],
        ),
        out_shape=[
            jax.ShapeDtypeStruct((blocks, rows, D // 3), bf16),
            jax.ShapeDtypeStruct((blocks, rows, D - D // 3), bf16),
            jax.ShapeDtypeStruct((blocks, slot, D), bf16),
            jax.ShapeDtypeStruct((blocks, slot, D), bf16),
        ],
        compiler_params=pltpu.CompilerParams(vmem_limit_bytes=60 * 1024 * 1024),
        cost_estimate=pl.CostEstimate(
            flops=24_000_000_000, bytes_accessed=42_000_000, transcendentals=4_000_000
        ),
        name="cross_grad",
    )(bounds, arrival, queries, mixed, place, keys, values)


def flag_of(orders_ref):
    return orders_ref[6 * CHUNKS]


def start_load(orders_ref, mine, other, stage, sem):
    flag = flag_of(orders_ref)
    for core, sources in ((flag, mine), (1 - flag, other)):
        place = 0
        for source in sources:
            count = source.shape[0]
            pltpu.make_async_copy(source, stage.at[core, pl.ds(place, count)], sem).start()
            place += count


def wait_load(into, sem):
    pltpu.make_async_copy(into, into, sem).wait()


def assemble(orders_ref, order, stage, columns, into):
    if stage.shape[1] == 1:
        into[...] = stage[0, 0, :, columns]
        return
    rows = 2 * stage.shape[2]
    for i in range(stage.shape[1]):
        base = pl.multiple_of(orders_ref[order * CHUNKS + i] * rows, 16)
        into[pl.ds(base, rows), :] = jnp.concatenate(
            [stage[0, i, :, columns], stage[1, i, :, columns]], axis=0
        )


def store_grad(orders_ref, order, grad, mine_ref, other_ref, columns):
    chunks, rows = mine_ref.shape[0], mine_ref.shape[1]
    if chunks == 1:
        mine_ref[0, :, columns] = grad[...].astype(bf16)
        return
    first = flag_of(orders_ref) == 0
    for i in range(chunks):
        to = orders_ref[(3 + order) * CHUNKS + i]
        low = grad[2 * i * rows : (2 * i + 1) * rows, :]
        high = grad[(2 * i + 1) * rows : (2 * i + 2) * rows, :]
        mine_ref[to, :, columns] = jnp.where(first, low, high).astype(bf16)
        other_ref[to, :, columns] = jnp.where(first, high, low).astype(bf16)


def iota(shape, axis):
    return lax.broadcasted_iota(jnp.int32, shape, axis)


def project_kernel(enc_ref, w_ref, out_ref):
    out_ref[...] = matmul(enc_ref[...], w_ref[0]).astype(bf16)


def encode_grad_kernel(dk_ref, dv_ref, wk_ref, wv_ref, *refs):
    out_ref = refs[-1]
    out_ref[...] = (dot_nt(dk_ref[...], wk_ref[0]) + dot_nt(dv_ref[...], wv_ref[0])).astype(bf16)


def weight_grad_kernel(steps, orders_ref, enc_ref, dk_ref, dv_ref, mine_ref, other_ref, sum_ref):
    step = pl.program_id(0)
    rows = enc_ref[...]
    products = [dot_tn(rows, dk_ref[...]), dot_tn(rows, dv_ref[...])]

    @pl.when(step == 0)
    def first():
        for i in range(2):
            sum_ref[i] = products[i]

    @pl.when(step > 0)
    def later():
        for i in range(2):
            sum_ref[i] += products[i]

    @pl.when(step == steps - 1)
    def store():
        for i in range(2):
            columns = slice(i * D, (i + 1) * D)
            store_grad(orders_ref, i, sum_ref.at[i], mine_ref, other_ref, columns)


def self_kernel(counts, orders_ref, states_ref, buckets_ref, *refs):
    refs = list(refs)
    pieces = []
    for mine, other in counts:
        pieces.append((refs[:mine], refs[mine : mine + other]))
        refs = refs[mine + other :]
    normed_ref, q_ref, k_ref, v_ref, mixed_ref, first_ref, normed_cross_ref = refs[:7]
    q_cross_ref, gains_ref, bias_ref, out_ref, w_ref, small_ref = refs[7:13]
    stages, sems, out_sems = refs[13:16], refs[16], refs[17]
    for order in (2, 0, 1):
        start_load(orders_ref, *pieces[order], stages[order], sems.at[order])

    def put(weight, order, place):
        assemble(
            orders_ref, order, stages[order], slice(place * D, (place + 1) * D), w_ref.at[weight]
        )
        pltpu.make_async_copy(w_ref.at[weight], out_ref.at[weight], out_sems.at[weight]).start()

    wait_load(stages[2], sems.at[2])
    assemble(orders_ref, 2, stages[2], slice(D, D + 128), small_ref)
    small = small_ref[...]
    gains_ref[...] = jnp.transpose(small.astype(f32))[:8]
    span = D // NB
    first_row, row = span * iota((NB, D), 0), iota((NB, D), 1)
    pick = ((row >= first_row) & (row < first_row + span)).astype(f32).astype(bf16)
    table = matmul(pick, small).astype(bf16)
    wide = (iota((128, H * TGT), 0) == 16 + (iota((128, H * TGT), 1) >> 5)).astype(f32).astype(bf16)
    table = matmul(table, wide)
    buckets = buckets_ref[...]
    later = iota((TGT, 128), 0) > (iota((TGT, 128), 1) & (TGT - 1))
    for g in range(GROUPS):
        bias = jnp.zeros((TGT, 128), f32)
        for n in range(NB):
            bias = jnp.where(buckets == n, table[n : n + 1, g * 128 : (g + 1) * 128], bias)
        bias_ref[:, g * 128 : (g + 1) * 128] = jnp.where(later, masked_score, bias)

    states = states_ref[...].astype(f32)
    normed = rms_norm(states, gains_ref[0:1]).astype(bf16)
    normed_ref[...] = normed
    wait_load(stages[0], sems.at[0])
    put(0, 0, 0)
    q_ref[...] = matmul(normed, w_ref[0]).astype(bf16)
    put(1, 0, 1)
    k_ref[...] = matmul(normed, w_ref[1]).astype(bf16)
    wait_load(stages[1], sems.at[1])
    put(2, 1, 0)
    v_ref[...] = matmul(normed, w_ref[2]).astype(bf16)
    for query in range(QPD):
        rows_of = slice(query * TGT, (query + 1) * TGT)
        for g in range(GROUPS):
            columns = slice(g * 256, (g + 1) * 256)
            spread = spread_heads(q_ref[rows_of, columns])
            scores = dot_nt(k_ref[rows_of, columns], spread) + bias_ref[:, g * 128 : (g + 1) * 128]
            raised = jnp.exp(scores - jnp.max(scores, axis=0, keepdims=True))
            soft = raised / jnp.sum(raised, axis=0, keepdims=True)
            tall = dot_tn(soft.astype(bf16), v_ref[rows_of, columns])
            mixed_ref[rows_of, columns] = gather_heads(tall).astype(bf16)
    put(3, 1, 1)
    first = states + matmul(mixed_ref[...], w_ref[3])
    first_ref[...] = first
    normed_cross = rms_norm(first, gains_ref[1:2]).astype(bf16)
    normed_cross_ref[...] = normed_cross
    put(4, 2, 0)
    q_cross_ref[...] = matmul(normed_cross, w_ref[4]).astype(bf16)
    put(5, 0, 2)
    put(6, 1, 2)
    for weight in range(7):
        pltpu.make_async_copy(w_ref.at[weight], out_ref.at[weight], out_sems.at[weight]).wait()


def exact_sum(values, picks):
    high, mid, low = pieces_of(values)
    return matmul(high, picks) + matmul(mid, picks) + matmul(low, picks)


def norm_back(values, gain, d_normed):
    scale = lax.rsqrt(jnp.mean(values * values, axis=-1, keepdims=True) + epsilon)
    scaled = d_normed * gain
    inner = jnp.mean(scaled * values, axis=-1, keepdims=True)
    d_values = scale * scaled - values * (scale * scale * scale * inner)
    d_gain = jnp.sum(d_normed * values * scale, axis=0, keepdims=True)
    return d_values, d_gain


def feed_kernel(
    back_ref,
    first_ref,
    cot_ref,
    gains_ref,
    fi_ref,
    fo_ref,
    co_ref,
    out_ref,
    send_ref,
    second_ref,
    branch_ref,
    mixed_ref,
    normed_ref,
    hidden_ref,
    pre_ref,
    gain_ref,
    wc_ref,
    wi_ref,
    wo_ref,
    logs_ref,
    sems,
):
    blocks, rows = back_ref.shape[0], back_ref.shape[1]
    copies = [
        pltpu.make_async_copy(source, into, sems.at[i])
        for i, (source, into) in enumerate(((co_ref, wc_ref), (fi_ref, wi_ref), (fo_ref, wo_ref)))
    ]
    for copy in copies:
        copy.start()
    widen = ((iota((128, D), 0) & 15) == (iota((128, D), 1) >> 6)) & (iota((128, D), 0) < 48)
    widen = widen.astype(f32).astype(bf16)

    def log_step(i, top):
        logs = matmul(back_ref[i, :, D:], widen)
        logs_ref[i] = logs
        return jnp.maximum(top, logs)

    top = lax.fori_loop(0, blocks, log_step, jnp.full((rows, D), masked_score, f32))

    def share_step(i, carry):
        total, mixed = carry
        share = jnp.exp(logs_ref[i] - top)
        return total + share, mixed + share * back_ref[i, :, :D].astype(f32)

    zero = jnp.zeros((rows, D), f32)
    total, mixed = lax.fori_loop(0, blocks, share_step, (zero, zero))
    mixed = mixed / total
    logs = top + jnp.log(total)
    mixed_ref[...] = mixed.astype(bf16)
    copies[0].wait()
    second = first_ref[...] + matmul(mixed_ref[...], wc_ref[...])
    normed = rms_norm(second, gains_ref[2:3]).astype(bf16)
    normed_ref[...] = normed
    copies[1].wait()
    copies[2].wait()
    cot = cot_ref[...]
    root = 0.7978845608028654

    def feed_step(t, carry):
        out, d_normed = carry
        pre = matmul(normed, wi_ref[t])
        w_out = wo_ref[pl.ds(pl.multiple_of(t * D, D), D), :]
        bent = jnp.tanh(root * (pre + 0.044715 * pre * pre * pre))
        hidden = (0.5 * pre * (1.0 + bent)).astype(bf16)
        slope = 0.5 * (1.0 + bent) + 0.5 * pre * (1.0 - bent * bent) * (
            root * (1.0 + 3 * 0.044715 * pre * pre)
        )
        d_pre = (dot_nt(cot, w_out) * slope).astype(bf16)
        hidden_ref[t] = hidden
        pre_ref[t] = d_pre
        return out + matmul(hidden, w_out), d_normed + dot_nt(d_pre, wi_ref[t])

    out, d_normed = lax.fori_loop(0, 4, feed_step, (zero, zero))
    out_ref[...] = (second + out).astype(bf16)
    d_values, gain_ref[...] = norm_back(second, gains_ref[2:3], d_normed)
    d_second = cot.astype(f32) + d_values
    second_ref[...] = d_second
    branch_ref[...] = d_second.astype(bf16)
    d_mixed = dot_nt(branch_ref[...], wc_ref[...]).astype(bf16)
    send_ref[:, :D] = d_mixed
    lane = iota((D, 128), 1)
    row = iota((D, 128), 0)
    pick = ((row == (lane & 15) * DH) & (lane < 48)).astype(f32).astype(bf16)
    add = (((row >> 6) == (lane & 15)) & (lane >= 48) & (lane < 96)).astype(f32).astype(bf16)
    extra = exact_sum(logs, pick) + exact_sum(d_mixed.astype(f32) * mixed, add)
    high, mid, low = pieces_of(extra)
    slot_of = iota((rows, 128), 1) >> 4
    slot_of = jnp.where(slot_of >= 3, slot_of - 3, slot_of)
    send_ref[:, D:] = jnp.where(
        slot_of == 0, high.astype(f32), jnp.where(slot_of == 1, mid.astype(f32), low.astype(f32))
    ).astype(bf16)


def feed_grad_kernel(hidden_ref, pre_ref, normed_ref, mixed_ref, branch_ref, cot_ref, out_ref):
    blocks, slabs, part, width = out_ref.shape

    def put(grad, block, slab, row):
        out_ref[block, slab] = grad[row : row + part].astype(bf16)

    for t in range(4):
        grad = dot_tn(normed_ref[...], pre_ref[t])
        for i in range(blocks):
            put(grad, i, t, i * part)
        grad = dot_tn(hidden_ref[t], cot_ref[...])
        for i in range(blocks):
            place = t * blocks + i
            put(grad, place // 4, 4 + place % 4, i * part)
    grad = dot_tn(mixed_ref[...], branch_ref[...])
    for i in range(blocks):
        put(grad, i, 8, i * part)


def self_grad_kernel(
    orders_ref,
    back_ref,
    second_ref,
    first_ref,
    states_ref,
    normed_cross_ref,
    normed_ref,
    q_ref,
    k_ref,
    v_ref,
    mixed_ref,
    gains_ref,
    bias_ref,
    buckets_ref,
    gain_feed_ref,
    *refs,
):
    weights_ref, out_ref, ga_ref, ha_ref, w_ref, dq_ref, dk_ref, dv_ref, dm_ref, sums_ref, sems = refs
    half = D // 2
    last = ga_ref.shape[2]
    cut = 2 * D + half + 128
    for i in (4, 3, 0, 1, 2):
        pltpu.make_async_copy(weights_ref.at[i], w_ref.at[i], sems.at[i]).start()

    d_query = back_ref[...].astype(bf16)
    grad = dot_tn(normed_cross_ref[...], d_query)
    store_grad(orders_ref, 0, grad[:, :half], ga_ref, ha_ref, slice(2 * D, 2 * D + half))
    store_grad(orders_ref, 1, grad[:, half:], ga_ref, ha_ref, slice(last - half, last))
    wait_load(w_ref.at[4], sems.at[4])
    d_values, gain_cross = norm_back(first_ref[...], gains_ref[1:2], dot_nt(d_query, w_ref[4]))
    d_first = second_ref[...] + d_values
    branch = d_first.astype(bf16)
    store_grad(orders_ref, 1, dot_tn(mixed_ref[...], branch), ga_ref, ha_ref, slice(cut + D, cut + 2 * D))
    wait_load(w_ref.at[3], sems.at[3])
    dm_ref[...] = dot_nt(branch, w_ref[3]).astype(bf16)
    sums_ref[...] = jnp.zeros_like(sums_ref)
    for query in range(QPD):
        rows_of = slice(query * TGT, (query + 1) * TGT)
        for g in range(GROUPS):
            columns = slice(g * 256, (g + 1) * 256)
            lanes = slice(g * 128, (g + 1) * 128)
            spread = spread_heads(q_ref[rows_of, columns])
            spread_m = spread_heads(dm_ref[rows_of, columns])
            keys = k_ref[rows_of, columns]
            scores = dot_nt(keys, spread) + bias_ref[:, lanes]
            raised = jnp.exp(scores - jnp.max(scores, axis=0, keepdims=True))
            soft = raised / jnp.sum(raised, axis=0, keepdims=True)
            d_soft = dot_nt(v_ref[rows_of, columns], spread_m)
            delta = jnp.sum(soft * d_soft, axis=0, keepdims=True)
            d_scores = (soft * (d_soft - delta)).astype(bf16)
            sums_ref[:, lanes] += d_scores.astype(f32)
            dq_ref[rows_of, columns] = gather_heads(dot_tn(d_scores, keys)).astype(bf16)
            dk_ref[rows_of, columns] = matmul(d_scores, spread).astype(bf16)
            dv_ref[rows_of, columns] = matmul(soft.astype(bf16), spread_m).astype(bf16)
    normed = normed_ref[...]
    store_grad(orders_ref, 0, dot_tn(normed, dq_ref[...]), ga_ref, ha_ref, slice(0, D))
    store_grad(orders_ref, 0, dot_tn(normed, dk_ref[...]), ga_ref, ha_ref, slice(D, 2 * D))
    store_grad(orders_ref, 1, dot_tn(normed, dv_ref[...]), ga_ref, ha_ref, slice(cut, cut + D))
    wait_load(w_ref.at[0], sems.at[0])
    wait_load(w_ref.at[1], sems.at[1])
    wait_load(w_ref.at[2], sems.at[2])
    d_normed = (
        dot_nt(dq_ref[...], w_ref[0]) + dot_nt(dk_ref[...], w_ref[1]) + dot_nt(dv_ref[...], w_ref[2])
    )
    d_values, gain_self = norm_back(states_ref[...].astype(f32), gains_ref[0:1], d_normed)
    out_ref[...] = (d_first + d_values).astype(bf16)
    buckets = buckets_ref[...]
    by_bucket = []
    for n in range(NB):
        sums = []
        for g in range(GROUPS):
            mine = jnp.where(buckets == n, sums_ref[:, g * 128 : (g + 1) * 128], 0.0)
            sums.append(jnp.sum(mine, axis=0, keepdims=True))
        by_bucket.append(jnp.concatenate(sums, axis=1))
    by_bucket = jnp.concatenate(by_bucket, axis=0)
    lane = iota((H * TGT, 128), 1)
    narrow = ((iota((H * TGT, 128), 0) >> 5) == lane - 16).astype(f32).astype(bf16)
    table = exact_sum(by_bucket, narrow).astype(bf16)
    span = D // NB
    first_row, row = span * iota((D, NB), 1), iota((D, NB), 0)
    put = ((row >= first_row) & (row < first_row + span)).astype(f32).astype(bf16)
    gains = jnp.concatenate([gain_self, gain_cross, gain_feed_ref[...], jnp.zeros((125, D), f32)])
    small = matmul(put, table) + jnp.transpose(gains)
    store_grad(orders_ref, 0, small, ga_ref, ha_ref, slice(cut - 128, cut))


hbm = pl.BlockSpec(memory_space=pl.ANY)
vmem = pl.BlockSpec(memory_space=pltpu.VMEM)
smem = pl.BlockSpec(memory_space=pltpu.SMEM)


def like(shape, kind=bf16):
    return jax.ShapeDtypeStruct(shape, kind)


def call(kernel, name, ins, outs, scratch, flops, moved, *values, **more):
    return pl.pallas_call(
        kernel,
        in_specs=ins,
        out_shape=outs,
        scratch_shapes=scratch,
        compiler_params=pltpu.CompilerParams(vmem_limit_bytes=60 * 1024 * 1024),
        cost_estimate=pl.CostEstimate(flops=flops, bytes_accessed=moved, transcendentals=0),
        name=name,
        **more,
    )(*values)


def weights(*shape):
    return pltpu.VMEM(shape, bf16)


class Wires:
    def __init__(self, n_dp, n_fsdp):
        self.n_dp, self.n_fsdp = n_dp, n_fsdp
        self.sizes = {"x": n_fsdp // 2, "y": n_fsdp // 2, "z": n_dp // (n_fsdp // 2), "c": 2}
        dp, fsdp = lax.axis_index("dp"), lax.axis_index("fsdp")
        size = self.sizes
        self.at = {"z": dp // size["x"], "x": dp % size["x"], "y": fsdp // 2, "c": fsdp % 2}

    def shift(self, value, axis, steps=1):
        size = self.sizes
        pairs = []
        for dp in range(self.n_dp):
            for fsdp in range(self.n_fsdp):
                at = {"z": dp // size["x"], "x": dp % size["x"], "y": fsdp // 2, "c": fsdp % 2}
                here = dp * self.n_fsdp + fsdp
                at[axis] = (at[axis] + steps) % size[axis]
                there = (at["z"] * size["x"] + at["x"]) * self.n_fsdp + at["y"] * 2 + at["c"]
                pairs.append((here, there))
        return lax.ppermute(value, both, pairs)

    def begin(self, walks):
        return [[self.shift(*ask) for ask in walk.asks] for walk in walks if not walk.over]

    def finish(self, walks, got, *tied):
        got, tied = lax.optimization_barrier((got, tied))
        for walk, values in zip([walk for walk in walks if not walk.over], got):
            walk.take(values)
        return tied

    def together(self, walks, steps=100):
        for step in range(steps):
            if all(walk.over for walk in walks):
                break
            self.finish(walks, self.begin(walks))
        return [walk.result for walk in walks]

    def around_asks(self, value, axis):
        return [(value, axis, steps) for steps in range(1, self.sizes[axis])]

    def gather_dp_walk(self, value, order):
        for axis in order:
            value = jnp.stack([value] + (yield self.around_asks(value, axis)))
        return value if order == "xz" else value.swapaxes(0, 1)

    def gather_dp(self, value):
        cut = value.shape[1] // 3 // 128 * 128
        walks = [
            Walk(self.gather_dp_walk(value[:, cut:], "zx")),
            Walk(self.gather_dp_walk(value[:, :cut], "xz")),
        ]

        def join():
            long, short = (walk.result for walk in walks)
            return jnp.concatenate([short, long], axis=3).reshape((-1,) + value.shape)

        return walks, join

    def scatter_dp(self, short, long):
        size = self.sizes
        parts = [value.reshape((size["z"], size["x"]) + value.shape[1:]) for value in (short, long)]

        def walk(value, first, second):
            held = yield from self.sum_walk(value, first, bf16)
            return (yield from self.sum_walk(held, second, f32))

        return [Walk(walk(parts[0], "z", "x")), Walk(walk(parts[1].swapaxes(0, 1), "x", "z"))]

    def arrival(self):
        size = self.sizes
        dp = jnp.arange(self.n_dp, dtype=jnp.int32)
        z_back = (self.at["z"] - dp // size["x"]) % size["z"]
        x_back = (self.at["x"] - dp % size["x"]) % size["x"]
        return z_back * size["x"] + x_back

    def orders(self):
        size = self.sizes
        chunk = jnp.arange(CHUNKS, dtype=jnp.int32)
        y, x, z = chunk % size["y"], chunk // size["y"] % size["x"], chunk // size["y"] // size["x"]
        places = []
        for order in stage_orders:
            place = jnp.zeros_like(chunk)
            for axis in reversed(order):
                value = {"x": x, "y": y, "z": z}[axis]
                place = place * size[axis] + (self.at[axis] - value) % size[axis]
            places.append(place)
        chunks = [jnp.sum(jnp.where(p[:, None] == chunk[None, :], chunk[:, None], 0), 0) for p in places]
        flat = jnp.concatenate(chunks + places + [self.at["c"][None]])
        return jnp.pad(flat, (0, 128 - flat.shape[0])).astype(jnp.int32)

    def gather_walk(self, block, order):
        held = block[None]
        for axis in order[:2]:
            held = jnp.concatenate([held] + (yield self.around_asks(held, axis)), axis=0)
        held = jnp.concatenate([held] + (yield self.around_asks(held, order[2])), axis=0)
        others = yield [(held, "c")]
        return [held], others

    def beside(self, *steps):
        walks = [Walk(step) for step in steps]
        while not all(walk.over for walk in walks):
            live = [walk for walk in walks if not walk.over]
            asks = [ask for walk in live for ask in walk.asks]
            got = yield asks
            for walk in live:
                count = len(walk.asks)
                walk.take(got[:count])
                got = got[count:]
        return [walk.result for walk in walks]

    def gather_pair_walk(self, block, cut):
        held = block[None]
        held = jnp.concatenate([held] + (yield self.around_asks(held, "z")), axis=0)

        def rest(held, first, second):
            *near, own = yield self.around_asks(held, first) + [(held, "c")]
            others = [own]
            held = jnp.concatenate([held] + near, axis=0)
            far = yield self.around_asks(held, second)
            others += yield [(value, "c") for value in near + far]
            return [held] + far, others

        return (
            yield from self.beside(
                rest(held[:, :, :cut], "x", "y"), rest(held[:, :, cut:], "y", "x")
            )
        )

    def sum_walk(self, value, axis, kind):
        n = value.shape[0]
        got = yield [(value[steps], axis, n - steps) for steps in range(1, n)]
        return sum((one.astype(f32) for one in got), value[0].astype(f32)).astype(kind)

    def scatter_walk(self, mine, other, order):
        (got,) = yield [(other, "c")]
        held = plus(mine, got)
        for stage, axis in enumerate(reversed(order)):
            value = held.reshape((self.sizes[axis], -1) + held.shape[1:])
            held = yield from self.sum_walk(value, axis, f32 if stage == 2 else bf16)
        return held[0]

    def scatter_pair_walk(self, mine, other, cut):
        (got,) = yield [(other, "c")]

        def first(held, one, two):
            for axis in (one, two):
                value = held.reshape((self.sizes[axis], -1) + held.shape[1:])
                held = yield from self.sum_walk(value, axis, bf16)
            return held

        parts = yield from self.beside(
            first(plus(mine[:, :, :cut], got[:, :, :cut]), "y", "x"),
            first(plus(mine[:, :, cut:], got[:, :, cut:]), "x", "y"),
        )
        held = yield from self.sum_walk(jnp.concatenate(parts, axis=2)[:, None], "z", f32)
        return held[0]


class Walk:
    def __init__(self, steps):
        self.steps, self.over, self.result = steps, False, None
        self.asks = next(steps)

    def tie(self, value):
        value, held = lax.optimization_barrier((value, [ask[0] for ask in self.asks]))
        self.asks = [(new, *ask[1:]) for new, ask in zip(held, self.asks)]
        return value

    def take(self, got):
        try:
            self.asks = self.steps.send(got)
        except StopIteration as end:
            self.over, self.result = True, end.value


def plus(one, two, kind=bf16):
    return (one.astype(f32) + two.astype(f32)).astype(kind)


def join_columns(one, two):
    return jnp.concatenate(lax.optimization_barrier((one, two)), axis=1)


def gather_plain(packs):
    return [([lax.all_gather(pack, both, axis=0, tiled=True)[None]], []) for pack in packs]


def scatter_plain(parts):
    whole = jnp.concatenate([part[0] for part in parts], axis=1)
    whole = lax.psum_scatter(whole, both, scatter_dimension=0, tiled=True).astype(f32)
    ends = [0]
    for part in parts:
        ends.append(ends[-1] + part.shape[2])
    return [whole[:, low:high] for low, high in zip(ends[:-1], ends[1:])]


def shards(
    n_dp,
    n_fsdp,
    decoder_states,
    encodings,
    owner_query,
    buckets,
    gain_self,
    bias_table,
    self_query,
    self_key,
    self_value,
    self_output,
    gain_cross,
    cross_query,
    cross_key,
    cross_value,
    cross_output,
    gain_feed,
    feed_in,
    feed_out,
    cotangent,
):
    n_dev = n_dp * n_fsdp
    wires = Wires(n_dp, n_fsdp)
    chunked = n_dev // 2 == CHUNKS and D % (8 * n_dev) == 0
    chunks = CHUNKS if chunked else 1
    rows = decoder_states.shape[0]
    keys_total = encodings.shape[0]
    slot = keys_total // n_dp
    part = D // n_dev
    bias_part = bias_table.shape[0]
    half = D // 2

    device = lax.axis_index("dp") * n_fsdp + lax.axis_index("fsdp")
    lane = jnp.arange(128, dtype=jnp.int32)
    entry = device * bias_part + jnp.arange(bias_part, dtype=jnp.int32)
    spot = (16 + entry % H)[:, None] == lane[None, :]
    small = jnp.sum(jnp.where(spot, bias_table[:, None].astype(f32), 0.0), axis=0)
    small = jnp.where(jnp.arange(part)[:, None] == 0, small[None, :], 0.0)
    for i, gain in enumerate((gain_self, gain_cross, gain_feed)):
        small = jnp.where(lane[None, :] == i, gain[:, None].astype(f32), small)
    small = small.astype(bf16)

    packs = [
        jnp.concatenate(values, axis=1)
        for values in (
            (self_query, self_key, cross_key),
            (self_value, self_output, cross_value),
            (cross_query, small),
        )
    ]

    def runs(owner_query, buckets):
        owners = owner_query.reshape(n_dp, slot)
        ids = (jnp.arange(n_dp, dtype=jnp.int32) * n_fsdp + lax.axis_index("fsdp")) * QPD
        before = owners[:, None, :] < (ids[:, None] + jnp.arange(QPD + 1, dtype=jnp.int32))[:, :, None]
        bounds = jnp.sum(before.astype(jnp.int32), axis=2)
        return bounds, wires.arrival(), jnp.tile(buckets.T, (1, 4)), orders_of()

    def orders_of():
        return wires.orders() if chunked else jnp.zeros((128,), jnp.int32)

    if chunked:
        walks = [
            Walk(wires.gather_pair_walk(join_columns(*packs[:2]), 3 * D)),
            Walk(wires.gather_walk(packs[2], "xyz")),
        ]
        owner_query, buckets = wires.finish(walks, wires.begin(walks), owner_query, buckets)
        got = wires.begin(walks)
        (places, feed_in, feed_out, cross_output) = wires.finish(
            walks, got, runs(owner_query, buckets), feed_in, feed_out, cross_output
        )
        bounds, arrival, buckets_wide, orders = places
        pair, third = wires.together(walks)
        first_weights = [*pair, third]
    else:
        first_weights = gather_plain(packs)
        bounds, arrival, buckets_wide, orders = runs(owner_query, buckets)
    feed_pack = jnp.concatenate(
        [feed_in[:, t * D : (t + 1) * D] for t in range(4)] + [feed_out, cross_output], axis=0
    )
    feed_pack = lax.all_gather(feed_pack, both, axis=0)
    w_feed_in = feed_pack[:, : 4 * part].reshape(n_dev, 4, part, D).transpose(1, 0, 2, 3)
    w_feed_in = w_feed_in.reshape(4, D, D)
    w_feed_out = feed_pack[:, 4 * part : 8 * part].reshape(4 * D, D)
    w_cross_output = feed_pack[:, 8 * part :].reshape(D, D)

    counts = [(len(mine), len(other)) for mine, other in first_weights]
    pieces = [piece for weight in first_weights for side in weight for piece in side]
    first_widths = [3 * D, 3 * D, D + 128]
    wide = (rows, D)
    (
        normed_self,
        query_self,
        key_self,
        value_self,
        self_mixed,
        first_residual,
        normed_cross,
        query_cross,
        gains,
        bias,
        w_first,
    ) = call(
        functools.partial(self_kernel, counts),
        "self_forward",
        [smem, vmem, vmem] + [hbm] * len(pieces),
        [like(wide)] * 5
        + [like(wide, f32), like(wide), like(wide), like((8, D), f32), like((TGT, H * TGT), f32)]
        + [like((7, D, D))],
        [weights(7, D, D), weights(D, 128)]
        + [weights(min(chunks, 2), chunks, D // (2 * chunks) if chunked else D, w) for w in first_widths]
        + [pltpu.SemaphoreType.DMA((3,)), pltpu.SemaphoreType.DMA((7,))],
        1_500_000_000,
        9_000_000,
        orders,
        decoder_states,
        buckets_wide,
        *pieces,
        out_specs=[vmem] * 10 + [hbm],
    )

    tall = math.gcd(keys_total, 1536)
    steps = keys_total // tall
    block = pl.BlockSpec((tall, D), lambda i: (i, 0))

    def weight_at(i):
        return pl.BlockSpec((1, D, D), lambda step: (i, 0, 0))

    def project(i):
        return call(
            project_kernel,
            "cross_project",
            [block, weight_at(i)],
            like((keys_total, D)),
            [],
            7_300_000_000,
            20_000_000,
            encodings,
            w_first,
            grid=(steps,),
            out_specs=block,
        ).reshape(n_dp, slot, D)

    walks, join = wires.gather_dp(query_cross)
    (key_cross,) = wires.finish(walks, wires.begin(walks), project(5))
    (value_cross,) = wires.finish(walks, wires.begin(walks), project(6))
    all_queries = join()
    parts = cross_mix(bounds, arrival, all_queries, key_cross, value_cross)
    back = lax.all_to_all(parts, "dp", split_axis=0, concat_axis=0)

    (
        layer_output,
        d_send,
        d_second,
        d_branch,
        cross_mixed,
        normed_feed,
        hidden,
        d_pre,
        grad_gain_feed,
    ) = call(
        feed_kernel,
        "feed_both_ways",
        [vmem] * 4 + [hbm] * 3,
        [
            like(wide),
            like((rows, D + 128)),
            like(wide, f32),
            like(wide),
            like(wide),
            like(wide),
            like((4, rows, D)),
            like((4, rows, D)),
            like((1, D), f32),
        ],
        [
            weights(D, D),
            weights(4, D, D),
            weights(4 * D, D),
            pltpu.VMEM((n_dp, rows, D), f32),
            pltpu.SemaphoreType.DMA((3,)),
        ],
        3_000_000_000,
        14_000_000,
        back,
        first_residual,
        cotangent,
        gains,
        w_feed_in,
        w_feed_out,
        w_cross_output,
    )
    blocks = n_dev if part % 8 == 0 else 1
    feed_grad = call(
        feed_grad_kernel,
        "feed_grads",
        [vmem] * 6,
        like((blocks, 9, D // blocks, D)),
        [],
        1_500_000_000,
        14_000_000,
        hidden,
        d_pre,
        normed_feed,
        cross_mixed,
        d_branch,
        cotangent,
    )
    if blocks == 1:
        feed_grad = jnp.concatenate(
            [
                feed_grad[0, :4].reshape(4, n_dev, part, D).transpose(1, 0, 2, 3),
                feed_grad[0, 4:8].reshape(n_dev, 4, part, D),
                feed_grad[0, 8].reshape(n_dev, 1, part, D),
            ],
            axis=1,
        )
    column = jnp.arange(2 * H * TGT, dtype=jnp.int32)
    place = (
        (lane[:, None] // 48 == column[None, :] // (H * TGT))
        & (lane[:, None] % 16 == (column[None, :] // TGT) % H)
    ).astype(bf16)
    walks, join = wires.gather_dp(d_send)
    (feed_grad,) = wires.finish(walks, wires.begin(walks), feed_grad)
    feed_sum = lax.psum_scatter(feed_grad, both, scatter_dimension=0).astype(f32)
    wires.together(walks)
    all_mixed = join()
    short, long, d_key_cross, d_value_cross = cross_grad(
        bounds, arrival, all_queries, all_mixed, place, key_cross, value_cross
    )

    height = D // (2 * chunks) if chunked else D

    def encode_grad(first, count, before=()):
        at = pl.BlockSpec((tall, D), lambda step: (step + first, 0))
        return call(
            encode_grad_kernel,
            "encodings_grad",
            [at, at, weight_at(5), weight_at(6)] + [hbm] * len(before),
            like((keys_total, D)),
            [],
            14_000_000_000 * count // steps,
            30_000_000 * count // steps,
            d_key_cross.reshape(keys_total, D),
            d_value_cross.reshape(keys_total, D),
            w_first,
            w_first,
            *before,
            grid=(count,),
            out_specs=at,
            input_output_aliases={4: 0} if before else {},
        )

    walks = wires.scatter_dp(short, long)
    got = wires.begin(walks)
    key_grads = call(
        functools.partial(weight_grad_kernel, steps),
        "cross_weight_grads",
        [smem, block, block, block],
        [like((chunks, height, 2 * D))] * 2,
        [pltpu.VMEM((2, D, D), f32)],
        14_500_000_000,
        32_000_000,
        orders,
        encodings,
        d_key_cross.reshape(keys_total, D),
        d_value_cross.reshape(keys_total, D),
        grid=(steps,),
        out_specs=[pl.BlockSpec((chunks, height, 2 * D), lambda i: (0, 0, 0))] * 2,
    )
    (key_grads,) = wires.finish(walks, got, key_grads)
    got = wires.begin(walks)
    if chunked:
        key_walk = [Walk(wires.scatter_pair_walk(*key_grads, D))]
        (got,) = wires.finish(key_walk, wires.begin(key_walk), got)
    (encodings_grad,) = wires.finish(walks, got, encode_grad(0, steps // 2))
    d_query_cross = jnp.concatenate([walk.result for walk in walks], axis=1)
    if chunked:
        d_query_cross = key_walk[0].tie(d_query_cross)
        got_key = wires.begin(key_walk)
    decoder_grad, *grads = call(
        self_grad_kernel,
        "self_backward",
        [smem] + [vmem] * 14 + [hbm],
        [
            like(wide),
            *[like((chunks, height, 5 * D + 128))] * 2,
        ],
        [
            weights(5, D, D),
            weights(rows, D),
            weights(rows, D),
            weights(rows, D),
            weights(rows, D),
            pltpu.VMEM((TGT, H * TGT), f32),
            pltpu.SemaphoreType.DMA((5,)),
        ],
        3_000_000_000,
        14_000_000,
        orders,
        d_query_cross,
        d_second,
        first_residual,
        decoder_states,
        normed_cross,
        normed_self,
        query_self,
        key_self,
        value_self,
        self_mixed,
        gains,
        bias,
        buckets_wide,
        grad_gain_feed,
        w_first,
    )

    cut = 2 * D + half + 128
    if chunked:
        (grads,) = wires.finish(key_walk, got_key, grads)
        walks = [Walk(wires.scatter_pair_walk(*grads, cut))]
        every = walks + key_walk
        (encodings_grad,) = wires.finish(every, wires.begin(every), encodings_grad)
        got = wires.begin(every)
        encodings_grad = encode_grad(steps // 2, steps - steps // 2, (encodings_grad,))
        (encodings_grad,) = wires.finish(every, got, encodings_grad)
        wires.together(every, 1)
        (feed_sum,) = wires.finish(every, wires.begin(every), feed_sum)
        first_sum, key_sum = walks[0].result, key_walk[0].result
    else:
        first_sum, key_sum = scatter_plain([grads[0], key_grads[0]])
        encodings_grad = encode_grad(steps // 2, steps - steps // 2, (encodings_grad,))

    small_sum = first_sum[:, cut - 128 : cut]
    bias_sum = jnp.sum(jnp.where(spot, small_sum[:1], 0.0), axis=1)
    return (
        layer_output,
        decoder_grad,
        encodings_grad,
        small_sum[:, 0],
        bias_sum,
        first_sum[:, :D],
        first_sum[:, D : 2 * D],
        first_sum[:, cut : cut + D],
        first_sum[:, cut + D : cut + 2 * D],
        small_sum[:, 1],
        jnp.concatenate([first_sum[:, 2 * D : 2 * D + half], first_sum[:, cut + 2 * D :]], axis=1),
        key_sum[:, :D],
        key_sum[:, D:],
        feed_sum[8],
        small_sum[:, 2],
        jnp.concatenate([feed_sum[t] for t in range(4)], axis=1),
        feed_sum[4:8].reshape(4 * part, D),
    )


def solution(mesh):
    rows = P(both, None)
    flat = P(both)
    in_specs = (rows, rows, flat, P(), flat, flat, rows, rows, rows, rows)
    in_specs += (flat, rows, rows, rows, rows, flat, rows, rows, rows)
    out_specs = (rows, rows, rows, flat, flat, rows, rows, rows, rows)
    out_specs += (flat, rows, rows, rows, rows, flat, rows, rows)
    return jax.shard_map(
        functools.partial(shards, mesh.shape["dp"], mesh.shape["fsdp"]),
        mesh=mesh,
        in_specs=in_specs,
        out_specs=out_specs,
        check_vma=False,
    )
```

```python
import functools
import math

import jax
import jax.numpy as jnp
from jax import lax
from jax.experimental import pallas as pl
from jax.experimental.pallas import tpu as pltpu
from jax.sharding import PartitionSpec as P

D = 768
H = 12
DH = 64
NB = 32
TGT = 32
QPD = 4
GROUPS = 3
TILE = 256
CHUNKS = 16
stage_orders = ("zxy", "zyx", "xyz")

epsilon = 1e-06
masked_score = -1e30
both = ("dp", "fsdp")
bf16 = jnp.bfloat16
f32 = jnp.float32


def matmul(left_side, right_side):
    return jnp.dot(left_side, right_side, preferred_element_type=f32)


def dot_tn(left_side, right_side):
    return lax.dot_general(
        left_side, right_side, (((0,), (0,)), ((), ())), preferred_element_type=f32
    )


def dot_nt(left_side, right_side):
    return lax.dot_general(
        left_side, right_side, (((1,), (1,)), ((), ())), preferred_element_type=f32
    )


def rms_norm(values, gain_vector):
    return (
        values
        * lax.rsqrt(jnp.mean(values * values, axis=-1, keepdims=True) + epsilon)
        * gain_vector
    )


def pieces_of(values):
    high = values.astype(bf16)
    rest = values - high.astype(f32)
    mid = rest.astype(bf16)
    low = (rest - mid.astype(f32)).astype(bf16)
    return high, mid, low


def split_pieces(values):
    high = lax.reduce_precision(values, 8, 7)
    mid = lax.reduce_precision(values - high, 8, 7)
    low = values - high - mid
    return high.astype(bf16), mid.astype(bf16), low.astype(bf16)


def spread_heads(rows):
    tall = jnp.concatenate([rows, rows, rows, rows], axis=0)
    head_row = lax.broadcasted_iota(jnp.int32, (4 * TGT, 4 * DH), 0) // TGT
    head_col = lax.broadcasted_iota(jnp.int32, (4 * TGT, 4 * DH), 1) // DH
    return jnp.where(head_row == head_col, tall, jnp.zeros_like(tall))


def gather_heads(tall):
    head_col = lax.broadcasted_iota(jnp.int32, (TGT, 4 * DH), 1) // DH
    rows = jnp.zeros((TGT, 4 * DH), f32)
    for head in range(4):
        rows = jnp.where(head_col == head, tall[head * TGT : (head + 1) * TGT], rows)
    return rows


def run_tiles(bounds_ref, block, query, slot):
    start = bounds_ref[block, query]
    end = bounds_ref[block, query + 1]
    first = (start // 16) * 16
    count = (end - first + TILE - 1) // TILE
    return start, end, first, count


def tile_rows(first, step, start, end, slot):
    want = first + step * TILE
    base = pl.multiple_of(jnp.minimum(want, slot - TILE), 16)
    rows = base + lax.broadcasted_iota(jnp.int32, (TILE, 4 * TGT), 0)
    inside = (rows >= jnp.maximum(start, want)) & (rows < end)
    return base, inside


def column_of(row):
    return jnp.transpose(jnp.broadcast_to(row, (8, 4 * TGT)))[:, :1]


def group_of(short_ref, long_ref, query, g):
    rows_of = slice(query * TGT, (query + 1) * TGT)
    if g == 0:
        return short_ref[0, rows_of, :]
    return long_ref[0, rows_of, (g - 1) * 256 : g * 256]


def mix_kernel(slot, bounds_ref, order_ref, short_ref, long_ref, k_ref, v_ref, o_ref, score_ref, mix_ref):
    block = pl.program_id(0)
    lane = lax.broadcasted_iota(jnp.int32, (TGT, 128), 1)
    runs = [run_tiles(bounds_ref, block, query, slot) for query in range(QPD)]
    pairs = [(query, g) for query in range(QPD) for g in range(GROUPS)]
    spread = {
        (query, g): spread_heads(group_of(short_ref, long_ref, query, g))
        for query, g in pairs
    }

    def score_step(step, some, tops):
        held = pl.ds(pl.multiple_of(step * TILE, TILE), TILE)
        new_tops = []
        for top, (query, g) in zip(tops, some):
            start, end, first, count = runs[query]
            base, inside = tile_rows(first, step, start, end, slot)
            keys = k_ref[0, pl.ds(base, TILE), g * 256 : (g + 1) * 256]
            scores = jnp.where(inside, dot_nt(keys, spread[query, g]), masked_score)
            score_ref[query * GROUPS + g, held, :] = scores
            new_tops.append(jnp.maximum(top, jnp.max(scores, axis=0, keepdims=True)))
        return tuple(new_tops)

    def mix_step(step, some, tops, sums):
        held = pl.ds(pl.multiple_of(step * TILE, TILE), TILE)
        new_sums, raised = [], []
        for total, top, (query, g) in zip(sums, tops, some):
            weights = jnp.exp(score_ref[query * GROUPS + g, held, :] - top)
            new_sums.append(total + jnp.sum(weights, axis=0, keepdims=True))
            raised.append(weights.astype(bf16))
        for weights, (query, g) in zip(raised, some):
            start, end, first, count = runs[query]
            base = tile_rows(first, step, start, end, slot)[0]
            values = v_ref[0, pl.ds(base, TILE), g * 256 : (g + 1) * 256]
            mix_ref[query * GROUPS + g] += dot_tn(weights, values)
        return tuple(new_sums)

    def of_query(query):
        return slice(query * GROUPS, (query + 1) * GROUPS)

    tops = score_step(0, pairs, [jnp.full((1, 4 * TGT), masked_score, f32) for pair in pairs])
    all_tops = []
    for query in range(QPD):
        all_tops += lax.fori_loop(
            1,
            runs[query][3],
            lambda step, tops, some=pairs[of_query(query)]: score_step(step, some, tops),
            tops[of_query(query)],
        )
    tops = tuple(all_tops)
    mix_ref[...] = jnp.zeros_like(mix_ref)
    sums = mix_step(0, pairs, tops, [jnp.zeros((1, 4 * TGT), f32) for pair in pairs])
    all_sums = []
    for query in range(QPD):
        mine = of_query(query)
        all_sums += lax.fori_loop(
            1,
            runs[query][3],
            lambda step, sums, mine=mine: mix_step(step, pairs[mine], tops[mine], sums),
            sums[mine],
        )
    sums = tuple(all_sums)
    total, top = jnp.concatenate(sums, axis=0), jnp.concatenate(tops, axis=0)
    scales = jnp.transpose(1.0 / total)
    log_sums = jnp.transpose(top + jnp.log(total))
    for query in range(QPD):
        rows_of = slice(query * TGT, (query + 1) * TGT)
        logs = jnp.zeros((TGT, 128), f32)
        for g in range(GROUPS):
            i = query * GROUPS + g
            scale = scales[:, i : i + 1]
            log_sum = log_sums[:, i : i + 1]
            o_ref[0, rows_of, g * 256 : (g + 1) * 256] = gather_heads(mix_ref[i] * scale).astype(
                bf16
            )
            for head in range(4):
                logs = jnp.where(
                    (lane % 16 == g * 4 + head) & (lane < 48),
                    log_sum[head * TGT : (head + 1) * TGT],
                    logs,
                )
        high, mid, low = pieces_of(logs)
        o_ref[0, rows_of, D:] = jnp.where(
            lane < 16, high.astype(f32), jnp.where(lane < 32, mid.astype(f32), low.astype(f32))
        ).astype(bf16)


def grad_kernel(
    slot,
    bounds_ref,
    order_ref,
    q_short_ref,
    q_long_ref,
    m_short_ref,
    m_long_ref,
    place_ref,
    k_ref,
    v_ref,
    short_ref,
    long_ref,
    dk_ref,
    dv_ref,
    sum_ref,
):
    block = pl.program_id(0)
    dk_ref[...] = jnp.zeros_like(dk_ref)
    dv_ref[...] = jnp.zeros_like(dv_ref)
    sum_ref[...] = jnp.zeros_like(sum_ref)
    runs = [run_tiles(bounds_ref, block, query, slot) for query in range(QPD)]
    pairs = [(query, g) for query in range(QPD) for g in range(GROUPS)]
    row = lax.broadcasted_iota(jnp.int32, (TGT, 2 * H * TGT), 0)
    target = lax.broadcasted_iota(jnp.int32, (TGT, 2 * H * TGT), 1) % TGT
    spread, spread_m, logs, deltas = {}, {}, {}, {}
    for query in range(QPD):
        rows_of = slice(query * TGT, (query + 1) * TGT)
        placed = matmul(m_long_ref[0, rows_of, 512:], place_ref[...])
        flat = jnp.sum(jnp.where(row == target, placed, 0.0), axis=0, keepdims=True)
        for g in range(GROUPS):
            spread[query, g] = spread_heads(group_of(q_short_ref, q_long_ref, query, g))
            spread_m[query, g] = spread_heads(group_of(m_short_ref, m_long_ref, query, g))
            logs[query, g] = flat[:, g * 128 : (g + 1) * 128]
            deltas[query, g] = flat[:, (GROUPS + g) * 128 : (GROUPS + g + 1) * 128]

    def step_of(step, some):
        places = {}
        for query in sorted({query for query, g in some}):
            start, end, first, count = runs[query]
            places[query] = tile_rows(first, step, start, end, slot)
        softs, changes = [], []
        for query, g in some:
            base, inside = places[query]
            columns = slice(g * 256, (g + 1) * 256)
            scores = dot_nt(k_ref[0, pl.ds(base, TILE), columns], spread[query, g])
            soft = jnp.where(inside, jnp.exp(scores - logs[query, g]), 0.0)
            d_soft = dot_nt(v_ref[0, pl.ds(base, TILE), columns], spread_m[query, g])
            changes.append((soft * (d_soft - deltas[query, g])).astype(bf16))
            softs.append(soft.astype(bf16))
        for change, (query, g) in zip(changes, some):
            keys = k_ref[0, pl.ds(places[query][0], TILE), g * 256 : (g + 1) * 256]
            sum_ref[query * GROUPS + g] += dot_tn(change, keys)
        for soft, change, (query, g) in zip(softs, changes, some):
            rows_of, columns = pl.ds(places[query][0], TILE), slice(g * 256, (g + 1) * 256)
            dk_ref[0, rows_of, columns] += matmul(change, spread[query, g]).astype(bf16)
            dv_ref[0, rows_of, columns] += matmul(soft, spread_m[query, g]).astype(bf16)

    step_of(0, pairs)
    for query in range(QPD):

        def one_query(step, carry, some=pairs[query * GROUPS : (query + 1) * GROUPS]):
            step_of(step, some)
            return carry

        lax.fori_loop(1, runs[query][3], one_query, 0)
    for query in range(QPD):
        rows_of = slice(query * TGT, (query + 1) * TGT)
        d_query = jnp.concatenate(
            [gather_heads(sum_ref[query * GROUPS + g]) for g in range(GROUPS)], axis=1
        )
        short_ref[0, rows_of, :] = d_query[:, : D // 3].astype(bf16)
        long_ref[0, rows_of, :] = d_query[:, D // 3 :].astype(bf16)


def cross_mix(bounds, arrival, queries, keys, values):
    blocks, slot = keys.shape[0], keys.shape[1]
    rows = queries[0].shape[1]
    at = lambda i, *refs: (i, 0, 0)
    short = lambda i, bounds_ref, order_ref: (order_ref[0, i], 0, 0)
    long = lambda i, bounds_ref, order_ref: (order_ref[1, i], 0, 0)
    return pl.pallas_call(
        functools.partial(mix_kernel, slot),
        grid_spec=pltpu.PrefetchScalarGridSpec(
            num_scalar_prefetch=2,
            grid=(blocks,),
            in_specs=[
                pl.BlockSpec((1, rows, D // 3), short),
                pl.BlockSpec((1, rows, D - D // 3), long),
                pl.BlockSpec((1, slot, D), at),
                pl.BlockSpec((1, slot, D), at),
            ],
            out_specs=[pl.BlockSpec((1, rows, D + 128), at)],
            scratch_shapes=[
                pltpu.VMEM((QPD * GROUPS, slot + TILE, 4 * TGT), f32),
                pltpu.VMEM((QPD * GROUPS, 4 * TGT, 256), f32),
            ],
        ),
        out_shape=[
            jax.ShapeDtypeStruct((blocks, rows, D + 128), bf16),
        ],
        compiler_params=pltpu.CompilerParams(vmem_limit_bytes=60 * 1024 * 1024),
        cost_estimate=pl.CostEstimate(
            flops=12_000_000_000, bytes_accessed=22_000_000, transcendentals=4_000_000
        ),
        name="cross_mix",
    )(bounds, arrival, *queries, keys, values)[0]


def cross_grad(bounds, arrival, queries, mixed, place, keys, values):
    blocks, slot = keys.shape[0], keys.shape[1]
    rows = queries[0].shape[1]
    at = lambda i, *refs: (i, 0, 0)
    short = lambda i, bounds_ref, order_ref: (order_ref[0, i], 0, 0)
    long = lambda i, bounds_ref, order_ref: (order_ref[1, i], 0, 0)
    return pl.pallas_call(
        functools.partial(grad_kernel, slot),
        grid_spec=pltpu.PrefetchScalarGridSpec(
            num_scalar_prefetch=2,
            grid=(blocks,),
            in_specs=[
                pl.BlockSpec((1, rows, D // 3), short),
                pl.BlockSpec((1, rows, D - D // 3), long),
                pl.BlockSpec((1, rows, D // 3), short),
                pl.BlockSpec((1, rows, D - D // 3 + 128), long),
                pl.BlockSpec((128, 2 * H * TGT), lambda i, *refs: (0, 0)),
                pl.BlockSpec((1, slot, D), at),
                pl.BlockSpec((1, slot, D), at),
            ],
            out_specs=[
                pl.BlockSpec((1, rows, D // 3), short),
                pl.BlockSpec((1, rows, D - D // 3), long),
                pl.BlockSpec((1, slot, D), at),
                pl.BlockSpec((1, slot, D), at),
            ],
            scratch_shapes=[pltpu.VMEM((QPD * GROUPS, 4 * TGT, 256), f32)],
        ),
        out_shape=[
            jax.ShapeDtypeStruct((blocks, rows, D // 3), bf16),
            jax.ShapeDtypeStruct((blocks, rows, D - D // 3), bf16),
            jax.ShapeDtypeStruct((blocks, slot, D), bf16),
            jax.ShapeDtypeStruct((blocks, slot, D), bf16),
        ],
        compiler_params=pltpu.CompilerParams(vmem_limit_bytes=60 * 1024 * 1024),
        cost_estimate=pl.CostEstimate(
            flops=24_000_000_000, bytes_accessed=42_000_000, transcendentals=4_000_000
        ),
        name="cross_grad",
    )(bounds, arrival, *queries, *mixed, place, keys, values)


def flag_of(orders_ref):
    return orders_ref[6 * CHUNKS]


def start_load(orders_ref, mine, other, stage, sem, columns=slice(None)):
    flag = flag_of(orders_ref)
    for core, sources in ((flag, mine), (1 - flag, other)):
        place = 0
        for source in sources:
            count = source.shape[0]
            pltpu.make_async_copy(
                source.at[:, :, columns], stage.at[core, pl.ds(place, count)], sem
            ).start()
            place += count


def wait_load(into, sem):
    pltpu.make_async_copy(into, into, sem).wait()


def assemble(orders_ref, order, stage, columns, into):
    if stage.shape[1] == 1:
        into[...] = stage[0, 0, :, columns]
        return
    rows = 2 * stage.shape[2]
    for i in range(stage.shape[1]):
        base = pl.multiple_of(orders_ref[order * CHUNKS + i] * rows, 16)
        into[pl.ds(base, rows), :] = jnp.concatenate(
            [stage[0, i, :, columns], stage[1, i, :, columns]], axis=0
        )


def store_grad(orders_ref, order, grad, mine_ref, other_ref, columns):
    chunks, rows = mine_ref.shape[0], mine_ref.shape[1]
    if chunks == 1:
        mine_ref[0, :, columns] = grad[...].astype(bf16)
        return
    first = flag_of(orders_ref) == 0
    for i in range(chunks):
        to = orders_ref[(3 + order) * CHUNKS + i]
        low = grad[2 * i * rows : (2 * i + 1) * rows, :]
        high = grad[(2 * i + 1) * rows : (2 * i + 2) * rows, :]
        mine_ref[to, :, columns] = jnp.where(first, low, high).astype(bf16)
        other_ref[to, :, columns] = jnp.where(first, high, low).astype(bf16)


def iota(shape, axis):
    return lax.broadcasted_iota(jnp.int32, shape, axis)


def project_kernel(order, count, orders_ref, enc_ref, *refs):
    pieces, (out_ref, w_ref, stage, sem) = refs[:-4], refs[-4:]

    @pl.when(pl.program_id(0) == 0)
    def load():
        mine, other = pieces[:count], pieces[count:]
        start_load(orders_ref, mine, other, stage, sem.at[0], slice(2 * D, 3 * D))
        wait_load(stage, sem.at[0])
        assemble(orders_ref, order, stage, slice(0, D), w_ref)

    out_ref[...] = matmul(enc_ref[...], w_ref[...]).astype(bf16)


def encode_grad_kernel(dk_ref, dv_ref, wk_ref, wv_ref, *refs):
    out_ref = refs[-1]
    out_ref[...] = (dot_nt(dk_ref[...], wk_ref[...]) + dot_nt(dv_ref[...], wv_ref[...])).astype(bf16)


def weight_grad_kernel(steps, orders_ref, enc_ref, dk_ref, dv_ref, mine_ref, other_ref, sum_ref):
    step = pl.program_id(0)
    rows = enc_ref[...]
    products = [dot_tn(rows, dk_ref[...]), dot_tn(rows, dv_ref[...])]

    @pl.when(step == 0)
    def first():
        for i in range(2):
            sum_ref[i] = products[i]

    @pl.when(step > 0)
    def later():
        for i in range(2):
            sum_ref[i] += products[i]

    @pl.when(step == steps - 1)
    def store():
        for i in range(2):
            columns = slice(i * D, (i + 1) * D)
            store_grad(orders_ref, i, sum_ref.at[i], mine_ref, other_ref, columns)


def soft_columns(scores):
    raised = jnp.exp(scores - jnp.max(scores, axis=0, keepdims=True))
    return raised / jnp.sum(raised, axis=0, keepdims=True)


def self_kernel(counts, orders_ref, states_ref, buckets_ref, *refs):
    refs = list(refs)
    pieces = []
    for mine, other in counts:
        pieces.append((refs[:mine], refs[mine : mine + other]))
        refs = refs[mine + other :]
    normed_ref, q_ref, k_ref, v_ref, mixed_ref, first_ref, normed_cross_ref = refs[:7]
    short_ref, long_ref, gains_ref, bias_ref, out_ref, w_ref, small_ref = refs[7:14]
    stages, sems, out_sems = refs[14:17], refs[17], refs[18]
    for order in (2, 0, 1):
        start_load(orders_ref, *pieces[order], stages[order], sems.at[order])

    def put(weight, order, place):
        assemble(
            orders_ref, order, stages[order], slice(place * D, (place + 1) * D), w_ref.at[weight]
        )
        pltpu.make_async_copy(w_ref.at[weight], out_ref.at[weight], out_sems.at[weight]).start()

    wait_load(stages[2], sems.at[2])
    assemble(orders_ref, 2, stages[2], slice(D, D + 128), small_ref)
    small = small_ref[...]
    gains_ref[...] = jnp.transpose(small.astype(f32))[:8]
    span = D // NB
    first_row, row = span * iota((NB, D), 0), iota((NB, D), 1)
    pick = ((row >= first_row) & (row < first_row + span)).astype(f32).astype(bf16)
    table = matmul(pick, small).astype(bf16)
    wide = (iota((128, H * TGT), 0) == 16 + (iota((128, H * TGT), 1) >> 5)).astype(f32).astype(bf16)
    table = matmul(table, wide)
    buckets = buckets_ref[...]
    later = iota((TGT, 128), 0) > (iota((TGT, 128), 1) & (TGT - 1))
    for g in range(GROUPS):
        bias = jnp.zeros((TGT, 128), f32)
        for n in range(NB):
            bias = jnp.where(buckets == n, table[n : n + 1, g * 128 : (g + 1) * 128], bias)
        bias_ref[:, g * 128 : (g + 1) * 128] = jnp.where(later, masked_score, bias)

    states = states_ref[...].astype(f32)
    normed = rms_norm(states, gains_ref[0:1]).astype(bf16)
    normed_ref[...] = normed
    wait_load(stages[0], sems.at[0])
    put(0, 0, 0)
    q_ref[...] = matmul(normed, w_ref[0]).astype(bf16)
    put(1, 0, 1)
    k_ref[...] = matmul(normed, w_ref[1]).astype(bf16)
    wait_load(stages[1], sems.at[1])
    put(2, 1, 0)
    v_ref[...] = matmul(normed, w_ref[2]).astype(bf16)
    places = [
        (slice(query * TGT, (query + 1) * TGT), slice(g * 256, (g + 1) * 256), g)
        for query in range(QPD)
        for g in range(GROUPS)
    ]
    scores = [
        dot_nt(k_ref[rows_of, columns], spread_heads(q_ref[rows_of, columns]))
        + bias_ref[:, g * 128 : (g + 1) * 128]
        for rows_of, columns, g in places
    ]
    softs = [soft_columns(score).astype(bf16) for score in scores]
    talls = [
        dot_tn(soft, v_ref[rows_of, columns]) for soft, (rows_of, columns, g) in zip(softs, places)
    ]
    for tall, (rows_of, columns, g) in zip(talls, places):
        mixed_ref[rows_of, columns] = gather_heads(tall).astype(bf16)
    put(3, 1, 1)
    first = states + matmul(mixed_ref[...], w_ref[3])
    first_ref[...] = first
    normed_cross = rms_norm(first, gains_ref[1:2]).astype(bf16)
    normed_cross_ref[...] = normed_cross
    put(4, 2, 0)
    query_cross = matmul(normed_cross, w_ref[4]).astype(bf16)
    short_ref[...] = query_cross[:, : D // 3]
    long_ref[...] = query_cross[:, D // 3 :]
    for weight in range(5):
        pltpu.make_async_copy(w_ref.at[weight], out_ref.at[weight], out_sems.at[weight]).wait()


def exact_sum(values, picks):
    high, mid, low = pieces_of(values)
    return matmul(high, picks) + matmul(mid, picks) + matmul(low, picks)


def norm_back(values, gain, d_normed):
    scale = lax.rsqrt(jnp.mean(values * values, axis=-1, keepdims=True) + epsilon)
    scaled = d_normed * gain
    inner = jnp.mean(scaled * values, axis=-1, keepdims=True)
    d_values = scale * scaled - values * (scale * scale * scale * inner)
    d_gain = jnp.sum(d_normed * values * scale, axis=0, keepdims=True)
    return d_values, d_gain


def feed_kernel(
    back_ref,
    first_ref,
    cot_ref,
    gains_ref,
    fi_ref,
    fo_ref,
    co_ref,
    out_ref,
    short_ref,
    long_ref,
    second_ref,
    branch_ref,
    mixed_ref,
    normed_ref,
    hidden_ref,
    pre_ref,
    gain_ref,
    wc_ref,
    wi_ref,
    wo_ref,
    logs_ref,
    sems,
):
    blocks, rows = back_ref.shape[0], back_ref.shape[1]
    copies = [
        pltpu.make_async_copy(source, into, sems.at[i])
        for i, (source, into) in enumerate(((co_ref, wc_ref), (fi_ref, wi_ref), (fo_ref, wo_ref)))
    ]
    for copy in copies:
        copy.start()
    widen = ((iota((128, D), 0) & 15) == (iota((128, D), 1) >> 6)) & (iota((128, D), 0) < 48)
    widen = widen.astype(f32).astype(bf16)

    def log_step(i, top):
        logs = matmul(back_ref[i, :, D:], widen)
        logs_ref[i] = logs
        return jnp.maximum(top, logs)

    top = lax.fori_loop(0, blocks, log_step, jnp.full((rows, D), masked_score, f32))

    def share_step(i, carry):
        total, mixed = carry
        share = jnp.exp(logs_ref[i] - top)
        return total + share, mixed + share * back_ref[i, :, :D].astype(f32)

    zero = jnp.zeros((rows, D), f32)
    total, mixed = lax.fori_loop(0, blocks, share_step, (zero, zero))
    mixed = mixed / total
    logs = top + jnp.log(total)
    mixed_ref[...] = mixed.astype(bf16)
    copies[0].wait()
    second = first_ref[...] + matmul(mixed_ref[...], wc_ref[...])
    normed = rms_norm(second, gains_ref[2:3]).astype(bf16)
    normed_ref[...] = normed
    copies[1].wait()
    copies[2].wait()
    cot = cot_ref[...]
    root = 0.7978845608028654

    def feed_step(t, carry):
        out, d_normed = carry
        pre = matmul(normed, wi_ref[t])
        w_out = wo_ref[t * D : (t + 1) * D, :]
        bent = jnp.tanh(root * (pre + 0.044715 * pre * pre * pre))
        hidden = (0.5 * pre * (1.0 + bent)).astype(bf16)
        slope = 0.5 * (1.0 + bent) + 0.5 * pre * (1.0 - bent * bent) * (
            root * (1.0 + 3 * 0.044715 * pre * pre)
        )
        d_pre = (dot_nt(cot, w_out) * slope).astype(bf16)
        hidden_ref[t] = hidden
        pre_ref[t] = d_pre
        return out + matmul(hidden, w_out), d_normed + dot_nt(d_pre, wi_ref[t])

    out, d_normed = zero, zero
    for t in range(4):
        out, d_normed = feed_step(t, (out, d_normed))
    out_ref[...] = (second + out).astype(bf16)
    d_values, gain_ref[...] = norm_back(second, gains_ref[2:3], d_normed)
    d_second = cot.astype(f32) + d_values
    second_ref[...] = d_second
    branch_ref[...] = d_second.astype(bf16)
    d_mixed = dot_nt(branch_ref[...], wc_ref[...]).astype(bf16)
    short_ref[...] = d_mixed[:, : D // 3]
    long_ref[:, : D - D // 3] = d_mixed[:, D // 3 :]
    lane = iota((D, 128), 1)
    row = iota((D, 128), 0)
    pick = ((row == (lane & 15) * DH) & (lane < 48)).astype(f32).astype(bf16)
    add = (((row >> 6) == (lane & 15)) & (lane >= 48) & (lane < 96)).astype(f32).astype(bf16)
    extra = exact_sum(logs, pick) + exact_sum(d_mixed.astype(f32) * mixed, add)
    high, mid, low = pieces_of(extra)
    slot_of = iota((rows, 128), 1) >> 4
    slot_of = jnp.where(slot_of >= 3, slot_of - 3, slot_of)
    long_ref[:, D - D // 3 :] = jnp.where(
        slot_of == 0, high.astype(f32), jnp.where(slot_of == 1, mid.astype(f32), low.astype(f32))
    ).astype(bf16)


def feed_grad_kernel(hidden_ref, pre_ref, normed_ref, mixed_ref, branch_ref, cot_ref, out_ref):
    blocks, slabs, part, width = out_ref.shape

    def put(grad, block, slab, row):
        out_ref[block, slab] = grad[row : row + part].astype(bf16)

    for t in range(4):
        grad = dot_tn(normed_ref[...], pre_ref[t])
        for i in range(blocks):
            put(grad, i, t, i * part)
        grad = dot_tn(hidden_ref[t], cot_ref[...])
        for i in range(blocks):
            place = t * blocks + i
            put(grad, place // 4, 4 + place % 4, i * part)
    grad = dot_tn(mixed_ref[...], branch_ref[...])
    for i in range(blocks):
        put(grad, i, 8, i * part)


def self_grad_kernel(
    orders_ref,
    back_ref,
    second_ref,
    first_ref,
    states_ref,
    normed_cross_ref,
    normed_ref,
    q_ref,
    k_ref,
    v_ref,
    mixed_ref,
    gains_ref,
    bias_ref,
    buckets_ref,
    gain_feed_ref,
    *refs,
):
    weights_ref, out_ref, ga_ref, ha_ref, w_ref, dq_ref, dk_ref, dv_ref, dm_ref, sums_ref, sems = refs
    half = D // 2
    last = ga_ref.shape[2]
    cut = 2 * D + half + 128
    for i in (4, 3, 0, 1, 2):
        pltpu.make_async_copy(weights_ref.at[i], w_ref.at[i], sems.at[i]).start()

    d_query = back_ref[...].astype(bf16)
    grad = dot_tn(normed_cross_ref[...], d_query)
    store_grad(orders_ref, 0, grad[:, :half], ga_ref, ha_ref, slice(2 * D, 2 * D + half))
    store_grad(orders_ref, 1, grad[:, half:], ga_ref, ha_ref, slice(last - half, last))
    wait_load(w_ref.at[4], sems.at[4])
    d_values, gain_cross = norm_back(first_ref[...], gains_ref[1:2], dot_nt(d_query, w_ref[4]))
    d_first = second_ref[...] + d_values
    branch = d_first.astype(bf16)
    store_grad(orders_ref, 1, dot_tn(mixed_ref[...], branch), ga_ref, ha_ref, slice(cut + D, cut + 2 * D))
    wait_load(w_ref.at[3], sems.at[3])
    dm_ref[...] = dot_nt(branch, w_ref[3]).astype(bf16)
    places = [
        (slice(query * TGT, (query + 1) * TGT), slice(g * 256, (g + 1) * 256), g)
        for query in range(QPD)
        for g in range(GROUPS)
    ]
    spreads = [spread_heads(q_ref[rows_of, columns]) for rows_of, columns, g in places]
    spreads_m = [spread_heads(dm_ref[rows_of, columns]) for rows_of, columns, g in places]
    scores = [
        dot_nt(k_ref[rows_of, columns], spread) + bias_ref[:, g * 128 : (g + 1) * 128]
        for spread, (rows_of, columns, g) in zip(spreads, places)
    ]
    d_softs = [
        dot_nt(v_ref[rows_of, columns], spread)
        for spread, (rows_of, columns, g) in zip(spreads_m, places)
    ]
    softs = [soft_columns(score) for score in scores]
    changes = []
    for soft, d_soft in zip(softs, d_softs):
        delta = jnp.sum(soft * d_soft, axis=0, keepdims=True)
        changes.append((soft * (d_soft - delta)).astype(bf16))
    for g in range(GROUPS):
        mine = [change.astype(f32) for change, place in zip(changes, places) if place[2] == g]
        sums_ref[:, g * 128 : (g + 1) * 128] = functools.reduce(jnp.add, mine)
    for change, (rows_of, columns, g) in zip(changes, places):
        d_rows = gather_heads(dot_tn(change, k_ref[rows_of, columns]))
        dq_ref[rows_of, columns] = d_rows.astype(bf16)
    for change, spread, (rows_of, columns, g) in zip(changes, spreads, places):
        dk_ref[rows_of, columns] = matmul(change, spread).astype(bf16)
    for soft, spread, (rows_of, columns, g) in zip(softs, spreads_m, places):
        dv_ref[rows_of, columns] = matmul(soft.astype(bf16), spread).astype(bf16)
    normed = normed_ref[...]
    store_grad(orders_ref, 0, dot_tn(normed, dq_ref[...]), ga_ref, ha_ref, slice(0, D))
    store_grad(orders_ref, 0, dot_tn(normed, dk_ref[...]), ga_ref, ha_ref, slice(D, 2 * D))
    store_grad(orders_ref, 1, dot_tn(normed, dv_ref[...]), ga_ref, ha_ref, slice(cut, cut + D))
    wait_load(w_ref.at[0], sems.at[0])
    wait_load(w_ref.at[1], sems.at[1])
    wait_load(w_ref.at[2], sems.at[2])
    d_normed = (
        dot_nt(dq_ref[...], w_ref[0]) + dot_nt(dk_ref[...], w_ref[1]) + dot_nt(dv_ref[...], w_ref[2])
    )
    d_values, gain_self = norm_back(states_ref[...].astype(f32), gains_ref[0:1], d_normed)
    out_ref[...] = (d_first + d_values).astype(bf16)
    buckets = buckets_ref[...]
    by_bucket = []
    for n in range(NB):
        sums = []
        for g in range(GROUPS):
            mine = jnp.where(buckets == n, sums_ref[:, g * 128 : (g + 1) * 128], 0.0)
            sums.append(jnp.sum(mine, axis=0, keepdims=True))
        by_bucket.append(jnp.concatenate(sums, axis=1))
    by_bucket = jnp.concatenate(by_bucket, axis=0)
    lane = iota((H * TGT, 128), 1)
    narrow = ((iota((H * TGT, 128), 0) >> 5) == lane - 16).astype(f32).astype(bf16)
    table = exact_sum(by_bucket, narrow).astype(bf16)
    span = D // NB
    first_row, row = span * iota((D, NB), 1), iota((D, NB), 0)
    put = ((row >= first_row) & (row < first_row + span)).astype(f32).astype(bf16)
    gains = jnp.concatenate([gain_self, gain_cross, gain_feed_ref[...], jnp.zeros((125, D), f32)])
    small = matmul(put, table) + jnp.transpose(gains)
    store_grad(orders_ref, 0, small, ga_ref, ha_ref, slice(cut - 128, cut))


hbm = pl.BlockSpec(memory_space=pl.ANY)
vmem = pl.BlockSpec(memory_space=pltpu.VMEM)
smem = pl.BlockSpec(memory_space=pltpu.SMEM)


def like(shape, kind=bf16):
    return jax.ShapeDtypeStruct(shape, kind)


def call(kernel, name, ins, outs, scratch, flops, moved, *values, **more):
    return pl.pallas_call(
        kernel,
        in_specs=ins,
        out_shape=outs,
        scratch_shapes=scratch,
        compiler_params=pltpu.CompilerParams(vmem_limit_bytes=60 * 1024 * 1024),
        cost_estimate=pl.CostEstimate(flops=flops, bytes_accessed=moved, transcendentals=0),
        name=name,
        **more,
    )(*values)


def weights(*shape):
    return pltpu.VMEM(shape, bf16)


class Wires:
    def __init__(self, n_dp, n_fsdp):
        self.n_dp, self.n_fsdp = n_dp, n_fsdp
        self.sizes = {"x": n_fsdp // 2, "y": n_fsdp // 2, "z": n_dp // (n_fsdp // 2), "c": 2}
        dp, fsdp = lax.axis_index("dp"), lax.axis_index("fsdp")
        size = self.sizes
        self.at = {"z": dp // size["x"], "x": dp % size["x"], "y": fsdp // 2, "c": fsdp % 2}

    def shift(self, value, axis, steps=1):
        size = self.sizes
        pairs = []
        for dp in range(self.n_dp):
            for fsdp in range(self.n_fsdp):
                at = {"z": dp // size["x"], "x": dp % size["x"], "y": fsdp // 2, "c": fsdp % 2}
                here = dp * self.n_fsdp + fsdp
                at[axis] = (at[axis] + steps) % size[axis]
                there = (at["z"] * size["x"] + at["x"]) * self.n_fsdp + at["y"] * 2 + at["c"]
                pairs.append((here, there))
        return lax.ppermute(value, both, pairs)

    def begin(self, walks):
        return [[self.shift(*ask) for ask in walk.asks] for walk in walks if not walk.over]

    def finish(self, walks, got, *tied):
        got, tied = lax.optimization_barrier((got, tied))
        for walk, values in zip([walk for walk in walks if not walk.over], got):
            walk.take(values)
        return tied

    def together(self, walks, steps=100):
        for step in range(steps):
            if all(walk.over for walk in walks):
                break
            self.finish(walks, self.begin(walks))
        return [walk.result for walk in walks]

    def around_asks(self, value, axis):
        return [(value, axis, steps) for steps in range(1, self.sizes[axis])]

    def gather_dp_walk(self, value, order):
        shape = value.shape
        for axis in order:
            value = jnp.stack([value] + (yield self.around_asks(value, axis)))
        return value.reshape((-1,) + shape)

    def gather_dp(self, short, long):
        return [
            Walk(self.gather_dp_walk(long, "zx")),
            Walk(self.gather_dp_walk(short, "xz")),
        ][::-1]

    def scatter_dp(self, short, long):
        z_size, x_size = self.sizes["z"], self.sizes["x"]

        def walk(value, sizes, first, second):
            value = value.reshape(sizes + value.shape[1:])
            held = yield from self.sum_walk(value, first, bf16)
            return (yield from self.sum_walk(held, second, f32))

        return [
            Walk(walk(short, (z_size, x_size), "z", "x")),
            Walk(walk(long, (x_size, z_size), "x", "z")),
        ]

    def arrival(self):
        size = self.sizes
        dp = jnp.arange(self.n_dp, dtype=jnp.int32)
        z_back = (self.at["z"] - dp // size["x"]) % size["z"]
        x_back = (self.at["x"] - dp % size["x"]) % size["x"]
        return jnp.stack([z_back * size["x"] + x_back, x_back * size["z"] + z_back])

    def orders(self):
        size = self.sizes
        chunk = jnp.arange(CHUNKS, dtype=jnp.int32)
        y, x, z = chunk % size["y"], chunk // size["y"] % size["x"], chunk // size["y"] // size["x"]
        places = []
        for order in stage_orders:
            place = jnp.zeros_like(chunk)
            for axis in reversed(order):
                value = {"x": x, "y": y, "z": z}[axis]
                place = place * size[axis] + (self.at[axis] - value) % size[axis]
            places.append(place)
        chunks = [jnp.sum(jnp.where(p[:, None] == chunk[None, :], chunk[:, None], 0), 0) for p in places]
        flat = jnp.concatenate(chunks + places + [self.at["c"][None]])
        return jnp.pad(flat, (0, 128 - flat.shape[0])).astype(jnp.int32)

    def gather_walk(self, block, order):
        held = block[None]
        for axis in order[:2]:
            held = jnp.concatenate([held] + (yield self.around_asks(held, axis)), axis=0)
        held = jnp.concatenate([held] + (yield self.around_asks(held, order[2])), axis=0)
        others = yield [(held, "c")]
        return [held], others

    def beside(self, *steps):
        walks = [Walk(step) for step in steps]
        while not all(walk.over for walk in walks):
            live = [walk for walk in walks if not walk.over]
            asks = [ask for walk in live for ask in walk.asks]
            got = yield asks
            for walk in live:
                count = len(walk.asks)
                walk.take(got[:count])
                got = got[count:]
        return [walk.result for walk in walks]

    def gather_pair_walk(self, block, cut):
        held = block[None]
        held = jnp.concatenate([held] + (yield self.around_asks(held, "z")), axis=0)

        def rest(held, first, second):
            *near, own = yield self.around_asks(held, first) + [(held, "c")]
            others = [own]
            held = jnp.concatenate([held] + near, axis=0)
            far = yield self.around_asks(held, second)
            others += yield [(value, "c") for value in near + far]
            return [held] + far, others

        return (
            yield from self.beside(
                rest(held[:, :, :cut], "x", "y"), rest(held[:, :, cut:], "y", "x")
            )
        )

    def sum_walk(self, value, axis, kind):
        n = value.shape[0]
        got = yield [(value[steps], axis, n - steps) for steps in range(1, n)]
        return sum((one.astype(f32) for one in got), value[0].astype(f32)).astype(kind)

    def scatter_walk(self, mine, other, order):
        (got,) = yield [(other, "c")]
        held = plus(mine, got)
        for stage, axis in enumerate(reversed(order)):
            value = held.reshape((self.sizes[axis], -1) + held.shape[1:])
            held = yield from self.sum_walk(value, axis, f32 if stage == 2 else bf16)
        return held[0]

    def scatter_pair_walk(self, mine, other, cut):
        (got,) = yield [(other, "c")]

        def first(held, one, two):
            for axis in (one, two):
                value = held.reshape((self.sizes[axis], -1) + held.shape[1:])
                held = yield from self.sum_walk(value, axis, bf16)
            return held

        parts = yield from self.beside(
            first(plus(mine[:, :, :cut], got[:, :, :cut]), "y", "x"),
            first(plus(mine[:, :, cut:], got[:, :, cut:]), "x", "y"),
        )
        held = yield from self.sum_walk(jnp.concatenate(parts, axis=2)[:, None], "z", f32)
        return held[0]


class Walk:
    def __init__(self, steps):
        self.steps, self.over, self.result = steps, False, None
        self.asks = next(steps)

    def tie(self, value):
        value, held = lax.optimization_barrier((value, [ask[0] for ask in self.asks]))
        self.asks = [(new, *ask[1:]) for new, ask in zip(held, self.asks)]
        return value

    def take(self, got):
        try:
            self.asks = self.steps.send(got)
        except StopIteration as end:
            self.over, self.result = True, end.value


def plus(one, two, kind=bf16):
    return (one.astype(f32) + two.astype(f32)).astype(kind)


def join_columns(one, two):
    return jnp.concatenate(lax.optimization_barrier((one, two)), axis=1)


def gather_plain(packs):
    return [([lax.all_gather(pack, both, axis=0, tiled=True)[None]], []) for pack in packs]


def scatter_plain(parts):
    whole = jnp.concatenate([part[0] for part in parts], axis=1)
    whole = lax.psum_scatter(whole, both, scatter_dimension=0, tiled=True).astype(f32)
    ends = [0]
    for part in parts:
        ends.append(ends[-1] + part.shape[2])
    return [whole[:, low:high] for low, high in zip(ends[:-1], ends[1:])]


def shards(
    n_dp,
    n_fsdp,
    decoder_states,
    encodings,
    owner_query,
    buckets,
    gain_self,
    bias_table,
    self_query,
    self_key,
    self_value,
    self_output,
    gain_cross,
    cross_query,
    cross_key,
    cross_value,
    cross_output,
    gain_feed,
    feed_in,
    feed_out,
    cotangent,
):
    n_dev = n_dp * n_fsdp
    wires = Wires(n_dp, n_fsdp)
    chunked = n_dev // 2 == CHUNKS and D % (8 * n_dev) == 0
    chunks = CHUNKS if chunked else 1
    rows = decoder_states.shape[0]
    keys_total = encodings.shape[0]
    slot = keys_total // n_dp
    part = D // n_dev
    bias_part = bias_table.shape[0]
    half = D // 2

    device = lax.axis_index("dp") * n_fsdp + lax.axis_index("fsdp")
    lane = jnp.arange(128, dtype=jnp.int32)
    entry = device * bias_part + jnp.arange(bias_part, dtype=jnp.int32)
    spot = (16 + entry % H)[:, None] == lane[None, :]
    small = jnp.sum(jnp.where(spot, bias_table[:, None].astype(f32), 0.0), axis=0)
    small = jnp.where(jnp.arange(part)[:, None] == 0, small[None, :], 0.0)
    for i, gain in enumerate((gain_self, gain_cross, gain_feed)):
        small = jnp.where(lane[None, :] == i, gain[:, None].astype(f32), small)
    small = small.astype(bf16)

    packs = [
        jnp.concatenate(values, axis=1)
        for values in (
            (self_query, self_key, cross_key),
            (self_value, self_output, cross_value),
            (cross_query, small),
        )
    ]

    def runs(owner_query, buckets):
        owners = owner_query.reshape(n_dp, slot)
        ids = (jnp.arange(n_dp, dtype=jnp.int32) * n_fsdp + lax.axis_index("fsdp")) * QPD
        before = owners[:, None, :] < (ids[:, None] + jnp.arange(QPD + 1, dtype=jnp.int32))[:, :, None]
        bounds = jnp.sum(before.astype(jnp.int32), axis=2)
        return bounds, wires.arrival(), jnp.tile(buckets.T, (1, 4)), orders_of()

    def orders_of():
        return wires.orders() if chunked else jnp.zeros((128,), jnp.int32)

    if chunked:
        walks = [
            Walk(wires.gather_pair_walk(join_columns(*packs[:2]), 3 * D)),
            Walk(wires.gather_walk(packs[2], "xyz")),
        ]
        owner_query, buckets = wires.finish(walks, wires.begin(walks), owner_query, buckets)
        got = wires.begin(walks)
        (places, feed_in, feed_out, cross_output) = wires.finish(
            walks, got, runs(owner_query, buckets), feed_in, feed_out, cross_output
        )
        bounds, arrival, buckets_wide, orders = places
        pair, third = wires.together(walks)
        first_weights = [*pair, third]
    else:
        first_weights = gather_plain(packs)
        bounds, arrival, buckets_wide, orders = runs(owner_query, buckets)
    feed_pack = jnp.concatenate(
        [feed_in[:, t * D : (t + 1) * D] for t in range(4)] + [feed_out, cross_output], axis=0
    )
    feed_pack = lax.all_gather(feed_pack, both, axis=0)
    w_feed_in = feed_pack[:, : 4 * part].reshape(n_dev, 4, part, D).transpose(1, 0, 2, 3)
    w_feed_in = w_feed_in.reshape(4, D, D)
    w_feed_out = feed_pack[:, 4 * part : 8 * part].reshape(4 * D, D)
    w_cross_output = feed_pack[:, 8 * part :].reshape(D, D)

    counts = [(len(mine), len(other)) for mine, other in first_weights]
    pieces = [piece for weight in first_weights for side in weight for piece in side]
    first_widths = [3 * D, 3 * D, D + 128]
    wide = (rows, D)
    (
        normed_self,
        query_self,
        key_self,
        value_self,
        self_mixed,
        first_residual,
        normed_cross,
        query_short,
        query_long,
        gains,
        bias,
        w_first,
    ) = call(
        functools.partial(self_kernel, counts),
        "self_forward",
        [smem, vmem, vmem] + [hbm] * len(pieces),
        [like(wide)] * 5
        + [like(wide, f32), like(wide), like((rows, D // 3)), like((rows, D - D // 3))]
        + [like((8, D), f32), like((TGT, H * TGT), f32), like((5, D, D))],
        [weights(5, D, D), weights(D, 128)]
        + [weights(min(chunks, 2), chunks, D // (2 * chunks) if chunked else D, w) for w in first_widths]
        + [pltpu.SemaphoreType.DMA((3,)), pltpu.SemaphoreType.DMA((5,))],
        1_500_000_000,
        9_000_000,
        orders,
        decoder_states,
        buckets_wide,
        *pieces,
        out_specs=[vmem] * 11 + [hbm],
    )

    tall = math.gcd(keys_total, 1536)
    steps = keys_total // tall
    block = pl.BlockSpec((tall, D), lambda i: (i, 0))

    full = pl.BlockSpec((D, D), lambda step: (0, 0))
    height = D // (2 * chunks) if chunked else D

    def project(order):
        mine, other = first_weights[order]
        keys, weight = call(
            functools.partial(project_kernel, order, len(mine)),
            "cross_project",
            [smem, block] + [hbm] * (len(mine) + len(other)),
            [like((keys_total, D)), like((D, D))],
            [weights(min(chunks, 2), chunks, height, D), pltpu.SemaphoreType.DMA((1,))],
            7_300_000_000,
            20_000_000,
            orders,
            encodings,
            *mine,
            *other,
            grid=(steps,),
            out_specs=[block, full],
        )
        return keys.reshape(n_dp, slot, D), weight

    walks = wires.gather_dp(query_short, query_long)
    ((key_cross, w_key),) = wires.finish(walks, wires.begin(walks), project(0))
    ((value_cross, w_value),) = wires.finish(walks, wires.begin(walks), project(1))
    all_queries = [walk.result for walk in walks]
    parts = cross_mix(bounds, arrival, all_queries, key_cross, value_cross)
    back = lax.all_to_all(parts, "dp", split_axis=0, concat_axis=0)

    (
        layer_output,
        d_short,
        d_long,
        d_second,
        d_branch,
        cross_mixed,
        normed_feed,
        hidden,
        d_pre,
        grad_gain_feed,
    ) = call(
        feed_kernel,
        "feed_both_ways",
        [vmem] * 4 + [hbm] * 3,
        [
            like(wide),
            like((rows, D // 3)),
            like((rows, D - D // 3 + 128)),
            like(wide, f32),
            like(wide),
            like(wide),
            like(wide),
            like((4, rows, D)),
            like((4, rows, D)),
            like((1, D), f32),
        ],
        [
            weights(D, D),
            weights(4, D, D),
            weights(4 * D, D),
            pltpu.VMEM((n_dp, rows, D), f32),
            pltpu.SemaphoreType.DMA((3,)),
        ],
        3_000_000_000,
        14_000_000,
        back,
        first_residual,
        cotangent,
        gains,
        w_feed_in,
        w_feed_out,
        w_cross_output,
    )
    blocks = n_dev if part % 8 == 0 else 1
    feed_grad = call(
        feed_grad_kernel,
        "feed_grads",
        [vmem] * 6,
        like((blocks, 9, D // blocks, D)),
        [],
        1_500_000_000,
        14_000_000,
        hidden,
        d_pre,
        normed_feed,
        cross_mixed,
        d_branch,
        cotangent,
    )
    if blocks == 1:
        feed_grad = jnp.concatenate(
            [
                feed_grad[0, :4].reshape(4, n_dev, part, D).transpose(1, 0, 2, 3),
                feed_grad[0, 4:8].reshape(n_dev, 4, part, D),
                feed_grad[0, 8].reshape(n_dev, 1, part, D),
            ],
            axis=1,
        )
    column = jnp.arange(2 * H * TGT, dtype=jnp.int32)
    place = (
        (lane[:, None] // 48 == column[None, :] // (H * TGT))
        & (lane[:, None] % 16 == (column[None, :] // TGT) % H)
    ).astype(bf16)
    walks = wires.gather_dp(d_short, d_long)
    (feed_grad,) = wires.finish(walks, wires.begin(walks), feed_grad)
    feed_sum = lax.psum_scatter(feed_grad, both, scatter_dimension=0).astype(f32)
    wires.together(walks)
    all_mixed = [walk.result for walk in walks]
    short, long, d_key_cross, d_value_cross = cross_grad(
        bounds, arrival, all_queries, all_mixed, place, key_cross, value_cross
    )

    height = D // (2 * chunks) if chunked else D

    def encode_grad(first, count, before=()):
        at = pl.BlockSpec((tall, D), lambda step: (step + first, 0))
        return call(
            encode_grad_kernel,
            "encodings_grad",
            [at, at, full, full] + [hbm] * len(before),
            like((keys_total, D)),
            [],
            14_000_000_000 * count // steps,
            30_000_000 * count // steps,
            d_key_cross.reshape(keys_total, D),
            d_value_cross.reshape(keys_total, D),
            w_key,
            w_value,
            *before,
            grid=(count,),
            out_specs=at,
            input_output_aliases={4: 0} if before else {},
        )

    walks = wires.scatter_dp(short, long)
    got = wires.begin(walks)
    key_grads = call(
        functools.partial(weight_grad_kernel, steps),
        "cross_weight_grads",
        [smem, block, block, block],
        [like((chunks, height, 2 * D))] * 2,
        [pltpu.VMEM((2, D, D), f32)],
        14_500_000_000,
        32_000_000,
        orders,
        encodings,
        d_key_cross.reshape(keys_total, D),
        d_value_cross.reshape(keys_total, D),
        grid=(steps,),
        out_specs=[pl.BlockSpec((chunks, height, 2 * D), lambda i: (0, 0, 0))] * 2,
    )
    (key_grads,) = wires.finish(walks, got, key_grads)
    got = wires.begin(walks)
    if chunked:
        key_walk = [Walk(wires.scatter_pair_walk(*key_grads, D))]
        (got,) = wires.finish(key_walk, wires.begin(key_walk), got)
    (encodings_grad,) = wires.finish(walks, got, encode_grad(0, steps // 2))
    d_query_cross = jnp.concatenate([walk.result for walk in walks], axis=1)
    if chunked:
        d_query_cross = key_walk[0].tie(d_query_cross)
        got_key = wires.begin(key_walk)
    decoder_grad, *grads = call(
        self_grad_kernel,
        "self_backward",
        [smem] + [vmem] * 14 + [hbm],
        [
            like(wide),
            *[like((chunks, height, 5 * D + 128))] * 2,
        ],
        [
            weights(5, D, D),
            weights(rows, D),
            weights(rows, D),
            weights(rows, D),
            weights(rows, D),
            pltpu.VMEM((TGT, H * TGT), f32),
            pltpu.SemaphoreType.DMA((5,)),
        ],
        3_000_000_000,
        14_000_000,
        orders,
        d_query_cross,
        d_second,
        first_residual,
        decoder_states,
        normed_cross,
        normed_self,
        query_self,
        key_self,
        value_self,
        self_mixed,
        gains,
        bias,
        buckets_wide,
        grad_gain_feed,
        w_first,
    )

    cut = 2 * D + half + 128
    if chunked:
        (grads,) = wires.finish(key_walk, got_key, grads)
        walks = [Walk(wires.scatter_pair_walk(*grads, cut))]
        every = walks + key_walk
        (encodings_grad,) = wires.finish(every, wires.begin(every), encodings_grad)
        got = wires.begin(every)
        encodings_grad = encode_grad(steps // 2, steps - steps // 2, (encodings_grad,))
        (encodings_grad,) = wires.finish(every, got, encodings_grad)
        wires.together(every, 1)
        (feed_sum,) = wires.finish(every, wires.begin(every), feed_sum)
        first_sum, key_sum = walks[0].result, key_walk[0].result
    else:
        first_sum, key_sum = scatter_plain([grads[0], key_grads[0]])
        encodings_grad = encode_grad(steps // 2, steps - steps // 2, (encodings_grad,))

    small_sum = first_sum[:, cut - 128 : cut]
    bias_sum = jnp.sum(jnp.where(spot, small_sum[:1], 0.0), axis=1)
    return (
        layer_output,
        decoder_grad,
        encodings_grad,
        small_sum[:, 0],
        bias_sum,
        first_sum[:, :D],
        first_sum[:, D : 2 * D],
        first_sum[:, cut : cut + D],
        first_sum[:, cut + D : cut + 2 * D],
        small_sum[:, 1],
        jnp.concatenate([first_sum[:, 2 * D : 2 * D + half], first_sum[:, cut + 2 * D :]], axis=1),
        key_sum[:, :D],
        key_sum[:, D:],
        feed_sum[8],
        small_sum[:, 2],
        jnp.concatenate([feed_sum[t] for t in range(4)], axis=1),
        feed_sum[4:8].reshape(4 * part, D),
    )


def solution(mesh):
    rows = P(both, None)
    flat = P(both)
    in_specs = (rows, rows, flat, P(), flat, flat, rows, rows, rows, rows)
    in_specs += (flat, rows, rows, rows, rows, flat, rows, rows, rows)
    out_specs = (rows, rows, rows, flat, flat, rows, rows, rows, rows)
    out_specs += (flat, rows, rows, rows, rows, flat, rows, rows)
    return jax.shard_map(
        functools.partial(shards, mesh.shape["dp"], mesh.shape["fsdp"]),
        mesh=mesh,
        in_specs=in_specs,
        out_specs=out_specs,
        check_vma=False,
    )
```
